256 devices in a mesh: slab: 32 (over z, x_lo, core), depth: 8 (over y, x_hi).
Axes of the slice: x: 4 (x_hi: 2, x_lo: 2; x = x_hi * 2 + x_lo), y: 4, z: 8, core: 2. Of those that a mesh axis runs over, the one named last changes fastest.
Arguments:
- pressure: float32 [16, 2048, 2048], P('depth', 'slab'), may hold values from -6 to 6
- zone_labels: int32 [16, 2048, 2048], P('depth', 'slab'), may hold values from 0 to 15
- perm_table: float32 [16], replicated, may hold values from 0.02 to 1
- asig_table: float32 [16], replicated, may hold values from 0.5 to 2
- well_cells: int32 [512, 3], replicated, may hold values from 0 to 2047, as said below
- rate_levels: int32 [2, 512], replicated, may hold values from 0 to 7
- green_spectrum: float32 [2048, 2048], P(None, 'slab'), may hold values from -1 to 1, as said below
- seis_state: float32 [16, 2048, 2048], P('depth', 'slab'), may hold values from 0.3 to 3
Outputs:
- pressure_out: float32 [16, 2048, 2048], P('depth', 'slab')
- state_out: float32 [16, 2048, 2048], P('depth', 'slab')
- rate_map: float32 [2048, 2048], P('slab', 'depth')
The draws below stay inside these ranges and needn't reach their ends.
Inputs may be any that keep to these rules, and one draw needn't show every extreme that they name: `well_cells`: column 0 lies below 16, column 1 below 2048, column 2 below 2048; several wells may share a cell. green_spectrum at (kx, ky) equals its value at ((2048 - kx) % 2048, (2048 - ky) % 2048).
All inputs are finite; a program needn't handle non-finite values.
Results may differ from the reference program's by a relative error of at most 0.00019.
Values sent between devices are 32-bit elements; how exact they have to be, the bound alone decides.
No kernel may reach another device: no remote copies, remote signals or barrier semaphores. Data moves between devices by JAX's collectives and lax.ppermute only.
A program may use at most 128 MiB of HBM per device.

```python
import math
import jax
import jax.numpy as jnp
from jax import lax

NX = 2048
NY = 2048
NZ = 16
ZONES = 16
WELLS = 512
SWEEPS = 2


def draw_green_spectrum(key, part):
    key = jax.random.fold_in(key, 11)
    values = jax.random.uniform(key, (NX, NY), jnp.float32, -1.0, 1.0)
    mirrored = jnp.roll(jnp.flip(values, (0, 1)), 1, (0, 1))
    return 0.5 * (values + mirrored)


def draw_well_cells(key, part):
    key = jax.random.fold_in(key, 5)
    subkeys = jax.random.split(key, 3)
    layer_pick = jax.random.randint(subkeys[0], (WELLS,), 0, NZ)
    first_pick = jax.random.randint(subkeys[1], (WELLS,), 0, NX)
    second_pick = jax.random.randint(subkeys[2], (WELLS,), 0, NY)
    first_pick = first_pick.at[0].set(0)
    second_pick = second_pick.at[0].set(NY - 1)
    return jnp.stack([layer_pick, first_pick, second_pick], 1).astype(jnp.int32)


def with_ends(drawn, key, smallest, high):
    index_at = [jax.random.randint(jax.random.fold_in(key, axis), (), 0, length) for axis, length in enumerate(drawn.shape)]
    main_axis = drawn.shape.index(max(drawn.shape))
    neighbour = index_at[:main_axis] + [(index_at[main_axis] + 1) % drawn.shape[main_axis]] + index_at[main_axis + 1:]
    return drawn.at[tuple(index_at)].set(smallest).at[tuple(neighbour)].set(high)


def steps_of(own_key, shape, cuts, smallest, top_value):
    level = 1.0
    for axis_at, shards_of in cuts:
        draws = jax.random.uniform(jax.random.fold_in(jax.random.fold_in(own_key, 6), axis_at), (shards_of,), jnp.float32, smallest / len(cuts), top_value / len(cuts))
        level = level * jnp.repeat(jnp.exp(draws), shape[axis_at] // shards_of).reshape((-1,) + (1,) * (len(shape) - 1 - axis_at))
    return level


def normal_values(rng, dims, width, most, pieces=(), held_as=jnp.bfloat16):
    drawn = width * jax.random.normal(rng, dims, jnp.float32)
    if pieces:
        drawn = drawn * steps_of(rng, dims, pieces, -0.22, 0.18)
    return jnp.clip(drawn, -most, most).astype(held_as)


def setup_inputs(seed: int = 0) -> dict:
    key_list = jax.random.split(jax.random.key(seed), 9)
    return {
        "pressure": normal_values(key_list[0], (NZ, NX, NY), 1.0, 6.0, ((0, 8), (1, 32)), jnp.float32),
        "zone_labels": with_ends(jax.random.randint(key_list[1], (NZ, NX, NY), 0, ZONES), jax.random.fold_in(key_list[1], 1), 0, ZONES - 1).astype(jnp.int32),
        "perm_table": jnp.clip(jnp.exp(jax.random.uniform(key_list[2], (ZONES,), jnp.float32, math.log(0.02), math.log(1.0))), 0.02, 1.0),
        "asig_table": jnp.clip(jnp.exp(jax.random.uniform(key_list[3], (ZONES,), jnp.float32, math.log(0.5), math.log(2.0))), 0.5, 2.0),
        "well_cells": draw_well_cells(jax.random.fold_in(key_list[8], 71), 0),
        "rate_levels": with_ends(jax.random.randint(key_list[5], (SWEEPS, WELLS), 0, 8), jax.random.fold_in(key_list[5], 1), 0, 7).astype(jnp.int32),
        "green_spectrum": draw_green_spectrum(jax.random.fold_in(key_list[8], 71), 0),
        "seis_state": jnp.clip(jnp.exp(math.log(3.0) - 2.3025851 * jax.random.uniform(key_list[7], (NZ, NX, NY), jnp.float32) ** steps_of(key_list[7], (NZ, NX, NY), ((0, 8), (1, 32)), -0.2, 0.2)), 0.3, 3.0),
    }


conduct = 0.15
rate_unit = 0.5
friction = 0.6
recovery = 0.6065306597126334

def diffuse(perm_pad, press_pad, source):
    perm_mid = perm_pad[1:-1, 1:-1]
    press_mid = press_pad[1:-1, 1:-1]
    flux = jnp.zeros_like(press_mid)
    sides = ((perm_pad[2:, 1:-1], press_pad[2:, 1:-1]), (perm_pad[:-2, 1:-1], press_pad[:-2, 1:-1]), (perm_pad[1:-1, 2:], press_pad[1:-1, 2:]), (perm_pad[1:-1, :-2], press_pad[1:-1, :-2]))
    for perm_side, press_side in sides:
        flux = flux + jnp.sqrt(perm_side * perm_mid) * (press_side - press_mid)
    along = jnp.sqrt(perm_mid[..., 1:] * perm_mid[..., :-1]) * (press_mid[..., 1:] - press_mid[..., :-1])
    zero_col = jnp.zeros_like(along[..., :1])
    flux = flux + jnp.concatenate([along, zero_col], -1) - jnp.concatenate([zero_col, along], -1)
    return press_mid + conduct * flux + source

def reference(pressure, zone_labels, perm_table, asig_table, well_cells, rate_levels, green_spectrum, seis_state):
    permeab = perm_table[zone_labels]
    strength = asig_table[zone_labels]
    flat_index = ((well_cells[:, 0] * NX + well_cells[:, 1]) * NY + well_cells[:, 2]).astype(jnp.int32)
    perm_pad = jnp.pad(permeab, ((1, 1), (1, 1), (0, 0)))
    press = pressure
    for sweep_index in range(SWEEPS):
        amounts = rate_unit * rate_levels[sweep_index].astype(jnp.float32)
        source = jnp.zeros((NZ * NX * NY,), jnp.float32).at[flat_index].add(amounts).reshape(NZ, NX, NY)
        press_pad = jnp.pad(press, ((1, 1), (1, 1), (0, 0)))

        def one_layer(layer_index, press_pad=press_pad, source=source):
            return diffuse(lax.dynamic_slice_in_dim(perm_pad, layer_index, 3, 0), lax.dynamic_slice_in_dim(press_pad, layer_index, 3, 0), lax.dynamic_slice_in_dim(source, layer_index, 1, 0))
        press = lax.map(one_layer, jnp.arange(NZ, dtype=jnp.int32)).reshape(NZ, NX, NY)

    def convolve(layer):
        return jnp.real(jnp.fft.ifft2(green_spectrum * jnp.fft.fft2(layer))).astype(jnp.float32)
    stress = lax.map(convolve, press)
    coulomb = stress + friction * press
    state_out = 1.0 + (seis_state * jnp.exp(-coulomb / strength) - 1.0) * recovery
    layer_pos = jnp.arange(NZ, dtype=jnp.int32).astype(jnp.float32)
    weights = (1.0 + 2.0 * layer_pos / (NZ - 1)) / (2.0 * NZ)
    rate_map = lax.optimization_barrier(jnp.sum(weights[:, None, None] * (1.0 / state_out), axis=0))
    return (press, state_out, rate_map)
```

```python
import functools
import math

import jax
import jax.numpy as jnp
import ml_dtypes
import numpy as np
from jax import lax
from jax.experimental import pallas as pl
from jax.experimental.pallas import tpu as pltpu
from jax.sharding import PartitionSpec as P

conduct = 0.15
rate_unit = 0.5
friction = 0.6
recovery = 0.6065306597126334

LANES = 128
SLABS = 32
DEPTHS = 8
N = 2048
ROWS = N // SLABS
TILES = N // LANES
PAIRS = TILES // 2
FREQS = LANES // SLABS
STEP = SLABS * FREQS
PARAMS = pltpu.CompilerParams(vmem_limit_bytes=48 * 1024 * 1024)
F32 = jnp.float32
BF16 = jnp.bfloat16


def blocks(theta):
    cos, sin = np.cos(theta), np.sin(theta)
    return np.stack([np.stack([cos, -sin]), np.stack([sin, cos])])


def halves(table):
    high = table.astype(ml_dtypes.bfloat16)
    low = (table - high.astype(np.float64)).astype(ml_dtypes.bfloat16)
    return high, low


def left_table(table):
    high, low = halves(table)
    return np.concatenate([high, high, low], 1)


def right_table(table):
    high, low = halves(table)
    return np.concatenate([high, high, low], 0)


@functools.lru_cache(maxsize=None)
def tables():
    two_pi = 2.0 * np.pi
    k2, n2 = np.arange(128)[:, None], np.arange(128)[None, :]
    fwd = blocks(-two_pi * ((k2 * n2) % 128) / 128)
    fwd = fwd.reshape(2, 2, SLABS, FREQS, 128).transpose(2, 0, 3, 1, 4).reshape(256, 256)
    inv = blocks(two_pi * ((k2 * n2) % 128) / 128)
    inv = inv.reshape(2, 2, 128, SLABS, FREQS).transpose(3, 1, 4, 0, 2).reshape(256, 256)
    s, k = np.arange(SLABS)[:, None], np.arange(SLABS)[None, :]
    eye = np.eye(FREQS)
    mid = blocks(-two_pi * ((s * k) % SLABS) / SLABS)
    mid = np.einsum("abks,ij->akisbj", mid, eye)
    mid = mid.reshape(256, 256)
    mid_inv = blocks(two_pi * ((s * k) % SLABS) / SLABS)
    mid_inv = np.einsum("absk,ij->saibkj", mid_inv, eye).reshape(256, 256)
    r, q = np.arange(ROWS)[:, None], np.arange(ROWS)[None, :]
    two = np.eye(2)
    inner = blocks(-two_pi * ((r * q) % ROWS) / ROWS)
    inner = np.einsum("abqr,ij->bjraiq", inner, two).reshape(256, 256)
    inner_inv = blocks(two_pi * ((r * q) % ROWS) / ROWS)
    inner_inv = np.einsum("abrq,ij->bjqair", inner_inv, two).reshape(256, 256)
    row_angle = -two_pi * ((np.arange(TILES)[:, None] * np.arange(128)[None, :]) % N) / N
    row_twist = np.stack([np.cos(row_angle), np.sin(row_angle)]).astype(np.float32)
    col_angle = -two_pi * ((np.arange(SLABS)[:, None] * np.arange(ROWS)[None, :]) % N) / N
    col_angle = np.tile(np.repeat(col_angle, FREQS, 0), (1, 2))
    col_twist = np.stack([np.cos(col_angle), np.sin(col_angle)]).astype(np.float32)
    return {
        "fwd": left_table(fwd),
        "inv": right_table(inv),
        "mid": left_table(mid),
        "mid_inv": left_table(mid_inv),
        "inner": right_table(inner),
        "inner_inv": right_table(inner_inv),
        "row_twist": row_twist,
        "col_twist": col_twist,
    }


def triple(value, axis):
    high = value.astype(BF16)
    low = (value - high.astype(F32)).astype(BF16)
    return jnp.concatenate([high, low, high], axis)


def matmul(left, right):
    return jnp.dot(left, right, preferred_element_type=F32)


def radix4(items, sign):
    (ar, ai), (br, bi), (cr, ci), (dr, di) = items
    pr, pi, mr, mi = ar + cr, ai + ci, ar - cr, ai - ci
    qr, qi, nr, ni = br + dr, bi + di, br - dr, bi - di
    tr, ti = (-ni, nr) if sign > 0 else (ni, -nr)
    return [(pr + qr, pi + qi), (mr + tr, mi + ti), (pr - qr, pi - qi), (mr - tr, mi - ti)]


def scale_by(item, angle):
    c, s = math.cos(angle), math.sin(angle)
    re, im = item
    if abs(s) < 1e-12:
        return (re, im) if c > 0 else (-re, -im)
    if abs(c) < 1e-12:
        return (-im, re) if s > 0 else (im, -re)
    return (re * c - im * s, re * s + im * c)


def dft16(items, sign):
    mids = [radix4([items[4 * b + a] for b in range(4)], sign) for a in range(4)]
    out = [None] * 16
    for k in range(4):
        column = [scale_by(mids[a][k], sign * 2.0 * math.pi * a * k / 16) for a in range(4)]
        for m, item in enumerate(radix4(column, sign)):
            out[k + 4 * m] = item
    return out


def pick(label, table, bit, base):
    if bit < 0:
        return table[base]
    mask = (label & (1 << bit)) != 0
    return jnp.where(mask, pick(label, table, bit - 1, base + (1 << bit)), pick(label, table, bit - 1, base))


def lookup_kernel(root_ref, inv_ref, label_ref, root_out, inv_out):
    width = 512

    def body(i, carry):
        for l in range(2):
            for c in range(N // width):
                rows, cols = pl.ds(pl.multiple_of(i * 8, 8), 8), pl.ds(c * width, width)
                label = label_ref[l, rows, cols]
                root_out[l, rows, cols] = pick(label, root_ref, 3, 0)
                inv_out[l, rows, cols] = pick(label, inv_ref, 3, 0)
        return carry

    lax.fori_loop(0, ROWS // 8, body, 0)


def wells_kernel(where_ref, amount_ref, col_ref, out_ref):
    row = lax.broadcasted_iota(jnp.int32, (128, 512), 0)
    hit = row == where_ref[...]
    left = [jnp.where(hit, amount_ref[s : s + 1, :], 0.0).astype(BF16) for s in range(2)]
    left = jnp.concatenate(left, 0)
    col_of = jnp.broadcast_to(col_ref[...], (512, 256))
    for c in range(N // 256):
        col = lax.broadcasted_iota(jnp.int32, (512, 256), 1) + c * 256
        right = jnp.where(col == col_of, 1.0, 0.0).astype(BF16)
        out_ref[:, c * 256 : (c + 1) * 256] = matmul(left, right)


def neighbours(padded, own, c, before, after, row, lane):
    left = jnp.where(lane == 0, pltpu.roll(padded[:, pl.ds(pl.multiple_of(c * 128, 128), 128)], 1, 1), pltpu.roll(own, 1, 1))
    right = jnp.where(
        lane == 127,
        pltpu.roll(padded[:, pl.ds(pl.multiple_of(c * 128 + 256, 128), 128)], 127, 1),
        pltpu.roll(own, 127, 1),
    )
    up = jnp.where(row == 0, before, pltpu.roll(own, 1, 0))
    down = jnp.where(row == ROWS - 1, after, pltpu.roll(own, ROWS - 1, 0))
    return (left + right) + (up + down)


def clear_ends(pad_ref):
    zero = jnp.zeros((ROWS, LANES), F32)
    for l in range(2):
        pad_ref[l, :, 0:128] = zero
        pad_ref[l, :, N + 128 : N + 256] = zero


def tile_at(c):
    return pl.ds(pl.multiple_of(c * 128, 128), 128)


def pad_at(c):
    return pl.ds(pl.multiple_of(c * 128 + 128, 128), 128)


def first_kernel(
    p_ref, q_ref, pb_ref, qb_ref, pa_ref, qa_ref, prb_ref, qrb_ref, pra_ref, qra_ref, src_ref,
    low_out, top_out, s_out, first_row, last_row, q_pad, u_pad,
):
    clear_ends(q_pad)
    clear_ends(u_pad)
    row = lax.broadcasted_iota(jnp.int32, (ROWS, LANES), 0)
    lane = lax.broadcasted_iota(jnp.int32, (ROWS, LANES), 1)

    def fill(c, carry):
        for l in range(2):
            q = q_ref[l, :, tile_at(c)]
            q_pad[l, :, pad_at(c)] = q
            u_pad[l, :, pad_at(c)] = q * p_ref[l, :, tile_at(c)]
        return carry

    lax.fori_loop(0, TILES, fill, 0)

    def body(c, carry):
        at = tile_at(c)
        for l in range(2):
            q, u = q_pad[l, :, pad_at(c)], u_pad[l, :, pad_at(c)]
            z_q, z_p = (qb_ref, pb_ref) if l == 0 else (qa_ref, pa_ref)
            zq = z_q[:, at]
            qrb, qra = qrb_ref[l, :, at], qra_ref[l, :, at]
            s = neighbours(q_pad.at[l], q, c, qrb, qra, row, lane)
            s = s + (zq + q_pad[1 - l, :, pad_at(c)])
            t = neighbours(u_pad.at[l], u, c, qrb * prb_ref[l, :, at], qra * pra_ref[l, :, at], row, lane)
            t = t + (zq * z_p[:, at] + u_pad[1 - l, :, pad_at(c)])
            p = p_ref[l, :, at]
            new = p + (conduct * q) * (t - p * s) + src_ref[l * ROWS : (l + 1) * ROWS, at]
            s_out[l, :, at] = s
            out = low_out if l == 0 else top_out
            out[:, at] = new
            first_row[l, :, at] = new[0:1]
            last_row[l, :, at] = new[ROWS - 1 : ROWS]
        return carry

    lax.fori_loop(0, TILES, body, 0)


def second_kernel(
    low_ref, top_ref, q_ref, s_ref, pb_ref, qb_ref, pa_ref, qa_ref, prb_ref, qrb_ref, pra_ref, qra_ref, src_ref,
    fwd_ref, twist_ref, p_out, spec_out, u_pad, mid_ref,
):
    clear_ends(u_pad)
    row = lax.broadcasted_iota(jnp.int32, (ROWS, LANES), 0)
    lane = lax.broadcasted_iota(jnp.int32, (ROWS, LANES), 1)

    def fill(c, carry):
        for l, ref in enumerate((low_ref, top_ref)):
            u_pad[l, :, pad_at(c)] = q_ref[l, :, tile_at(c)] * ref[:, tile_at(c)]
        return carry

    lax.fori_loop(0, TILES, fill, 0)

    def body(c, carry):
        at = tile_at(c)
        for l in range(2):
            u = u_pad[l, :, pad_at(c)]
            z_q, z_p = (qb_ref, pb_ref) if l == 0 else (qa_ref, pa_ref)
            t = neighbours(
                u_pad.at[l], u, c, qrb_ref[l, :, at] * prb_ref[l, :, at], qra_ref[l, :, at] * pra_ref[l, :, at], row, lane
            )
            t = t + (z_q[:, at] * z_p[:, at] + u_pad[1 - l, :, pad_at(c)])
            p = (low_ref if l == 0 else top_ref)[:, at]
            p_out[l, :, at] = (
                p + (conduct * q_ref[l, :, at]) * (t - p * s_ref[l, :, at]) + src_ref[l * ROWS : (l + 1) * ROWS, at]
            )
        return carry

    lax.fori_loop(0, TILES, body, 0)
    spectrum_of_rows(p_out, fwd_ref, twist_ref, spec_out, mid_ref)


def spectrum_of_rows(p_ref, fwd_ref, twist_ref, spec_out, mid_ref):
    def body(i, carry):
        rows = pl.ds(pl.multiple_of(i * 8, 8), 8)
        items = [(p_ref[0, rows, n * 128 : (n + 1) * 128], p_ref[1, rows, n * 128 : (n + 1) * 128]) for n in range(TILES)]
        for k, (re, im) in enumerate(dft16(items, -1)):
            if k:
                cos, sin = twist_ref[0, k : k + 1, :], twist_ref[1, k : k + 1, :]
                re, im = re * cos - im * sin, re * sin + im * cos
            at = pl.ds(pl.multiple_of(k * ROWS + i * 8, 8), 8)
            mid_ref[at, 0:128] = re
            mid_ref[at, 128:256] = im
        return carry

    lax.fori_loop(0, ROWS // 8, body, 0)
    for c in range(4):
        part = triple(mid_ref[c * 256 : (c + 1) * 256, :], 1)
        spec_out[:, c * 256 : (c + 1) * 256] = lax.dot_general(
            fwd_ref[...], part, (((1,), (1,)), ((), ())), preferred_element_type=F32
        )


def middle_kernel(spec_ref, green_ref, mid_ref, mid_inv_ref, inner_ref, inner_inv_ref, twist_ref, out_ref):
    cos, sin = twist_ref[0], twist_ref[1]
    for p in range(0, PAIRS, 2):
        at = slice(p * 128, (p + 2) * 128)
        spread = matmul(mid_ref[...], triple(spec_ref[:, at], 0))
        rows = []
        for h in range(2):
            re, im = spread[0:128, h * 128 : (h + 1) * 128], spread[128:256, h * 128 : (h + 1) * 128]
            rows.append(jnp.concatenate([re * cos - im * sin, re * sin + im * cos], 1))
        freq = matmul(triple(jnp.concatenate(rows, 0), 1), inner_ref[...])
        green = jnp.concatenate([green_ref[p], green_ref[p + 1]], 0)
        freq = freq * jnp.concatenate([green, green], 1)
        back = matmul(triple(freq, 1), inner_inv_ref[...])
        cols = []
        for h in range(2):
            re, im = back[h * 128 : (h + 1) * 128, 0:128], back[h * 128 : (h + 1) * 128, 128:256]
            cols.append(jnp.concatenate([re * cos + im * sin, im * cos - re * sin], 0))
        out_ref[:, at] = matmul(mid_inv_ref[...], triple(jnp.concatenate(cols, 1), 0))


def last_kernel(weight_ref, spec_ref, p_ref, inv_ref, seis_ref, table_ref, twist_ref, state_out, rate_out, mid_ref):
    for c in range(4):
        turned = jnp.transpose(spec_ref[:, c * 256 : (c + 1) * 256])
        mid_ref[c * 256 : (c + 1) * 256, :] = matmul(triple(turned, 1), table_ref[...])

    def body(i, carry):
        rows = pl.ds(pl.multiple_of(i * 8, 8), 8)
        items = []
        for k in range(TILES):
            at = pl.ds(pl.multiple_of(k * ROWS + i * 8, 8), 8)
            re, im = mid_ref[at, 0:128], mid_ref[at, 128:256]
            if k:
                cos, sin = twist_ref[0, k : k + 1, :], twist_ref[1, k : k + 1, :]
                re, im = re * cos + im * sin, im * cos - re * sin
            items.append((re, im))
        for n, stress in enumerate(dft16(items, 1)):
            at = slice(n * 128, (n + 1) * 128)
            total = None
            for l in range(2):
                coulomb = stress[l] + friction * p_ref[l, rows, at]
                grown = seis_ref[l, rows, at] * jnp.exp(-coulomb * inv_ref[l, rows, at])
                state = 1.0 + (grown - 1.0) * recovery
                state_out[l, rows, at] = state
                term = weight_ref[l] / state
                total = term if total is None else total + term
            rate_out[n // 2, rows, (n % 2) * 128 : (n % 2) * 128 + 128] = total
        return carry

    lax.fori_loop(0, ROWS // 8, body, 0)


def sum_kernel(part_ref, out_ref):
    total = part_ref[0]
    for d in range(1, DEPTHS):
        total = total + part_ref[d]
    out_ref[...] = total


def vec(*shape):
    return jax.ShapeDtypeStruct(shape, F32)


def in_vmem(count):
    return [pl.BlockSpec(memory_space=pltpu.VMEM)] * count


def in_smem(count):
    return [pl.BlockSpec(memory_space=pltpu.SMEM)] * count


def call(kernel, outs, smem, args, scratch=()):
    return pl.pallas_call(
        kernel,
        out_shape=outs,
        in_specs=in_smem(smem) + in_vmem(len(args) - smem),
        out_specs=tuple(in_vmem(len(outs))) if isinstance(outs, tuple) else in_vmem(1)[0],
        scratch_shapes=[pltpu.VMEM(s, F32) for s in scratch],
        compiler_params=PARAMS,
    )(*args)


def shift(value, axis, step):
    peers = lax.axis_size(axis)
    pairs = [(i, i + step) for i in range(peers) if 0 <= i + step < peers]
    return lax.ppermute(value, axis, pairs)


def shards(pressure, zone_labels, perm_table, asig_table, well_cells, rate_levels, green_spectrum, seis_state):
    tab = {name: jnp.asarray(value) for name, value in tables().items()}
    z_start = lax.axis_index("depth") * 2
    x_start = lax.axis_index("slab") * ROWS
    block = vec(2, ROWS, N)
    layer = vec(ROWS, N)
    edge = vec(2, 1, N)

    p_below = shift(pressure[1], "depth", 1)
    p_above = shift(pressure[0], "depth", -1)
    p_before = shift(pressure[:, ROWS - 1 :], "slab", 1)
    p_after = shift(pressure[:, :1], "slab", -1)

    root, inv = call(
        lookup_kernel, (block, block), 2, (jnp.sqrt(perm_table), 1.0 / asig_table, zone_labels)
    )
    q_below = shift(root[1], "depth", 1)
    q_above = shift(root[0], "depth", -1)
    q_before = shift(root[:, ROWS - 1 :], "slab", 1)
    q_after = shift(root[:, :1], "slab", -1)

    z_local = well_cells[:, 0] - z_start
    x_local = well_cells[:, 1] - x_start
    inside = (z_local >= 0) & (z_local < 2) & (x_local >= 0) & (x_local < ROWS)
    spot = jnp.where(inside, z_local * ROWS + x_local, -1)[None, :]
    amounts = rate_unit * rate_levels.astype(F32)
    sources = call(wells_kernel, vec(256, N), 0, (spot, amounts, well_cells[:, 2:3]))

    green = (green_spectrum * (1.0 / (N * N))).reshape(ROWS, SLABS, FREQS, PAIRS, 2)
    green = green.transpose(3, 1, 2, 4, 0).reshape(PAIRS, STEP, LANES)

    low, top, s_sum, first, last = call(
        first_kernel,
        (layer, layer, block, edge, edge),
        0,
        (pressure, root, p_below, q_below, p_above, q_above, p_before, q_before, p_after, q_after, sources[:128]),
        ((2, ROWS, N + 256), (2, ROWS, N + 256)),
    )
    p_below = shift(top, "depth", 1)
    p_above = shift(low, "depth", -1)
    p_before = shift(last, "slab", 1)
    p_after = shift(first, "slab", -1)
    press, spec = call(
        second_kernel,
        (block, vec(256, 1024)),
        0,
        (low, top, root, s_sum, p_below, q_below, p_above, q_above, p_before, q_before, p_after, q_after, sources[128:],
         tab["fwd"], tab["row_twist"]),
        ((2, ROWS, N + 256), (1024, 256)),
    )
    spec = lax.all_to_all(spec.reshape(SLABS, 8, 1024), "slab", 0, 0, tiled=True).reshape(256, 1024)
    spec = call(
        middle_kernel,
        vec(256, 1024),
        0,
        (spec, green, tab["mid"], tab["mid_inv"], tab["inner"], tab["inner_inv"], tab["col_twist"]),
    )
    spec = lax.all_to_all(spec.reshape(SLABS, 8, 1024), "slab", 0, 0, tiled=True).reshape(256, 1024)
    layer_pos = (z_start + jnp.arange(2, dtype=jnp.int32)).astype(F32)
    weights = (1.0 + 2.0 * layer_pos / (2 * DEPTHS - 1)) / (4.0 * DEPTHS)
    state, rate = call(
        last_kernel,
        (block, vec(DEPTHS, ROWS, 2 * LANES)),
        1,
        (weights, spec, press, inv, seis_state, tab["inv"], tab["row_twist"]),
        ((1024, 256),),
    )
    rate = lax.all_to_all(rate, "depth", 0, 0, tiled=True)
    rate_map = call(sum_kernel, vec(ROWS, 2 * LANES), 0, (rate,))
    return (press, state, rate_map)


def solution(mesh):
    in_specs = (
        P("depth", "slab", None),
        P("depth", "slab", None),
        P(),
        P(),
        P(),
        P(),
        P(None, "slab"),
        P("depth", "slab", None),
    )
    out_specs = (P("depth", "slab", None), P("depth", "slab", None), P("slab", "depth"))
    return jax.shard_map(shards, mesh=mesh, in_specs=in_specs, out_specs=out_specs, check_vma=False)
```

```python
import functools
import math

import jax
import jax.numpy as jnp
import ml_dtypes
import numpy as np
from jax import lax
from jax.experimental import pallas as pl
from jax.experimental.pallas import tpu as pltpu
from jax.sharding import PartitionSpec as P

conduct = 0.15
rate_unit = 0.5
friction = 0.6
recovery = 0.6065306597126334

LANES = 128
SLABS = 32
DEPTHS = 8
N = 2048
ROWS = N // SLABS
TILES = N // LANES
FREQS = LANES // SLABS
STEP = SLABS * FREQS
F32 = jnp.float32
BF16 = jnp.bfloat16


def blocks(theta):
    cos, sin = np.cos(theta), np.sin(theta)
    return np.stack([np.stack([cos, -sin]), np.stack([sin, cos])])


def halves(table):
    high = table.astype(ml_dtypes.bfloat16)
    low = (table - high.astype(np.float64)).astype(ml_dtypes.bfloat16)
    return high, low


def left_table(table):
    high, low = halves(table)
    return np.concatenate([high, high, low], 1)


def right_table(table):
    high, low = halves(table)
    return np.concatenate([high, high, low], 0)


@functools.lru_cache(maxsize=None)
def tables():
    two_pi = 2.0 * np.pi
    k2, n2 = np.arange(128)[:, None], np.arange(128)[None, :]
    fwd = blocks(-two_pi * ((k2 * n2) % 128) / 128)
    fwd = fwd.reshape(2, 2, SLABS, FREQS, 128).transpose(2, 0, 3, 1, 4).reshape(256, 256)
    inv = blocks(two_pi * ((k2 * n2) % 128) / 128)
    inv = inv.reshape(2, 2, 128, SLABS, FREQS).transpose(3, 1, 4, 0, 2).reshape(256, 256)
    i, k = np.arange(SLABS)[:, None], np.arange(SLABS)[None, :]
    eye = np.eye(FREQS)
    angle = two_pi * ((i * k) % SLABS) / SLABS
    mid = np.einsum("absk,ij->akisbj", blocks(-angle), eye).reshape(256, 256)
    mid_inv = np.einsum("absk,ij->saibkj", blocks(angle), eye).reshape(256, 256)
    r, q = np.arange(8)[:, None], np.arange(8)[None, :]
    many = np.eye(TILES)
    angle = two_pi * ((r * q) % 8) / 8
    inner = np.einsum("abrq,ij->bjraiq", blocks(-angle), many).reshape(256, 256)
    inner_inv = np.einsum("abrq,ij->bjqair", blocks(angle), many).reshape(256, 256)
    row_angle = -two_pi * ((np.arange(TILES)[:, None] * np.arange(128)[None, :]) % N) / N
    row_twist = np.stack([np.cos(row_angle), np.sin(row_angle)]).astype(np.float32)
    row = (8 * np.arange(8)[:, None] + np.arange(8)[None, :])[:, None, :]
    col_angle = -two_pi * ((row * np.arange(SLABS)[None, :, None]) % N) / N
    col_angle = np.tile(np.repeat(col_angle, FREQS, 1), (1, 1, TILES))
    col_twist = np.stack([np.cos(col_angle), np.sin(col_angle)]).astype(np.float32)
    in_angle = np.tile(-two_pi * ((r * q) % 64) / 64, (1, TILES))
    in_twist = np.stack([np.cos(in_angle), np.sin(in_angle)]).astype(np.float32)
    return {
        "fwd": left_table(fwd),
        "inv": right_table(inv),
        "mid": left_table(mid),
        "mid_inv": left_table(mid_inv),
        "inner": right_table(inner),
        "inner_inv": right_table(inner_inv),
        "row_twist": row_twist,
        "col_twist": col_twist,
        "in_twist": in_twist,
    }


def triple(value, axis):
    high = value.astype(BF16)
    low = (value - high.astype(F32)).astype(BF16)
    return jnp.concatenate([high, low, high], axis)


def matmul(left, right):
    return jnp.dot(left, right, preferred_element_type=F32)


def radix4(items, sign):
    (ar, ai), (br, bi), (cr, ci), (dr, di) = items
    pr, pi, mr, mi = ar + cr, ai + ci, ar - cr, ai - ci
    qr, qi, nr, ni = br + dr, bi + di, br - dr, bi - di
    tr, ti = (-ni, nr) if sign > 0 else (ni, -nr)
    return [(pr + qr, pi + qi), (mr + tr, mi + ti), (pr - qr, pi - qi), (mr - tr, mi - ti)]


def scale_by(item, angle):
    c, s = math.cos(angle), math.sin(angle)
    re, im = item
    if abs(s) < 1e-12:
        return (re, im) if c > 0 else (-re, -im)
    if abs(c) < 1e-12:
        return (-im, re) if s > 0 else (im, -re)
    return (re * c - im * s, re * s + im * c)


def dft16(items, sign):
    mids = [radix4([items[4 * b + a] for b in range(4)], sign) for a in range(4)]
    out = [None] * 16
    for k in range(4):
        column = [scale_by(mids[a][k], sign * 2.0 * math.pi * a * k / 16) for a in range(4)]
        for m, item in enumerate(radix4(column, sign)):
            out[k + 4 * m] = item
    return out


def pick(label, table, bit, base):
    if bit < 0:
        return table[base]
    mask = (label & (1 << bit)) != 0
    return jnp.where(mask, pick(label, table, bit - 1, base + (1 << bit)), pick(label, table, bit - 1, base))


def lookup_kernel(root_ref, inv_ref, label_ref, root_out, inv_out):
    width = 512

    def body(i, carry):
        for l in range(2):
            for c in range(N // width):
                rows, cols = pl.ds(pl.multiple_of(i * 8, 8), 8), pl.ds(c * width, width)
                label = label_ref[l, rows, cols]
                root_out[l, rows, cols] = pick(label, root_ref, 3, 0)
                inv_out[l, rows, cols] = pick(label, inv_ref, 3, 0)
        return carry

    lax.fori_loop(0, ROWS // 8, body, 0)


def wells_kernel(where1_ref, where2_ref, amount_ref, col_ref, out1_ref, out2_ref):
    def hits(where_ref, rows, s):
        row = lax.broadcasted_iota(jnp.int32, (rows, 512), 0)
        return jnp.where(row == where_ref[...], amount_ref[s : s + 1, :], 0.0).astype(BF16)

    left = jnp.concatenate([hits(where1_ref, 256, 0), hits(where2_ref, 128, 1)], 0)
    col_of = jnp.broadcast_to(col_ref[...], (512, 256))
    for c in range(N // 256):
        at = slice(c * 256, (c + 1) * 256)
        col = lax.broadcasted_iota(jnp.int32, (512, 256), 1) + c * 256
        both = matmul(left, jnp.where(col == col_of, 1.0, 0.0).astype(BF16))
        out1_ref[:, at] = both[0:256]
        out2_ref[:, at] = both[256:384]


def pack_kernel(p_ref, q_ref, p_before, p_after, q_before, q_after, out_ref):
    width = 1024
    row = lax.broadcasted_iota(jnp.int32, (8, width), 0)
    for c in range(N // width):
        at = slice(c * width, (c + 1) * width)
        for v, (ref, before, after) in enumerate(((p_ref, p_before, p_after), (q_ref, q_before, q_after))):
            for d in range(DEPTHS):
                sides = []
                for l in range(2):
                    out_ref[d, v * 24 + l * 8 : v * 24 + l * 8 + 8, at] = ref[l, d * 8 : d * 8 + 8, at]
                    prev = ref[l, d * 8 - 8 : d * 8, at] if d else before[l, :, at]
                    then = ref[l, d * 8 + 8 : d * 8 + 16, at] if d < DEPTHS - 1 else after[l, :, at]
                    sides.append(jnp.where(row < 4, then, prev))
                both = jnp.where((row < 2) | (row >= 6), sides[0], pltpu.roll(sides[1], 4, 0))
                out_ref[d, v * 24 + 16 : v * 24 + 24, at] = both


def sideways(value, col):
    left = jnp.where(col == 0, 0.0, pltpu.roll(value, 1, 1))
    right = jnp.where(col == N - 1, 0.0, pltpu.roll(value, N - 1, 1))
    return left + right


def around(main, side, row):
    main_up, side_up = pltpu.roll(main, 1, 0), pltpu.roll(side, 1, 0)
    main_down, side_down = pltpu.roll(main, 7, 0), pltpu.roll(side, 7, 0)
    first, last = row == 0, row == 7
    of_main = jnp.where(first, side_up, main_up) + jnp.where(last, side_down, main_down)
    of_side = jnp.where(first, main_up, side_up) + jnp.where(last, main_down, side_down)
    return of_main, of_side


def diffuse_kernel(me_ref, msg_ref, src1_ref, src2_ref, fwd_ref, twist_ref, *rest):
    outs, spec_out, (q_ref, u_ref, w_ref, p_ref, s_ref, mid_ref) = rest[:8], rest[8], rest[9:]
    me = me_ref[0]
    zero = jnp.zeros((16, N), F32)
    for ref in (q_ref, u_ref, w_ref):
        ref[0] = zero
        ref[17] = zero
    row = lax.broadcasted_iota(jnp.int32, (8, N), 0)
    col = lax.broadcasted_iota(jnp.int32, (8, N), 1)

    def fill(d, carry):
        p_side, q_side = msg_ref[d, 16:24, :], msg_ref[d, 40:48, :]
        for l in range(2):
            z = d * 2 + l + 1
            q, p = msg_ref[d, 24 + l * 8 : 32 + l * 8, :], msg_ref[d, l * 8 : l * 8 + 8, :]
            q_ref[z, 0:8, :] = q
            u_ref[z, 0:8, :] = q * p
            q = q_side if l == 0 else pltpu.roll(q_side, 4, 0)
            p = p_side if l == 0 else pltpu.roll(p_side, 4, 0)
            q_ref[z, 8:16, :] = q
            u_ref[z, 8:16, :] = q * p
            p_ref[z - 1, 8:16, :] = p
        return carry

    lax.fori_loop(0, DEPTHS, fill, 0)

    def first(z, carry):
        d, l = z // 2, z % 2
        q, q_side = q_ref[z + 1, 0:8, :], q_ref[z + 1, 8:16, :]
        sums, sides = around(q, q_side, row)
        s = sums + sideways(q, col) + (q_ref[z, 0:8, :] + q_ref[z + 2, 0:8, :])
        s_side = sides + sideways(q_side, col) + (q_ref[z, 8:16, :] + q_ref[z + 2, 8:16, :])
        u, u_side = u_ref[z + 1, 0:8, :], u_ref[z + 1, 8:16, :]
        sums, sides = around(u, u_side, row)
        t = sums + sideways(u, col) + (u_ref[z, 0:8, :] + u_ref[z + 2, 0:8, :])
        t_side = sides + sideways(u_side, col) + (u_ref[z, 8:16, :] + u_ref[z + 2, 8:16, :])
        at = pl.ds(pl.multiple_of(z * 16, 16), 8)
        side_at = pl.ds(pl.multiple_of(z * 16 + 8, 8), 8)
        p = msg_ref[d, pl.ds(pl.multiple_of(l * 8, 8), 8), :]
        new = p + (conduct * q) * (t - p * s) + src1_ref[at, :]
        p_side = p_ref[z, 8:16, :]
        new_side = p_side + (conduct * q_side) * (t_side - p_side * s_side) + src1_ref[side_at, :]
        s_ref[z] = s
        p_ref[z, 0:8, :] = new
        w_ref[z + 1, 0:8, :] = q * new
        w_ref[z + 1, 8:16, :] = q_side * new_side
        return carry

    lax.fori_loop(0, 2 * DEPTHS, first, 0)

    for k in range(DEPTHS):
        d = lax.rem(me + k, DEPTHS)
        for l in range(2):
            z = d * 2 + l
            w = w_ref[z + 1, 0:8, :]
            sums, _ = around(w, w_ref[z + 1, 8:16, :], row)
            t = sums + sideways(w, col) + (w_ref[z, 0:8, :] + w_ref[z + 2, 0:8, :])
            p = p_ref[z, 0:8, :]
            at = pl.ds(pl.multiple_of(z * 8, 8), 8)
            new = p + (conduct * q_ref[z + 1, 0:8, :]) * (t - p * s_ref[z]) + src2_ref[at, :]
            outs[k][l] = new
        spectrum_of_rows(outs[k], twist_ref, mid_ref, d)
    for c in range(4):
        part = triple(mid_ref[c * 256 : (c + 1) * 256, :], 1)
        block = lax.dot_general(fwd_ref[...], part, (((1,), (1,)), ((), ())), preferred_element_type=F32)
        for h in range(2):
            spec_out[:, c * 2 + h] = block[:, h * 128 : (h + 1) * 128].reshape(SLABS, 8, 128)


def spectrum_of_rows(p_ref, twist_ref, mid_ref, d):
    items = [(p_ref[0, :, n * 128 : (n + 1) * 128], p_ref[1, :, n * 128 : (n + 1) * 128]) for n in range(TILES)]
    for k, (re, im) in enumerate(dft16(items, -1)):
        if k:
            cos, sin = twist_ref[0, k : k + 1, :], twist_ref[1, k : k + 1, :]
            re, im = re * cos - im * sin, re * sin + im * cos
        at = pl.ds(pl.multiple_of(d * 128 + k * 8, 8), 8)
        mid_ref[at, 0:128] = re
        mid_ref[at, 128:256] = im


def dft8(items, sign):
    even, odd = radix4(items[0::2], sign), radix4(items[1::2], sign)
    odd = [scale_by(item, sign * 2.0 * math.pi * k / 8) for k, item in enumerate(odd)]
    plus = [(a[0] + b[0], a[1] + b[1]) for a, b in zip(even, odd)]
    minus = [(a[0] - b[0], a[1] - b[1]) for a, b in zip(even, odd)]
    return plus + minus


def turn(item, cos, sin, sign):
    re, im = item
    if sign < 0:
        return re * cos - im * sin, re * sin + im * cos
    return re * cos + im * sin, im * cos - re * sin


def across(ref, sign, col_ref, in_ref):
    def body(i, carry):
        at = pl.ds(pl.multiple_of(i * 8, 8), 8)

        def by_block(items):
            return [turn(item, col_ref[0, d, at, :], col_ref[1, d, at, :], sign) for d, item in enumerate(items)]

        def by_digit(items):
            return [turn(item, in_ref[0, d : d + 1, :], in_ref[1, d : d + 1, :], sign) for d, item in enumerate(items)]

        items = [(ref[0, d, at, :], ref[1, d, at, :]) for d in range(DEPTHS)]
        items = by_block(items) if sign < 0 else by_digit(items)
        items = dft8(items, sign)
        items = by_digit(items) if sign < 0 else by_block(items)
        for d, (re, im) in enumerate(items):
            ref[0, d, at, :] = re
            ref[1, d, at, :] = im
        return carry

    lax.fori_loop(0, STEP // 8, body, 0)


def middle_kernel(
    spec_ref, green_ref, mid_ref, mid_inv_ref, inner_ref, inner_inv_ref, col_ref, in_ref, out_ref, work
):
    for d in range(0, DEPTHS, 2):
        part = jnp.concatenate([spec_ref[:, d + h].reshape(256, 128) for h in range(2)], 1)
        spread = matmul(mid_ref[...], triple(part, 0))
        for h in range(2):
            work[0, d + h] = spread[0:128, h * 128 : (h + 1) * 128]
            work[1, d + h] = spread[128:256, h * 128 : (h + 1) * 128]
    across(work, -1, col_ref, in_ref)
    for k in range(0, DEPTHS, 2):
        part = [jnp.concatenate([work[0, k + h], work[1, k + h]], 1) for h in range(2)]
        freq = matmul(triple(jnp.concatenate(part, 0), 1), inner_ref[...])
        green = jnp.concatenate([green_ref[k], green_ref[k + 1]], 0)
        freq = freq * jnp.concatenate([green, green], 1)
        back = matmul(triple(freq, 1), inner_inv_ref[...])
        for h in range(2):
            work[0, k + h] = back[h * 128 : (h + 1) * 128, 0:128]
            work[1, k + h] = back[h * 128 : (h + 1) * 128, 128:256]
    across(work, 1, col_ref, in_ref)
    for d in range(0, DEPTHS, 2):
        part = [jnp.concatenate([work[0, d + h], work[1, d + h]], 0) for h in range(2)]
        out_ref[:, d * 128 : (d + 2) * 128] = matmul(mid_inv_ref[...], triple(jnp.concatenate(part, 1), 0))


def last_kernel(me_ref, weight_ref, spec_ref, inv_ref, seis_ref, table_ref, twist_ref, *rest):
    parts, (p_out, state_out, rate_out, mid_ref) = rest[:DEPTHS], rest[DEPTHS:]
    me = me_ref[0]
    for c in range(4):
        turned = jnp.transpose(spec_ref[:, c * 256 : (c + 1) * 256])
        mid_ref[c * 256 : (c + 1) * 256, :] = matmul(triple(turned, 1), table_ref[...])
    for k in range(DEPTHS):
        d = lax.rem(me + (DEPTHS - k), DEPTHS)
        p_out[:, pl.ds(pl.multiple_of(d * 8, 8), 8), :] = parts[k][...]

    def body(i, carry):
        rows = pl.ds(pl.multiple_of(i * 8, 8), 8)
        items = []
        for k in range(TILES):
            at = pl.ds(pl.multiple_of(i * 128 + k * 8, 8), 8)
            re, im = mid_ref[at, 0:128], mid_ref[at, 128:256]
            if k:
                cos, sin = twist_ref[0, k : k + 1, :], twist_ref[1, k : k + 1, :]
                re, im = re * cos + im * sin, im * cos - re * sin
            items.append((re, im))
        for n, stress in enumerate(dft16(items, 1)):
            at = slice(n * 128, (n + 1) * 128)
            total = None
            for l in range(2):
                coulomb = stress[l] + friction * p_out[l, rows, at]
                grown = seis_ref[l, rows, at] * jnp.exp(-coulomb * inv_ref[l, rows, at])
                state = 1.0 + (grown - 1.0) * recovery
                state_out[l, rows, at] = state
                term = weight_ref[l] / state
                total = term if total is None else total + term
            rate_out[n // 2, rows, (n % 2) * 128 : (n % 2) * 128 + 128] = total
        return carry

    lax.fori_loop(0, ROWS // 8, body, 0)


def sum_kernel(part_ref, out_ref):
    total = part_ref[0]
    for d in range(1, DEPTHS):
        total = total + part_ref[d]
    out_ref[...] = total


def vec(*shape):
    return jax.ShapeDtypeStruct(shape, F32)


def in_vmem(count):
    return [pl.BlockSpec(memory_space=pltpu.VMEM)] * count


def in_smem(count):
    return [pl.BlockSpec(memory_space=pltpu.SMEM)] * count


def call(kernel, mib, outs, smem, args, scratch=()):
    return pl.pallas_call(
        kernel,
        out_shape=outs,
        in_specs=in_smem(smem) + in_vmem(len(args) - smem),
        out_specs=tuple(in_vmem(len(outs))) if isinstance(outs, tuple) else in_vmem(1)[0],
        scratch_shapes=[pltpu.VMEM(s, F32) for s in scratch],
        compiler_params=pltpu.CompilerParams(vmem_limit_bytes=mib * 1024 * 1024),
    )(*args)


def shift(value, axis, step):
    peers = lax.axis_size(axis)
    pairs = [(i, i + step) for i in range(peers) if 0 <= i + step < peers]
    return lax.ppermute(value, axis, pairs)


def shards(pressure, zone_labels, perm_table, asig_table, well_cells, rate_levels, green_spectrum, seis_state):
    tab = {name: jnp.asarray(value) for name, value in tables().items()}
    depth, slab = lax.axis_index("depth"), lax.axis_index("slab")
    me = depth.reshape(1)
    block = vec(2, ROWS, N)

    p_before = shift(pressure[:, ROWS - 8 :], "slab", 1)
    p_after = shift(pressure[:, :8], "slab", -1)
    root, inv = call(
        lookup_kernel, 12, (block, block), 2, (jnp.sqrt(perm_table), 1.0 / asig_table, zone_labels)
    )
    q_before = shift(root[:, ROWS - 8 :], "slab", 1)
    q_after = shift(root[:, :8], "slab", -1)

    offset = well_cells[:, 1] - (slab * ROWS + depth * 8)
    near = (offset >= -2) & (offset < 10)
    spot1 = jnp.where(near, well_cells[:, 0] * 16 + (offset & 15), -1)[None, :]
    own = (offset >= 0) & (offset < 8)
    spot2 = jnp.where(own, well_cells[:, 0] * 8 + offset, -1)[None, :]
    amounts = rate_unit * rate_levels.astype(F32)
    src1, src2 = call(wells_kernel, 12, (vec(256, N), vec(128, N)), 0, (spot1, spot2, amounts, well_cells[:, 2:3]))

    green = (green_spectrum * (1.0 / (N * N))).reshape(8, 8, SLABS, FREQS, TILES)
    green = green.transpose(1, 2, 3, 4, 0).reshape(8, STEP, LANES)

    msg = call(pack_kernel, 14, vec(DEPTHS, 48, N), 0, (pressure, root, p_before, p_after, q_before, q_after))
    msg = lax.all_to_all(msg, "depth", 0, 0, tiled=True)
    *parts, spec = call(
        diffuse_kernel,
        30,
        (vec(2, 8, N),) * DEPTHS + (vec(SLABS, DEPTHS, 8, LANES),),
        1,
        (me, msg, src1, src2, tab["fwd"], tab["row_twist"]),
        ((18, 16, N), (18, 16, N), (18, 16, N), (16, 16, N), (16, 8, N), (1024, 256)),
    )
    spec = lax.all_to_all(spec.reshape(SLABS * DEPTHS, 8, LANES), ("slab", "depth"), 0, 0, tiled=True)
    for k in range(1, DEPTHS):
        parts[k] = lax.ppermute(parts[k], "depth", [(i, (i + k) % DEPTHS) for i in range(DEPTHS)])
    spec = call(
        middle_kernel,
        24,
        vec(256, 1024),
        0,
        (spec.reshape(SLABS, DEPTHS, 8, LANES), green, tab["mid"], tab["mid_inv"], tab["inner"], tab["inner_inv"],
         tab["col_twist"], tab["in_twist"]),
        ((2, DEPTHS, STEP, LANES),),
    )
    spec = lax.all_to_all(spec.reshape(SLABS, 8, 1024), "slab", 0, 0, tiled=True).reshape(256, 1024)
    layer_pos = (depth * 2 + jnp.arange(2, dtype=jnp.int32)).astype(F32)
    weights = (1.0 + 2.0 * layer_pos / (2 * DEPTHS - 1)) / (4.0 * DEPTHS)
    press, state, rate = call(
        last_kernel,
        18,
        (block, block, vec(DEPTHS, ROWS, 2 * LANES)),
        2,
        (me, weights, spec, inv, seis_state, tab["inv"], tab["row_twist"], *parts),
        ((1024, 256),),
    )
    rate = lax.all_to_all(rate, "depth", 0, 0, tiled=True)
    rate_map = call(sum_kernel, 4, vec(ROWS, 2 * LANES), 0, (rate,))
    return (press, state, rate_map)


def solution(mesh):
    in_specs = (
        P("depth", "slab", None),
        P("depth", "slab", None),
        P(),
        P(),
        P(),
        P(),
        P(None, "slab"),
        P("depth", "slab", None),
    )
    out_specs = (P("depth", "slab", None), P("depth", "slab", None), P("slab", "depth"))
    return jax.shard_map(shards, mesh=mesh, in_specs=in_specs, out_specs=out_specs, check_vma=False)
```

```python
import functools
import math

import jax
import jax.numpy as jnp
import ml_dtypes
import numpy as np
from jax import lax
from jax.experimental import pallas as pl
from jax.experimental.pallas import tpu as pltpu
from jax.sharding import PartitionSpec as P

conduct = 0.15
rate_unit = 0.5
friction = 0.6
recovery = 0.6065306597126334

LANES = 128
SLABS = 32
DEPTHS = 8
N = 2048
ROWS = N // SLABS
TILES = N // LANES
FREQS = LANES // SLABS
STEP = SLABS * FREQS
F32 = jnp.float32
BF16 = jnp.bfloat16


def blocks(theta):
    cos, sin = np.cos(theta), np.sin(theta)
    return np.stack([np.stack([cos, -sin]), np.stack([sin, cos])])


def halves(table):
    high = table.astype(ml_dtypes.bfloat16)
    low = (table - high.astype(np.float64)).astype(ml_dtypes.bfloat16)
    return high, low


def left_table(table):
    high, low = halves(table)
    return np.concatenate([high, high, low], 1)


def right_table(table):
    high, low = halves(table)
    return np.concatenate([high, high, low], 0)


@functools.lru_cache(maxsize=None)
def tables():
    two_pi = 2.0 * np.pi
    k2, n2 = np.arange(128)[:, None], np.arange(128)[None, :]
    fwd = blocks(-two_pi * ((k2 * n2) % 128) / 128)
    fwd = fwd.reshape(2, 2, SLABS, FREQS, 128).transpose(2, 0, 3, 1, 4).reshape(256, 256)
    inv = blocks(two_pi * ((k2 * n2) % 128) / 128)
    inv = inv.reshape(2, 2, 128, SLABS, FREQS).transpose(3, 1, 4, 0, 2).reshape(256, 256)
    i, k = np.arange(SLABS)[:, None], np.arange(SLABS)[None, :]
    eye = np.eye(FREQS)
    angle = two_pi * ((i * k) % SLABS) / SLABS
    mid = np.einsum("absk,ij->akisbj", blocks(-angle), eye).reshape(256, 256)
    mid_inv = np.einsum("absk,ij->saibkj", blocks(angle), eye).reshape(256, 256)
    r, q = np.arange(8)[:, None], np.arange(8)[None, :]
    many = np.eye(TILES)
    angle = two_pi * ((r * q) % 8) / 8
    inner = np.einsum("abrq,ij->bjraiq", blocks(-angle), many).reshape(256, 256)
    inner_inv = np.einsum("abrq,ij->bjqair", blocks(angle), many).reshape(256, 256)
    row_angle = -two_pi * ((np.arange(TILES)[:, None] * np.arange(128)[None, :]) % N) / N
    row_twist = np.stack([np.cos(row_angle), np.sin(row_angle)]).astype(np.float32)
    row = (8 * np.arange(8)[:, None] + np.arange(8)[None, :])[:, None, :]
    col_angle = -two_pi * ((row * np.arange(SLABS)[None, :, None]) % N) / N
    col_angle = np.tile(np.repeat(col_angle, FREQS, 1), (1, 1, TILES))
    col_twist = np.stack([np.cos(col_angle), np.sin(col_angle)]).astype(np.float32)
    in_angle = np.tile(-two_pi * ((r * q) % 64) / 64, (1, TILES))
    in_twist = np.stack([np.cos(in_angle), np.sin(in_angle)]).astype(np.float32)
    return {
        "fwd": left_table(fwd),
        "inv": right_table(inv),
        "mid": left_table(mid),
        "mid_inv": left_table(mid_inv),
        "inner": right_table(inner),
        "inner_inv": right_table(inner_inv),
        "row_twist": row_twist,
        "col_twist": col_twist,
        "in_twist": in_twist,
    }


def triple(value, axis):
    high = value.astype(BF16)
    low = (value - high.astype(F32)).astype(BF16)
    return jnp.concatenate([high, low, high], axis)


def matmul(left, right):
    return jnp.dot(left, right, preferred_element_type=F32)


def radix4(items, sign):
    (ar, ai), (br, bi), (cr, ci), (dr, di) = items
    pr, pi, mr, mi = ar + cr, ai + ci, ar - cr, ai - ci
    qr, qi, nr, ni = br + dr, bi + di, br - dr, bi - di
    tr, ti = (-ni, nr) if sign > 0 else (ni, -nr)
    return [(pr + qr, pi + qi), (mr + tr, mi + ti), (pr - qr, pi - qi), (mr - tr, mi - ti)]


def scale_by(item, angle):
    c, s = math.cos(angle), math.sin(angle)
    re, im = item
    if abs(s) < 1e-12:
        return (re, im) if c > 0 else (-re, -im)
    if abs(c) < 1e-12:
        return (-im, re) if s > 0 else (im, -re)
    return (re * c - im * s, re * s + im * c)


def dft16(items, sign):
    mids = [radix4([items[4 * b + a] for b in range(4)], sign) for a in range(4)]
    out = [None] * 16
    for k in range(4):
        column = [scale_by(mids[a][k], sign * 2.0 * math.pi * a * k / 16) for a in range(4)]
        for m, item in enumerate(radix4(column, sign)):
            out[k + 4 * m] = item
    return out


def pick(label, table, bit, base):
    if bit < 0:
        return table[base]
    mask = (label & (1 << bit)) != 0
    return jnp.where(mask, pick(label, table, bit - 1, base + (1 << bit)), pick(label, table, bit - 1, base))


def start(src, dst, sem):
    copy = pltpu.make_async_copy(src, dst, sem)
    copy.start()
    return copy


def rows_of(d):
    return pl.ds(pl.multiple_of(d * 8, 8), 8)


def lookup_kernel(root_ref, inv_ref, label_hbm, p_hbm, root_out, inv_out, p_out, label, sems):
    copy = start(p_hbm, p_out, sems.at[8])
    loads = [start(label_hbm.at[:, rows_of(d), :], label.at[:, rows_of(d), :], sems.at[d]) for d in range(DEPTHS)]
    width = 512
    for d in range(DEPTHS):
        loads[d].wait()

        def body(c, carry, d=d):
            cols = pl.ds(pl.multiple_of(c * width, width), width)
            for l in range(2):
                zone = label[l, rows_of(d), cols]
                root_out[l, rows_of(d), cols] = pick(zone, root_ref, 3, 0)
                inv_out[l, rows_of(d), cols] = pick(zone, inv_ref, 3, 0)
            return carry

        lax.fori_loop(0, N // width, body, 0)
    copy.wait()


def wells_kernel(where1_ref, where2_ref, amount_ref, col_ref, out1_ref, out2_ref, buf, sems):
    def hits(where_ref, rows, s):
        row = lax.broadcasted_iota(jnp.int32, (rows, 512), 0)
        return jnp.where(row == where_ref[...], amount_ref[s : s + 1, :], 0.0).astype(BF16)

    left = jnp.concatenate([hits(where1_ref, 256, 0), hits(where2_ref, 128, 1)], 0)
    col_of = jnp.broadcast_to(col_ref[...], (512, 256))
    for c in range(N // 256):
        at = slice(c * 256, (c + 1) * 256)
        col = lax.broadcasted_iota(jnp.int32, (512, 256), 1) + c * 256
        buf[:, at] = matmul(left, jnp.where(col == col_of, 1.0, 0.0).astype(BF16))
    copies = [start(buf.at[0:256, :], out1_ref, sems.at[0]), start(buf.at[256:384, :], out2_ref, sems.at[1])]
    for copy in copies:
        copy.wait()


def pack_kernel(root_ref, p_ref, q_ref, before_ref, after_ref, out_hbm, edge_ref, out_ref, sems):
    width = 512

    def outside(c, carry):
        cols = pl.ds(pl.multiple_of(c * width, width), width)
        for i, ref in enumerate((before_ref, after_ref)):
            for l in range(2):
                zone = ref[1, l, :, cols].astype(jnp.int32)
                edge_ref[i, l, :, cols] = jnp.where(zone > 0, pick(zone - 1, root_ref, 3, 0), 0.0)
        return carry

    lax.fori_loop(0, N // width, outside, 0)
    row = lax.broadcasted_iota(jnp.int32, (8, N), 0)
    copies = []
    for d in range(DEPTHS):
        for v, ref in enumerate((p_ref, q_ref)):
            sides = []
            for l in range(2):
                out_ref[d, v * 24 + l * 8 : v * 24 + l * 8 + 8, :] = ref[l, d * 8 : d * 8 + 8, :]
                if d:
                    prev = ref[l, d * 8 - 8 : d * 8, :]
                else:
                    prev = edge_ref[0, l] if v else before_ref[0, l]
                if d < DEPTHS - 1:
                    then = ref[l, d * 8 + 8 : d * 8 + 16, :]
                else:
                    then = edge_ref[1, l] if v else after_ref[0, l]
                sides.append(jnp.where(row < 4, then, prev))
            both = jnp.where((row < 2) | (row >= 6), sides[0], pltpu.roll(sides[1], 4, 0))
            out_ref[d, v * 24 + 16 : v * 24 + 24, :] = both
        copies.append(start(out_ref.at[d], out_hbm.at[d], sems.at[d]))
    for copy in copies:
        copy.wait()


def sideways(value, col):
    left = jnp.where(col == 0, 0.0, pltpu.roll(value, 1, 1))
    right = jnp.where(col == N - 1, 0.0, pltpu.roll(value, N - 1, 1))
    return left + right


def around(main, side, row):
    main_up, side_up = pltpu.roll(main, 1, 0), pltpu.roll(side, 1, 0)
    main_down, side_down = pltpu.roll(main, 7, 0), pltpu.roll(side, 7, 0)
    first, last = row == 0, row == 7
    of_main = jnp.where(first, side_up, main_up) + jnp.where(last, side_down, main_down)
    of_side = jnp.where(first, main_up, side_up) + jnp.where(last, main_down, side_down)
    return of_main, of_side


def diffuse_kernel(me_ref, msg_ref, src1_hbm, src2_hbm, fwd_hbm, twist_ref, *rest):
    outs, spec_hbm = rest[:8], rest[8]
    q_ref, u_ref, w_ref, p_ref, s_ref, mid_ref, new_ref, spec_out, src1_ref, src2_ref, fwd_ref, sems = rest[9:]
    me = me_ref[0]
    src1_load = start(src1_hbm, src1_ref, sems.at[0, 0])
    src2_load = start(src2_hbm, src2_ref, sems.at[0, 1])
    fwd_load = start(fwd_hbm, fwd_ref, sems.at[0, 2])
    zero = jnp.zeros((16, N), F32)
    for ref in (q_ref, u_ref, w_ref):
        ref[0] = zero
        ref[17] = zero
    row = lax.broadcasted_iota(jnp.int32, (8, N), 0)
    col = lax.broadcasted_iota(jnp.int32, (8, N), 1)

    def fill(d, carry):
        p_side, q_side = msg_ref[d, 16:24, :], msg_ref[d, 40:48, :]
        for l in range(2):
            z = d * 2 + l + 1
            q, p = msg_ref[d, 24 + l * 8 : 32 + l * 8, :], msg_ref[d, l * 8 : l * 8 + 8, :]
            q_ref[z, 0:8, :] = q
            u_ref[z, 0:8, :] = q * p
            q = q_side if l == 0 else pltpu.roll(q_side, 4, 0)
            p = p_side if l == 0 else pltpu.roll(p_side, 4, 0)
            q_ref[z, 8:16, :] = q
            u_ref[z, 8:16, :] = q * p
            p_ref[z - 1, 8:16, :] = p
        return carry

    lax.fori_loop(0, DEPTHS, fill, 0)
    src1_load.wait()

    def first(z, carry):
        q, q_side = q_ref[z + 1, 0:8, :], q_ref[z + 1, 8:16, :]
        sums, sides = around(q, q_side, row)
        s = sums + sideways(q, col) + (q_ref[z, 0:8, :] + q_ref[z + 2, 0:8, :])
        s_side = sides + sideways(q_side, col) + (q_ref[z, 8:16, :] + q_ref[z + 2, 8:16, :])
        u, u_side = u_ref[z + 1, 0:8, :], u_ref[z + 1, 8:16, :]
        sums, sides = around(u, u_side, row)
        t = sums + sideways(u, col) + (u_ref[z, 0:8, :] + u_ref[z + 2, 0:8, :])
        t_side = sides + sideways(u_side, col) + (u_ref[z, 8:16, :] + u_ref[z + 2, 8:16, :])
        at = pl.ds(pl.multiple_of(z * 16, 16), 8)
        side_at = pl.ds(pl.multiple_of(z * 16 + 8, 8), 8)
        p = msg_ref[z // 2, pl.ds(pl.multiple_of(z % 2 * 8, 8), 8), :]
        new = p + (conduct * q) * (t - p * s) + src1_ref[at, :]
        p_side = p_ref[z, 8:16, :]
        new_side = p_side + (conduct * q_side) * (t_side - p_side * s_side) + src1_ref[side_at, :]
        s_ref[z] = s
        p_ref[z, 0:8, :] = new
        w_ref[z + 1, 0:8, :] = q * new
        w_ref[z + 1, 8:16, :] = q_side * new_side
        return carry

    lax.fori_loop(0, 2 * DEPTHS, first, 0)

    src2_load.wait()
    copies = []
    for k in (1, 2, 3, 4, 5, 6, 7, 0):
        d = lax.rem(me + k, DEPTHS)
        for l in range(2):
            z = d * 2 + l
            w = w_ref[z + 1, 0:8, :]
            sums, _ = around(w, w_ref[z + 1, 8:16, :], row)
            t = sums + sideways(w, col) + (w_ref[z, 0:8, :] + w_ref[z + 2, 0:8, :])
            p = p_ref[z, 0:8, :]
            new = p + (conduct * q_ref[z + 1, 0:8, :]) * (t - p * s_ref[z]) + src2_ref[rows_of(z), :]
            new_ref[k, l] = new
        copies.append(start(new_ref.at[k], outs[k], sems.at[1, k]))
        spectrum_of_rows(new_ref.at[k], twist_ref, mid_ref, d)
    fwd_load.wait()
    for c in range(4):
        part = triple(mid_ref[c * 256 : (c + 1) * 256, :], 1)
        block = lax.dot_general(fwd_ref[...], part, (((1,), (1,)), ((), ())), preferred_element_type=F32)
        for h in range(2):
            at = c * 2 + h
            spec_out[:, at] = block[:, h * 128 : (h + 1) * 128].reshape(SLABS, 8, 128)
            copies.append(start(spec_out.at[:, at], spec_hbm.at[:, at], sems.at[2, at]))
    for copy in copies:
        copy.wait()


def spectrum_of_rows(p_ref, twist_ref, mid_ref, d):
    items = [(p_ref[0, :, n * 128 : (n + 1) * 128], p_ref[1, :, n * 128 : (n + 1) * 128]) for n in range(TILES)]
    for k, (re, im) in enumerate(dft16(items, -1)):
        if k:
            cos, sin = twist_ref[0, k : k + 1, :], twist_ref[1, k : k + 1, :]
            re, im = re * cos - im * sin, re * sin + im * cos
        at = pl.ds(pl.multiple_of(d * 128 + k * 8, 8), 8)
        mid_ref[at, 0:128] = re
        mid_ref[at, 128:256] = im


def dft8(items, sign):
    even, odd = radix4(items[0::2], sign), radix4(items[1::2], sign)
    odd = [scale_by(item, sign * 2.0 * math.pi * k / 8) for k, item in enumerate(odd)]
    plus = [(a[0] + b[0], a[1] + b[1]) for a, b in zip(even, odd)]
    minus = [(a[0] - b[0], a[1] - b[1]) for a, b in zip(even, odd)]
    return plus + minus


def turn(item, cos, sin, sign):
    re, im = item
    if sign < 0:
        return re * cos - im * sin, re * sin + im * cos
    return re * cos + im * sin, im * cos - re * sin


def across(ref, sign, col_ref, in_ref):
    def body(i, carry):
        at = pl.ds(pl.multiple_of(i * 8, 8), 8)

        def by_block(items):
            return [turn(item, col_ref[0, d, at, :], col_ref[1, d, at, :], sign) for d, item in enumerate(items)]

        def by_digit(items):
            return [turn(item, in_ref[0, d : d + 1, :], in_ref[1, d : d + 1, :], sign) for d, item in enumerate(items)]

        items = [(ref[0, d, at, :], ref[1, d, at, :]) for d in range(DEPTHS)]
        items = by_block(items) if sign < 0 else by_digit(items)
        items = dft8(items, sign)
        items = by_digit(items) if sign < 0 else by_block(items)
        for d, (re, im) in enumerate(items):
            ref[0, d, at, :] = re
            ref[1, d, at, :] = im
        return carry

    lax.fori_loop(0, STEP // 8, body, 0)


def middle_kernel(
    spec_ref, green_ref, mid_hbm, mid_inv_hbm, inner_hbm, inner_inv_hbm, col_hbm, in_ref, out_hbm,
    work, out_ref, mid_ref, mid_inv_ref, inner_ref, inner_inv_ref, col_ref, sems,
):
    pairs = (
        (mid_hbm, mid_ref), (col_hbm, col_ref), (inner_hbm, inner_ref), (inner_inv_hbm, inner_inv_ref),
        (mid_inv_hbm, mid_inv_ref),
    )
    loads = [start(src, dst, sems.at[i]) for i, (src, dst) in enumerate(pairs)]
    loads[0].wait()
    for d in range(0, DEPTHS, 2):
        part = jnp.concatenate([spec_ref[:, d + h].reshape(256, 128) for h in range(2)], 1)
        spread = matmul(mid_ref[...], triple(part, 0))
        for h in range(2):
            work[0, d + h] = spread[0:128, h * 128 : (h + 1) * 128]
            work[1, d + h] = spread[128:256, h * 128 : (h + 1) * 128]
    for copy in loads[1:]:
        copy.wait()
    across(work, -1, col_ref, in_ref)
    for k in range(0, DEPTHS, 2):
        part = [jnp.concatenate([work[0, k + h], work[1, k + h]], 1) for h in range(2)]
        freq = matmul(triple(jnp.concatenate(part, 0), 1), inner_ref[...])
        green = jnp.concatenate([green_ref[k], green_ref[k + 1]], 0)
        freq = freq * jnp.concatenate([green, green], 1)
        back = matmul(triple(freq, 1), inner_inv_ref[...])
        for h in range(2):
            work[0, k + h] = back[h * 128 : (h + 1) * 128, 0:128]
            work[1, k + h] = back[h * 128 : (h + 1) * 128, 128:256]
    across(work, 1, col_ref, in_ref)
    copies = []
    for d in range(0, DEPTHS, 2):
        part = [jnp.concatenate([work[0, d + h], work[1, d + h]], 0) for h in range(2)]
        at = slice(d * 128, (d + 2) * 128)
        out_ref[:, at] = matmul(mid_inv_ref[...], triple(jnp.concatenate(part, 1), 0))
        copies.append(start(out_ref.at[:, at], out_hbm.at[:, at], sems.at[5 + d]))
    for copy in copies:
        copy.wait()


def last_kernel(me_ref, weight_ref, spec_ref, inv_hbm, seis_hbm, table_hbm, twist_ref, *rest):
    parts, rest = rest[:DEPTHS], rest[DEPTHS:]
    p_out, state_out, rate_out, rest = rest[0], rest[1], rest[2], rest[3:]
    p_ref, inv_ref, seis_ref, table_ref, state_ref, rate_ref, mid_ref, sems = rest
    me = me_ref[0]
    table_load = start(table_hbm, table_ref, sems.at[4, 0])
    loads = [start(inv_hbm, inv_ref, sems.at[4, 1]), start(seis_hbm, seis_ref, sems.at[4, 2])]
    copies = []
    for k in range(DEPTHS):
        d = lax.rem(me + (DEPTHS - k), DEPTHS)
        loads.append(start(parts[k], p_ref.at[:, rows_of(d), :], sems.at[0, k]))
    table_load.wait()
    for c in range(4):
        turned = jnp.transpose(spec_ref[:, c * 256 : (c + 1) * 256])
        mid_ref[c * 256 : (c + 1) * 256, :] = matmul(triple(turned, 1), table_ref[...])
    for copy in loads:
        copy.wait()
    copies.append(start(p_ref, p_out, sems.at[1, 0]))

    def body(i, carry):
        rows = rows_of(i)
        items = []
        for k in range(TILES):
            at = pl.ds(pl.multiple_of(i * 128 + k * 8, 8), 8)
            item = (mid_ref[at, 0:128], mid_ref[at, 128:256])
            if k:
                item = turn(item, twist_ref[0, k : k + 1, :], twist_ref[1, k : k + 1, :], 1)
            items.append(item)
        for n, stress in enumerate(dft16(items, 1)):
            at = slice(n * 128, (n + 1) * 128)
            total = None
            for l in range(2):
                coulomb = stress[l] + friction * p_ref[l, rows, at]
                grown = seis_ref[l, rows, at] * jnp.exp(-coulomb * inv_ref[l, rows, at])
                state = 1.0 + (grown - 1.0) * recovery
                state_ref[i, l, :, at] = state
                term = weight_ref[l] / state
                total = term if total is None else total + term
            rate_ref[n // 2, rows, (n % 2) * 128 : (n % 2) * 128 + 128] = total
        pltpu.make_async_copy(state_ref.at[i], state_out.at[:, rows, :], sems.at[2, i]).start()
        return carry

    lax.fori_loop(0, DEPTHS, body, 0)
    copies.append(start(rate_ref, rate_out, sems.at[3, 0]))
    for i in range(DEPTHS):
        pltpu.make_async_copy(state_ref.at[i], state_out.at[:, rows_of(i), :], sems.at[2, i]).wait()
    for copy in copies:
        copy.wait()


def sum_kernel(part_ref, out_ref):
    total = part_ref[0]
    for d in range(1, DEPTHS):
        total = total + part_ref[d]
    out_ref[...] = total


def vec(*shape):
    return jax.ShapeDtypeStruct(shape, F32)


SMEM, VMEM, ANY, HBM = pltpu.SMEM, pltpu.VMEM, pl.ANY, pltpu.HBM
DMA = pltpu.SemaphoreType.DMA


def call(kernel, mib, args, outs, scratch=()):
    values = [pltpu.with_memory_space_constraint(value, space) if space is HBM else value for space, value in args]
    return pl.pallas_call(
        kernel,
        out_shape=[HBM(shape, F32) if space is HBM else vec(*shape) for space, shape in outs],
        in_specs=[pl.BlockSpec(memory_space=space) for space, _ in args],
        out_specs=[pl.BlockSpec(memory_space=space) for space, _ in outs],
        scratch_shapes=scratch,
        compiler_params=pltpu.CompilerParams(vmem_limit_bytes=mib * 1024 * 1024),
    )(*values)


def buf(*shape, dtype=F32):
    return pltpu.VMEM(shape, dtype)


def shift(value, axis, step):
    peers = lax.axis_size(axis)
    pairs = [(i, i + step) for i in range(peers) if 0 <= i + step < peers]
    return lax.ppermute(value, axis, pairs)


def rotate(values):
    moved = [lax.ppermute(v, "depth", [(i, (i + k) % DEPTHS) for i in range(DEPTHS)]) for k, v in enumerate(values) if k]
    return [values[0]] + moved


def shards(pressure, zone_labels, perm_table, asig_table, well_cells, rate_levels, green_spectrum, seis_state):
    tab = {name: jnp.asarray(value) for name, value in tables().items()}
    depth, slab = lax.axis_index("depth"), lax.axis_index("slab")
    me = (SMEM, depth.reshape(1))
    rows, block = (2, 8, N), (2, ROWS, N)

    def edge(at):
        return jnp.stack([pressure[:, at], (zone_labels[:, at] + 1).astype(F32)])

    before, after = shift(edge(slice(ROWS - 8, ROWS)), "slab", 1), shift(edge(slice(0, 8)), "slab", -1)
    root_table = (SMEM, jnp.sqrt(perm_table))
    root, inv, p_copy = call(
        lookup_kernel,
        12,
        (root_table, (SMEM, 1.0 / asig_table), (HBM, zone_labels), (HBM, pressure)),
        [(VMEM, block)] * 3,
        [buf(*block, dtype=jnp.int32), DMA((9,))],
    )

    offset = well_cells[:, 1] - (slab * ROWS + depth * 8)
    near = (offset >= -2) & (offset < 10)
    spot1 = jnp.where(near, well_cells[:, 0] * 16 + (offset & 15), -1)[None, :]
    own = (offset >= 0) & (offset < 8)
    spot2 = jnp.where(own, well_cells[:, 0] * 8 + offset, -1)[None, :]
    amounts = rate_unit * rate_levels.astype(F32)
    src1, src2 = call(
        wells_kernel,
        12,
        ((VMEM, spot1), (VMEM, spot2), (VMEM, amounts), (VMEM, well_cells[:, 2:3])),
        [(HBM, (256, N)), (HBM, (128, N))],
        [buf(384, N), DMA((2,))],
    )

    green = (green_spectrum * (1.0 / (N * N))).reshape(8, 8, SLABS, FREQS, TILES)
    green = green.transpose(1, 2, 3, 4, 0).reshape(8, STEP, LANES)

    (msg,) = call(
        pack_kernel,
        16,
        (root_table, (VMEM, p_copy), (VMEM, root), (VMEM, before), (VMEM, after)),
        [(HBM, (DEPTHS, 48, N))],
        [buf(2, *rows), buf(DEPTHS, 48, N), DMA((8,))],
    )
    msg = lax.all_to_all(msg, "depth", 0, 0, tiled=True)
    *parts, spec = call(
        diffuse_kernel,
        30,
        (me, (VMEM, msg), (HBM, src1), (HBM, src2), (HBM, tab["fwd"]), (VMEM, tab["row_twist"])),
        [(HBM, rows)] * DEPTHS + [(HBM, (SLABS, DEPTHS, 8, LANES))],
        [buf(18, 16, N), buf(18, 16, N), buf(18, 16, N), buf(16, 16, N), buf(16, 8, N), buf(1024, 256),
         buf(8, *rows), buf(SLABS, DEPTHS, 8, LANES), buf(256, N), buf(128, N), buf(256, 768, dtype=BF16), DMA((3, 8))],
    )
    spec = lax.all_to_all(spec.reshape(SLABS * DEPTHS, 8, LANES), ("slab", "depth"), 0, 0, tiled=True)
    parts = rotate(parts)
    (spec,) = call(
        middle_kernel,
        16,
        ((VMEM, spec.reshape(SLABS, DEPTHS, 8, LANES)), (VMEM, green), (HBM, tab["mid"]), (HBM, tab["mid_inv"]),
         (HBM, tab["inner"]), (HBM, tab["inner_inv"]), (HBM, tab["col_twist"]), (VMEM, tab["in_twist"])),
        [(HBM, (256, 1024))],
        [buf(2, DEPTHS, STEP, LANES), buf(256, 1024), buf(256, 768, dtype=BF16), buf(256, 768, dtype=BF16),
         buf(768, 256, dtype=BF16), buf(768, 256, dtype=BF16), buf(2, 8, STEP, LANES), DMA((12,))],
    )
    spec = lax.all_to_all(spec.reshape(SLABS, 8, 1024), "slab", 0, 0, tiled=True).reshape(256, 1024)
    layer_pos = (depth * 2 + jnp.arange(2, dtype=jnp.int32)).astype(F32)
    weights = (1.0 + 2.0 * layer_pos / (2 * DEPTHS - 1)) / (4.0 * DEPTHS)
    press, state, rate = call(
        last_kernel,
        18,
        (me, (SMEM, weights), (VMEM, spec), (HBM, inv), (HBM, seis_state), (HBM, tab["inv"]), (VMEM, tab["row_twist"]),
         *[(ANY, v) for v in parts]),
        [(HBM, block)] * 2 + [(HBM, (DEPTHS, ROWS, 2 * LANES))],
        [buf(*block), buf(*block), buf(*block), buf(768, 256, dtype=BF16), buf(8, *rows),
         buf(DEPTHS, ROWS, 2 * LANES), buf(1024, 256), DMA((5, 8))],
    )
    rate = lax.all_to_all(rate, "depth", 0, 0, tiled=True)
    (rate_map,) = call(sum_kernel, 4, [(VMEM, rate)], [(VMEM, (ROWS, 2 * LANES))])
    return (press, state, rate_map)


def solution(mesh):
    in_specs = (
        P("depth", "slab", None),
        P("depth", "slab", None),
        P(),
        P(),
        P(),
        P(),
        P(None, "slab"),
        P("depth", "slab", None),
    )
    out_specs = (P("depth", "slab", None), P("depth", "slab", None), P("slab", "depth"))
    return jax.shard_map(shards, mesh=mesh, in_specs=in_specs, out_specs=out_specs, check_vma=False)
```

```python
import functools
import math

import jax
import jax.numpy as jnp
import ml_dtypes
import numpy as np
from jax import lax
from jax.experimental import pallas as pl
from jax.experimental.pallas import tpu as pltpu
from jax.sharding import PartitionSpec as P

conduct = 0.15
rate_unit = 0.5
friction = 0.6
recovery = 0.6065306597126334

LANES = 128
SLABS = 32
DEPTHS = 8
N = 2048
ROWS = N // SLABS
TILES = N // LANES
FREQS = LANES // SLABS
STEP = SLABS * FREQS
F32 = jnp.float32
BF16 = jnp.bfloat16


def blocks(theta):
    cos, sin = np.cos(theta), np.sin(theta)
    return np.stack([np.stack([cos, -sin]), np.stack([sin, cos])])


def halves(table):
    high = table.astype(ml_dtypes.bfloat16)
    low = (table - high.astype(np.float64)).astype(ml_dtypes.bfloat16)
    return high, low


def left_table(table):
    high, low = halves(table)
    return np.concatenate([high, high, low], 1)


def right_table(table):
    high, low = halves(table)
    return np.concatenate([high, high, low], 0)


@functools.lru_cache(maxsize=None)
def tables():
    two_pi = 2.0 * np.pi
    k2, n2 = np.arange(128)[:, None], np.arange(128)[None, :]
    fwd = blocks(-two_pi * ((k2 * n2) % 128) / 128)
    fwd = fwd.reshape(2, 2, SLABS, FREQS, 128).transpose(2, 0, 3, 1, 4).reshape(256, 256)
    inv = blocks(two_pi * ((k2 * n2) % 128) / 128)
    inv = inv.reshape(2, 2, 128, SLABS, FREQS).transpose(3, 1, 4, 0, 2).reshape(256, 256)
    i, k = np.arange(SLABS)[:, None], np.arange(SLABS)[None, :]
    eye = np.eye(FREQS)
    angle = two_pi * ((i * k) % SLABS) / SLABS
    mid = np.einsum("absk,ij->akisbj", blocks(-angle), eye).reshape(256, 256)
    mid_inv = np.einsum("absk,ij->saibkj", blocks(angle), eye).reshape(256, 256)
    r, q = np.arange(8)[:, None], np.arange(8)[None, :]
    many = np.eye(TILES)
    angle = two_pi * ((r * q) % 8) / 8
    inner = np.einsum("abrq,ij->bjraiq", blocks(-angle), many).reshape(256, 256)
    inner_inv = np.einsum("abrq,ij->bjqair", blocks(angle), many).reshape(256, 256)
    row_angle = -two_pi * ((np.arange(TILES)[:, None] * np.arange(128)[None, :]) % N) / N
    row_twist = np.stack([np.cos(row_angle), np.sin(row_angle)]).astype(np.float32)
    row = (8 * np.arange(8)[:, None] + np.arange(8)[None, :])[:, None, :]
    col_angle = -two_pi * ((row * np.arange(SLABS)[None, :, None]) % N) / N
    col_angle = np.tile(np.repeat(col_angle, FREQS, 1), (1, 1, TILES))
    col_twist = np.stack([np.cos(col_angle), np.sin(col_angle)]).astype(np.float32)
    in_angle = np.tile(-two_pi * ((r * q) % 64) / 64, (1, TILES))
    in_twist = np.stack([np.cos(in_angle), np.sin(in_angle)]).astype(np.float32)
    return {
        "fwd": left_table(fwd),
        "inv": right_table(inv),
        "mid": left_table(mid),
        "mid_inv": left_table(mid_inv),
        "inner": right_table(inner),
        "inner_inv": right_table(inner_inv),
        "row_twist": row_twist,
        "col_twist": col_twist,
        "in_twist": in_twist,
    }


def triple(value, axis):
    high = value.astype(BF16)
    low = (value - high.astype(F32)).astype(BF16)
    return jnp.concatenate([high, low, high], axis)


def matmul(left, right):
    return jnp.dot(left, right, preferred_element_type=F32)


def radix4(items, sign):
    (ar, ai), (br, bi), (cr, ci), (dr, di) = items
    pr, pi, mr, mi = ar + cr, ai + ci, ar - cr, ai - ci
    qr, qi, nr, ni = br + dr, bi + di, br - dr, bi - di
    tr, ti = (-ni, nr) if sign > 0 else (ni, -nr)
    return [(pr + qr, pi + qi), (mr + tr, mi + ti), (pr - qr, pi - qi), (mr - tr, mi - ti)]


def scale_by(item, angle):
    c, s = math.cos(angle), math.sin(angle)
    re, im = item
    if abs(s) < 1e-12:
        return (re, im) if c > 0 else (-re, -im)
    if abs(c) < 1e-12:
        return (-im, re) if s > 0 else (im, -re)
    return (re * c - im * s, re * s + im * c)


def dft16(items, sign):
    mids = [radix4([items[4 * b + a] for b in range(4)], sign) for a in range(4)]
    out = [None] * 16
    for k in range(4):
        column = [scale_by(mids[a][k], sign * 2.0 * math.pi * a * k / 16) for a in range(4)]
        for m, item in enumerate(radix4(column, sign)):
            out[k + 4 * m] = item
    return out


def pick(label, table, bit, base):
    if bit < 0:
        return table[base]
    mask = (label & (1 << bit)) != 0
    return jnp.where(mask, pick(label, table, bit - 1, base + (1 << bit)), pick(label, table, bit - 1, base))


def start(src, dst, sem):
    copy = pltpu.make_async_copy(src, dst, sem)
    copy.start()
    return copy


def rows_of(d):
    return pl.ds(pl.multiple_of(d * 8, 8), 8)


def edge_kernel(perm_hbm, p_hbm, label_hbm, first_out, last_out, perm_ref, label, sems):
    table = start(perm_hbm, perm_ref, sems.at[4])
    first, last = slice(0, 8), slice(ROWS - 8, ROWS)
    loads = [
        start(label_hbm.at[:, first, :], label.at[0], sems.at[0]),
        start(label_hbm.at[:, last, :], label.at[1], sems.at[1]),
        start(p_hbm.at[:, first, :], first_out.at[0], sems.at[2]),
        start(p_hbm.at[:, last, :], last_out.at[0], sems.at[3]),
    ]
    table.wait()
    for copy in loads:
        copy.wait()
    width = 1024

    def body(c, carry):
        cols = pl.ds(pl.multiple_of(c * width, width), width)
        for l in range(2):
            first_out[1, l, :, cols] = jnp.sqrt(pick(label[0, l, :, cols], perm_ref, 3, 0))
            last_out[1, l, :, cols] = jnp.sqrt(pick(label[1, l, :, cols], perm_ref, 3, 0))
        return carry

    lax.fori_loop(0, N // width, body, 0)


def each_part(label_hbm, label, sems, work, done):
    loads = [start(label_hbm.at[:, rows_of(d), :], label.at[:, rows_of(d), :], sems.at[d]) for d in range(DEPTHS)]
    width = 1024
    for d in range(DEPTHS):
        loads[d].wait()

        def body(c, carry, d=d):
            cols = pl.ds(pl.multiple_of(c * width, width), width)
            for l in range(2):
                work(label[l, rows_of(d), cols], (l, rows_of(d), cols))
            return carry

        lax.fori_loop(0, N // width, body, 0)
        done(d)


def lookup_kernel(perm_hbm, label_hbm, p_hbm, root_out, p_out, msg_hbm, perm_ref, label, sems, msg_sems):
    table = start(perm_hbm, perm_ref, sems.at[8])
    loads = [start(p_hbm.at[:, rows_of(d), :], p_out.at[:, rows_of(d), :], msg_sems.at[2, d]) for d in range(DEPTHS)]
    copies = []

    def work(zone, at):
        root_out[at] = jnp.sqrt(pick(zone, perm_ref, 3, 0))

    def done(d):
        loads[d].wait()
        copies.append(start(p_out.at[:, rows_of(d), :], msg_hbm.at[d, 0:2], msg_sems.at[1, d]))
        copies.append(start(root_out.at[:, rows_of(d), :], msg_hbm.at[d, 3:5], msg_sems.at[0, d]))

    table.wait()
    each_part(label_hbm, label, sems, work, done)
    for copy in copies:
        copy.wait()


def strength_kernel(asig_hbm, label_hbm, inv_hbm, asig_ref, label, inv, sems, inv_sems):
    start(asig_hbm, asig_ref, sems.at[8]).wait()
    copies = []

    def work(zone, at):
        inv[at] = 1.0 / pick(zone, asig_ref, 3, 0)

    def done(d):
        copies.append(start(inv.at[:, rows_of(d), :], inv_hbm.at[:, rows_of(d), :], inv_sems.at[d]))

    each_part(label_hbm, label, sems, work, done)
    for copy in copies:
        copy.wait()


def wells_kernel(where1_ref, where2_ref, amount_ref, col_ref, out1_ref, out2_ref, both, sems):
    def hits(where_ref, rows, s):
        row = lax.broadcasted_iota(jnp.int32, (rows, 512), 0)
        return jnp.where(row == where_ref[...], amount_ref[s : s + 1, :], 0.0).astype(BF16)

    left = jnp.concatenate([hits(where1_ref, 192, 0), hits(where2_ref, 128, 1)], 0)
    col_of = jnp.broadcast_to(col_ref[...], (512, 256))
    for c in range(N // 256):
        at = slice(c * 256, (c + 1) * 256)
        col = lax.broadcasted_iota(jnp.int32, (512, 256), 1) + c * 256
        both[:, at] = matmul(left, jnp.where(col == col_of, 1.0, 0.0).astype(BF16))
    copies = [start(both.at[0:192, :], out1_ref, sems.at[0]), start(both.at[192:320, :], out2_ref, sems.at[1])]
    for copy in copies:
        copy.wait()


def pack_kernel(p_ref, q_ref, before_ref, after_ref, msg_hbm, out_hbm, side_ref, sems):
    row = lax.broadcasted_iota(jnp.int32, (8, N), 0)
    copies = []
    for d in range(DEPTHS):
        for v, ref in enumerate((p_ref, q_ref)):
            sides = []
            for l in range(2):
                prev = ref[l, d * 8 - 8 : d * 8, :] if d else before_ref[v, l]
                then = ref[l, d * 8 + 8 : d * 8 + 16, :] if d < DEPTHS - 1 else after_ref[v, l]
                sides.append(jnp.where(row < 4, then, prev))
            side_ref[d, v] = jnp.where((row < 2) | (row >= 6), sides[0], pltpu.roll(sides[1], 4, 0))
            copies.append(start(side_ref.at[d, v], out_hbm.at[d, v * 3 + 2], sems.at[v, d]))
    for copy in copies:
        copy.wait()


class Tiles:
    def __init__(self, load):
        self.load, self.kept, self.turned = load, {}, {}

    def __getitem__(self, c):
        if c not in self.kept:
            self.kept[c] = self.load(c)
        return self.kept[c]

    def roll(self, c, by):
        if (c, by) not in self.turned:
            self.turned[c, by] = pltpu.roll(self[c], by, 1)
        return self.turned[c, by]

    def beside(self, c, lane):
        left = self.roll(c - 1, 1) if c else 0.0
        right = self.roll(c + 1, 127) if c < TILES - 1 else 0.0
        return jnp.where(lane == 0, left, self.roll(c, 1)) + jnp.where(lane == 127, right, self.roll(c, 127))


def of_rows(main0, main1, side, row):
    first, last = row == 0, row == 7
    up0 = jnp.where(first, pltpu.roll(side, 1, 0), pltpu.roll(main0, 1, 0))
    down0 = jnp.where(last, pltpu.roll(side, 7, 0), pltpu.roll(main0, 7, 0))
    up1 = jnp.where(first, pltpu.roll(side, 5, 0), pltpu.roll(main1, 1, 0))
    down1 = jnp.where(last, pltpu.roll(side, 3, 0), pltpu.roll(main1, 7, 0))
    return up0 + down0, up1 + down1


def of_side_rows(main0, main1, side, row):
    up = jnp.where(row == 0, pltpu.roll(main0, 1, 0), jnp.where(row == 4, pltpu.roll(main1, 5, 0), pltpu.roll(side, 1, 0)))
    down = jnp.where(row == 7, pltpu.roll(main0, 7, 0), jnp.where(row == 3, pltpu.roll(main1, 3, 0), pltpu.roll(side, 7, 0)))
    return up + down


def tile(c):
    return slice(c * LANES, (c + 1) * LANES)


def diffuse_kernel(me_ref, msg_ref, src1_hbm, src2_hbm, fwd_hbm, twist_ref, *rest):
    outs, spec_hbm = rest[:8], rest[8]
    w_ref, p_ref, s_ref, mid_ref, new_ref, spec_out, src1_ref, src2_ref, fwd_ref, sems = rest[9:]
    me = me_ref[0]
    for d in range(DEPTHS):
        start(src1_hbm.at[d], src1_ref.at[d], sems.at[3, d])
    src2_load = start(src2_hbm, src2_ref, sems.at[0, 1])
    fwd_load = start(fwd_hbm, fwd_ref, sems.at[0, 2])
    w_ref[0] = jnp.zeros((3, 8, N), F32)
    w_ref[DEPTHS + 1] = jnp.zeros((3, 8, N), F32)
    row = lax.broadcasted_iota(jnp.int32, (8, LANES), 0)
    lane = lax.broadcasted_iota(jnp.int32, (8, LANES), 1)
    of_second = (row >= 2) & (row < 6)

    def first(d, carry):
        below, above = jnp.maximum(d - 1, 0), jnp.minimum(d + 1, DEPTHS - 1)
        has_below, has_above = (d > 0).astype(F32), (d < DEPTHS - 1).astype(F32)
        pltpu.make_async_copy(src1_hbm.at[d], src1_ref.at[d], sems.at[3, d]).wait()
        q = [Tiles(lambda c, i=i: msg_ref[d, 3 + i, :, tile(c)]) for i in range(3)]
        p = [Tiles(lambda c, i=i: msg_ref[d, i, :, tile(c)]) for i in range(3)]
        u = [Tiles(lambda c, i=i: q[i][c] * p[i][c]) for i in range(3)]
        for c in range(TILES):
            at = tile(c)
            q_below = [msg_ref[below, 3 + i, :, at] * has_below for i in (1, 2)]
            q_above = [msg_ref[above, 3 + i, :, at] * has_above for i in (0, 2)]
            u_below = [x * msg_ref[below, i, :, at] for x, i in zip(q_below, (1, 2))]
            u_above = [x * msg_ref[above, i, :, at] for x, i in zip(q_above, (0, 2))]
            sums = []
            for own, low, high in ((q, q_below, q_above), (u, u_below, u_above)):
                x0, x1, side = own[0][c], own[1][c], own[2][c]
                sum0, sum1 = of_rows(x0, x1, side, row)
                depth = pltpu.roll(side + jnp.where(of_second, low[1], high[1]), 4, 0)
                sums.append((
                    sum0 + own[0].beside(c, lane) + (low[0] + x1),
                    sum1 + own[1].beside(c, lane) + (x0 + high[0]),
                    of_side_rows(x0, x1, side, row) + own[2].beside(c, lane) + depth,
                ))
            for i in range(3):
                s, t = sums[0][i], sums[1][i]
                new = p[i][c] + (conduct * q[i][c]) * (t - p[i][c] * s) + src1_ref[d, i, :, at]
                w_ref[d + 1, i, :, at] = q[i][c] * new
                if i < 2:
                    s_ref[d, i, :, at] = s
                    p_ref[d, i, :, at] = new
        return carry

    lax.fori_loop(0, DEPTHS, first, 0)
    src2_load.wait()

    def second(n, carry):
        k = lax.rem(n + 1, DEPTHS)
        d = lax.rem(me + k, DEPTHS)
        w = [Tiles(lambda c, i=i: w_ref[d + 1, i, :, tile(c)]) for i in range(3)]
        for c in range(TILES):
            at = tile(c)
            x0, x1 = w[0][c], w[1][c]
            sum0, sum1 = of_rows(x0, x1, w[2][c], row)
            t0 = sum0 + w[0].beside(c, lane) + (w_ref[d, 1, :, at] + x1)
            t1 = sum1 + w[1].beside(c, lane) + (x0 + w_ref[d + 2, 0, :, at])
            for l, t in ((0, t0), (1, t1)):
                p = p_ref[d, l, :, at]
                new_ref[k, l, :, at] = (
                    p + (conduct * msg_ref[d, 3 + l, :, at]) * (t - p * s_ref[d, l, :, at]) + src2_ref[d, l, :, at]
                )
        spectrum_of_rows(new_ref.at[k], twist_ref, mid_ref, d)
        return carry

    lax.fori_loop(0, DEPTHS, second, 0)
    copies = [start(new_ref.at[k], outs[k], sems.at[1, k]) for k in range(DEPTHS)]
    fwd_load.wait()
    for c in range(4):
        part = triple(mid_ref[c * 256 : (c + 1) * 256, :], 1)
        block = lax.dot_general(fwd_ref[...], part, (((1,), (1,)), ((), ())), preferred_element_type=F32)
        for h in range(2):
            at = c * 2 + h
            spec_out[:, at] = block[:, h * 128 : (h + 1) * 128].reshape(SLABS, 8, 128)
            copies.append(start(spec_out.at[:, at], spec_hbm.at[:, at], sems.at[2, at]))
    for copy in copies:
        copy.wait()


def spectrum_of_rows(p_ref, twist_ref, mid_ref, d):
    items = [(p_ref[0, :, n * 128 : (n + 1) * 128], p_ref[1, :, n * 128 : (n + 1) * 128]) for n in range(TILES)]
    for k, (re, im) in enumerate(dft16(items, -1)):
        if k:
            cos, sin = twist_ref[0, k : k + 1, :], twist_ref[1, k : k + 1, :]
            re, im = re * cos - im * sin, re * sin + im * cos
        at = pl.ds(pl.multiple_of(d * 128 + k * 8, 8), 8)
        mid_ref[at, 0:128] = re
        mid_ref[at, 128:256] = im


def dft8(items, sign):
    even, odd = radix4(items[0::2], sign), radix4(items[1::2], sign)
    odd = [scale_by(item, sign * 2.0 * math.pi * k / 8) for k, item in enumerate(odd)]
    plus = [(a[0] + b[0], a[1] + b[1]) for a, b in zip(even, odd)]
    minus = [(a[0] - b[0], a[1] - b[1]) for a, b in zip(even, odd)]
    return plus + minus


def turn(item, cos, sin, sign):
    re, im = item
    if sign < 0:
        return re * cos - im * sin, re * sin + im * cos
    return re * cos + im * sin, im * cos - re * sin


def across(ref, sign, col_ref, in_ref):
    def body(i, carry):
        at = pl.ds(pl.multiple_of(i * 8, 8), 8)

        def by_block(items):
            return [turn(item, col_ref[0, d, at, :], col_ref[1, d, at, :], sign) for d, item in enumerate(items)]

        def by_digit(items):
            return [turn(item, in_ref[0, d : d + 1, :], in_ref[1, d : d + 1, :], sign) for d, item in enumerate(items)]

        items = [(ref[0, d, at, :], ref[1, d, at, :]) for d in range(DEPTHS)]
        items = by_block(items) if sign < 0 else by_digit(items)
        items = dft8(items, sign)
        items = by_digit(items) if sign < 0 else by_block(items)
        for d, (re, im) in enumerate(items):
            ref[0, d, at, :] = re
            ref[1, d, at, :] = im
        return carry

    lax.fori_loop(0, STEP // 8, body, 0)


def middle_kernel(
    spec_ref, green_ref, mid_hbm, mid_inv_hbm, inner_hbm, inner_inv_hbm, col_hbm, in_ref, out_hbm,
    work, out_ref, mid_ref, mid_inv_ref, inner_ref, inner_inv_ref, col_ref, sems,
):
    pairs = (
        (mid_hbm, mid_ref), (col_hbm, col_ref), (inner_hbm, inner_ref), (inner_inv_hbm, inner_inv_ref),
        (mid_inv_hbm, mid_inv_ref),
    )
    loads = [start(src, dst, sems.at[i]) for i, (src, dst) in enumerate(pairs)]
    loads[0].wait()
    for d in range(0, DEPTHS, 2):
        part = jnp.concatenate([spec_ref[:, d + h].reshape(256, 128) for h in range(2)], 1)
        spread = matmul(mid_ref[...], triple(part, 0))
        for h in range(2):
            work[0, d + h] = spread[0:128, h * 128 : (h + 1) * 128]
            work[1, d + h] = spread[128:256, h * 128 : (h + 1) * 128]
    for copy in loads[1:]:
        copy.wait()
    across(work, -1, col_ref, in_ref)
    for k in range(0, DEPTHS, 2):
        part = [jnp.concatenate([work[0, k + h], work[1, k + h]], 1) for h in range(2)]
        freq = matmul(triple(jnp.concatenate(part, 0), 1), inner_ref[...])
        green = jnp.concatenate([green_ref[k], green_ref[k + 1]], 0)
        freq = freq * jnp.concatenate([green, green], 1)
        back = matmul(triple(freq, 1), inner_inv_ref[...])
        for h in range(2):
            work[0, k + h] = back[h * 128 : (h + 1) * 128, 0:128]
            work[1, k + h] = back[h * 128 : (h + 1) * 128, 128:256]
    across(work, 1, col_ref, in_ref)
    copies = []
    for d in range(0, DEPTHS, 2):
        part = [jnp.concatenate([work[0, d + h], work[1, d + h]], 0) for h in range(2)]
        at = slice(d * 128, (d + 2) * 128)
        out_ref[:, at] = matmul(mid_inv_ref[...], triple(jnp.concatenate(part, 1), 0))
        copies.append(start(out_ref.at[:, at], out_hbm.at[:, at], sems.at[5 + d]))
    for copy in copies:
        copy.wait()


def last_kernel(me_ref, weight_ref, spec_ref, inv_hbm, seis_hbm, table_hbm, twist_ref, *rest):
    parts, rest = rest[:DEPTHS], rest[DEPTHS:]
    p_out, state_out, rate_out, rest = rest[0], rest[1], rest[2], rest[3:]
    p_ref, inv_ref, seis_ref, table_ref, state_ref, rate_ref, mid_ref, sems = rest
    me = me_ref[0]
    table_load = start(table_hbm, table_ref, sems.at[4, 0])
    loads = [start(inv_hbm, inv_ref, sems.at[4, 1]), start(seis_hbm, seis_ref, sems.at[4, 2])]
    copies = []
    for k in range(DEPTHS):
        d = lax.rem(me + (DEPTHS - k), DEPTHS)
        loads.append(start(parts[k], p_ref.at[:, rows_of(d), :], sems.at[0, k]))
    table_load.wait()
    for c in range(4):
        turned = jnp.transpose(spec_ref[:, c * 256 : (c + 1) * 256])
        mid_ref[c * 256 : (c + 1) * 256, :] = matmul(triple(turned, 1), table_ref[...])
    for copy in loads:
        copy.wait()
    copies.append(start(p_ref, p_out, sems.at[1, 0]))

    def body(i, carry):
        rows = rows_of(i)
        items = []
        for k in range(TILES):
            at = pl.ds(pl.multiple_of(i * 128 + k * 8, 8), 8)
            item = (mid_ref[at, 0:128], mid_ref[at, 128:256])
            if k:
                item = turn(item, twist_ref[0, k : k + 1, :], twist_ref[1, k : k + 1, :], 1)
            items.append(item)
        for n, stress in enumerate(dft16(items, 1)):
            at = slice(n * 128, (n + 1) * 128)
            total = None
            for l in range(2):
                coulomb = stress[l] + friction * p_ref[l, rows, at]
                grown = seis_ref[l, rows, at] * jnp.exp(-coulomb * inv_ref[l, rows, at])
                state = 1.0 + (grown - 1.0) * recovery
                state_ref[i, l, :, at] = state
                term = weight_ref[l] / state
                total = term if total is None else total + term
            rate_ref[n // 2, rows, (n % 2) * 128 : (n % 2) * 128 + 128] = total
        pltpu.make_async_copy(state_ref.at[i], state_out.at[:, rows, :], sems.at[2, i]).start()
        return carry

    lax.fori_loop(0, DEPTHS, body, 0)
    copies.append(start(rate_ref, rate_out, sems.at[3, 0]))
    for i in range(DEPTHS):
        pltpu.make_async_copy(state_ref.at[i], state_out.at[:, rows_of(i), :], sems.at[2, i]).wait()
    for copy in copies:
        copy.wait()


def sum_kernel(part_ref, out_ref):
    total = part_ref[0]
    for d in range(1, DEPTHS):
        total = total + part_ref[d]
    out_ref[...] = total


def vec(*shape):
    return jax.ShapeDtypeStruct(shape, F32)


SMEM, VMEM, ANY, HBM = pltpu.SMEM, pltpu.VMEM, pl.ANY, pltpu.HBM
DMA = pltpu.SemaphoreType.DMA


def call(kernel, mib, args, outs, scratch=(), aliases={}):
    values = [pltpu.with_memory_space_constraint(value, space) if space is HBM else value for space, value in args]
    return pl.pallas_call(
        kernel,
        out_shape=[HBM(shape, F32) if space is HBM else vec(*shape) for space, shape in outs],
        in_specs=[pl.BlockSpec(memory_space=space) for space, _ in args],
        out_specs=[pl.BlockSpec(memory_space=space) for space, _ in outs],
        scratch_shapes=scratch,
        input_output_aliases=aliases,
        compiler_params=pltpu.CompilerParams(vmem_limit_bytes=mib * 1024 * 1024),
    )(*values)


def buf(*shape, dtype=F32):
    return pltpu.VMEM(shape, dtype)


def shift(value, axis, step):
    peers = lax.axis_size(axis)
    pairs = [(i, i + step) for i in range(peers) if 0 <= i + step < peers]
    return lax.ppermute(value, axis, pairs)


def rotate(values):
    moved = [lax.ppermute(v, "depth", [(i, (i + k) % DEPTHS) for i in range(DEPTHS)]) for k, v in enumerate(values) if k]
    return [values[0]] + moved


def shards(pressure, zone_labels, perm_table, asig_table, well_cells, rate_levels, green_spectrum, seis_state):
    tab = {name: jnp.asarray(value) for name, value in tables().items()}
    depth, slab = lax.axis_index("depth"), lax.axis_index("slab")
    me = (SMEM, depth.reshape(1))
    rows, block = (2, 8, N), (2, ROWS, N)

    table = pltpu.SMEM((perm_table.shape[0],), F32)
    first, last = call(
        edge_kernel,
        4,
        ((HBM, perm_table), (HBM, pressure), (HBM, zone_labels)),
        [(VMEM, (2,) + rows)] * 2,
        [table, buf(2, *rows, dtype=jnp.int32), DMA((5,))],
    )
    before, after = shift(last, "slab", 1), shift(first, "slab", -1)
    root, p_copy, msg = call(
        lookup_kernel,
        8,
        ((HBM, perm_table), (HBM, zone_labels), (HBM, pressure)),
        [(VMEM, block)] * 2 + [(HBM, (DEPTHS, 6, 8, N))],
        [table, buf(*block, dtype=jnp.int32), DMA((9,)), DMA((3, 8))],
    )
    (inv,) = call(
        strength_kernel,
        8,
        ((HBM, asig_table), (HBM, zone_labels)),
        [(HBM, block)],
        [table, buf(*block, dtype=jnp.int32), buf(*block), DMA((9,)), DMA((8,))],
    )

    layer, offset = well_cells[:, 0], well_cells[:, 1] - (slab * ROWS + depth * 8)
    own = (offset >= 0) & (offset < 8)
    near = (offset >= -2) & (offset < 10)
    inner = jnp.where(own, layer % 2 * 8 + offset, 16 + (offset + layer % 2 * 4) % 8)
    spot1 = jnp.where(near, layer // 2 * 24 + inner, -1)[None, :]
    spot2 = jnp.where(own, layer * 8 + offset, -1)[None, :]
    amounts = rate_unit * rate_levels.astype(F32)
    src1, src2 = call(
        wells_kernel,
        12,
        ((VMEM, spot1), (VMEM, spot2), (VMEM, amounts), (VMEM, well_cells[:, 2:3])),
        [(HBM, (192, N)), (HBM, (128, N))],
        [buf(320, N), DMA((2,))],
    )

    green = (green_spectrum * (1.0 / (N * N))).reshape(8, 8, SLABS, FREQS, TILES)
    green = green.transpose(1, 2, 3, 4, 0).reshape(8, STEP, LANES)

    (msg,) = call(
        pack_kernel,
        8,
        ((VMEM, p_copy), (VMEM, root), (VMEM, before), (VMEM, after), (HBM, msg)),
        [(HBM, (DEPTHS, 6, 8, N))],
        [buf(DEPTHS, *rows), DMA((2, 8))],
        {4: 0},
    )
    msg = lax.all_to_all(msg, "depth", 0, 0, tiled=True)
    *parts, spec = call(
        diffuse_kernel,
        24,
        (me, (VMEM, msg), (HBM, src1.reshape(DEPTHS, 3, 8, N)), (HBM, src2.reshape(DEPTHS, 2, 8, N)), (HBM, tab["fwd"]),
         (VMEM, tab["row_twist"])),
        [(HBM, rows)] * DEPTHS + [(HBM, (SLABS, DEPTHS, 8, LANES))],
        [buf(DEPTHS + 2, 3, 8, N), buf(DEPTHS, *rows), buf(DEPTHS, *rows), buf(1024, 256), buf(DEPTHS, *rows),
         buf(SLABS, DEPTHS, 8, LANES), buf(DEPTHS, 3, 8, N), buf(DEPTHS, *rows), buf(256, 768, dtype=BF16), DMA((4, 8))],
    )
    spec = lax.all_to_all(spec.reshape(SLABS * DEPTHS, 8, LANES), ("slab", "depth"), 0, 0, tiled=True)
    parts = rotate(parts)
    (spec,) = call(
        middle_kernel,
        16,
        ((VMEM, spec.reshape(SLABS, DEPTHS, 8, LANES)), (VMEM, green), (HBM, tab["mid"]), (HBM, tab["mid_inv"]),
         (HBM, tab["inner"]), (HBM, tab["inner_inv"]), (HBM, tab["col_twist"]), (VMEM, tab["in_twist"])),
        [(HBM, (256, 1024))],
        [buf(2, DEPTHS, STEP, LANES), buf(256, 1024), buf(256, 768, dtype=BF16), buf(256, 768, dtype=BF16),
         buf(768, 256, dtype=BF16), buf(768, 256, dtype=BF16), buf(2, 8, STEP, LANES), DMA((12,))],
    )
    spec = lax.all_to_all(spec.reshape(SLABS, 8, 1024), "slab", 0, 0, tiled=True).reshape(256, 1024)
    layer_pos = (depth * 2 + jnp.arange(2, dtype=jnp.int32)).astype(F32)
    weights = (1.0 + 2.0 * layer_pos / (2 * DEPTHS - 1)) / (4.0 * DEPTHS)
    press, state, rate = call(
        last_kernel,
        18,
        (me, (SMEM, weights), (VMEM, spec), (HBM, inv), (HBM, seis_state), (HBM, tab["inv"]), (VMEM, tab["row_twist"]),
         *[(ANY, v) for v in parts]),
        [(HBM, block)] * 2 + [(HBM, (DEPTHS, ROWS, 2 * LANES))],
        [buf(*block), buf(*block), buf(*block), buf(768, 256, dtype=BF16), buf(8, *rows),
         buf(DEPTHS, ROWS, 2 * LANES), buf(1024, 256), DMA((5, 8))],
    )
    rate = lax.all_to_all(rate, "depth", 0, 0, tiled=True)
    (rate_map,) = call(sum_kernel, 4, [(VMEM, rate)], [(VMEM, (ROWS, 2 * LANES))])
    return (press, state, rate_map)


def solution(mesh):
    in_specs = (
        P("depth", "slab", None),
        P("depth", "slab", None),
        P(),
        P(),
        P(),
        P(),
        P(None, "slab"),
        P("depth", "slab", None),
    )
    out_specs = (P("depth", "slab", None), P("depth", "slab", None), P("slab", "depth"))
    return jax.shard_map(shards, mesh=mesh, in_specs=in_specs, out_specs=out_specs, check_vma=False)
```

```python
import functools
import math

import jax
import jax.numpy as jnp
import ml_dtypes
import numpy as np
from jax import lax
from jax.experimental import pallas as pl
from jax.experimental.pallas import tpu as pltpu
from jax.sharding import PartitionSpec as P

conduct = 0.15
rate_unit = 0.5
friction = 0.6
recovery = 0.6065306597126334

LANES = 128
SLABS = 32
DEPTHS = 8
N = 2048
ROWS = N // SLABS
TILES = N // LANES
HALF = N // 2
HALVES = TILES // 2
FREQS = LANES // SLABS
STEP = SLABS * FREQS
F32 = jnp.float32
BF16 = jnp.bfloat16


def blocks(theta):
    cos, sin = np.cos(theta), np.sin(theta)
    return np.stack([np.stack([cos, -sin]), np.stack([sin, cos])])


def halves(table):
    high = table.astype(ml_dtypes.bfloat16)
    low = (table - high.astype(np.float64)).astype(ml_dtypes.bfloat16)
    return high, low


def left_table(table):
    high, low = halves(table)
    return np.concatenate([high, high, low], 1)


def right_table(table):
    high, low = halves(table)
    return np.concatenate([high, high, low], 0)


@functools.lru_cache(maxsize=None)
def tables():
    two_pi = 2.0 * np.pi
    k2, n2 = np.arange(128)[:, None], np.arange(128)[None, :]
    fwd = blocks(-two_pi * ((k2 * n2) % 128) / 128)
    fwd = fwd.reshape(2, 2, SLABS, FREQS, 128).transpose(2, 0, 3, 1, 4).reshape(256, 256)
    inv = blocks(two_pi * ((k2 * n2) % 128) / 128)
    inv = inv.reshape(2, 2, 128, SLABS, FREQS).transpose(3, 1, 4, 0, 2).reshape(256, 256)
    i, k = np.arange(SLABS)[:, None], np.arange(SLABS)[None, :]
    eye = np.eye(FREQS)
    angle = two_pi * ((i * k) % SLABS) / SLABS
    mid = np.einsum("absk,ij->akisbj", blocks(-angle), eye).reshape(256, 256)
    mid_inv = np.einsum("absk,ij->saibkj", blocks(angle), eye).reshape(256, 256)
    r, q = np.arange(8)[:, None], np.arange(8)[None, :]
    many = np.eye(TILES)
    angle = two_pi * ((r * q) % 8) / 8
    inner = np.einsum("abrq,ij->bjraiq", blocks(-angle), many).reshape(256, 256)
    inner_inv = np.einsum("abrq,ij->bjqair", blocks(angle), many).reshape(256, 256)
    row_angle = -two_pi * ((np.arange(TILES)[:, None] * np.arange(128)[None, :]) % N) / N
    row_twist = np.stack([np.cos(row_angle), np.sin(row_angle)]).astype(np.float32)
    row = (8 * np.arange(8)[:, None] + np.arange(8)[None, :])[:, None, :]
    col_angle = -two_pi * ((row * np.arange(SLABS)[None, :, None]) % N) / N
    col_angle = np.tile(np.repeat(col_angle, FREQS, 1), (1, 1, TILES))
    col_twist = np.stack([np.cos(col_angle), np.sin(col_angle)]).astype(np.float32)
    in_angle = np.tile(-two_pi * ((r * q) % 64) / 64, (1, TILES))
    in_twist = np.stack([np.cos(in_angle), np.sin(in_angle)]).astype(np.float32)
    return {
        "fwd": left_table(fwd),
        "inv": right_table(inv),
        "mid": left_table(mid),
        "mid_inv": left_table(mid_inv),
        "inner": right_table(inner),
        "inner_inv": right_table(inner_inv),
        "row_twist": row_twist,
        "col_twist": col_twist,
        "in_twist": in_twist,
    }


def triple(value, axis):
    high = value.astype(BF16)
    low = (value - high.astype(F32)).astype(BF16)
    return jnp.concatenate([high, low, high], axis)


def matmul(left, right):
    return jnp.dot(left, right, preferred_element_type=F32)


def radix4(items, sign):
    (ar, ai), (br, bi), (cr, ci), (dr, di) = items
    pr, pi, mr, mi = ar + cr, ai + ci, ar - cr, ai - ci
    qr, qi, nr, ni = br + dr, bi + di, br - dr, bi - di
    tr, ti = (-ni, nr) if sign > 0 else (ni, -nr)
    return [(pr + qr, pi + qi), (mr + tr, mi + ti), (pr - qr, pi - qi), (mr - tr, mi - ti)]


def scale_by(item, angle):
    c, s = math.cos(angle), math.sin(angle)
    re, im = item
    if abs(s) < 1e-12:
        return (re, im) if c > 0 else (-re, -im)
    if abs(c) < 1e-12:
        return (-im, re) if s > 0 else (im, -re)
    return (re * c - im * s, re * s + im * c)


def dft16(items, sign):
    mids = [radix4([items[4 * b + a] for b in range(4)], sign) for a in range(4)]
    out = [None] * 16
    for k in range(4):
        column = [scale_by(mids[a][k], sign * 2.0 * math.pi * a * k / 16) for a in range(4)]
        for m, item in enumerate(radix4(column, sign)):
            out[k + 4 * m] = item
    return out


def pick(label, table, bit, base):
    if bit < 0:
        return table[base]
    mask = (label & (1 << bit)) != 0
    return jnp.where(mask, pick(label, table, bit - 1, base + (1 << bit)), pick(label, table, bit - 1, base))


def start(src, dst, sem):
    copy = pltpu.make_async_copy(src, dst, sem)
    copy.start()
    return copy


def rows_of(d):
    return pl.ds(pl.multiple_of(d * 8, 8), 8)


def edge_kernel(perm_hbm, p_hbm, label_hbm, first_out, last_out, perm_ref, label, sems):
    table = start(perm_hbm, perm_ref, sems.at[4])
    first, last = slice(0, 8), slice(ROWS - 8, ROWS)
    loads = [
        start(label_hbm.at[:, first, :], label.at[0], sems.at[0]),
        start(label_hbm.at[:, last, :], label.at[1], sems.at[1]),
        start(p_hbm.at[:, first, :], first_out.at[0], sems.at[2]),
        start(p_hbm.at[:, last, :], last_out.at[0], sems.at[3]),
    ]
    table.wait()
    for copy in loads:
        copy.wait()
    width = 1024

    def body(c, carry):
        cols = pl.ds(pl.multiple_of(c * width, width), width)
        for l in range(2):
            first_out[1, l, :, cols] = jnp.sqrt(pick(label[0, l, :, cols], perm_ref, 3, 0))
            last_out[1, l, :, cols] = jnp.sqrt(pick(label[1, l, :, cols], perm_ref, 3, 0))
        return carry

    lax.fori_loop(0, N // width, body, 0)


def each_part(label_hbm, label, sems, work, done):
    loads = [start(label_hbm.at[:, rows_of(d), :], label.at[:, rows_of(d), :], sems.at[d]) for d in range(DEPTHS)]
    width = 1024
    for d in range(DEPTHS):
        loads[d].wait()

        def body(c, carry, d=d):
            cols = pl.ds(pl.multiple_of(c * width, width), width)
            for l in range(2):
                work(label[l, rows_of(d), cols], (l, rows_of(d), cols))
            return carry

        lax.fori_loop(0, N // width, body, 0)
        done(d)


def lookup_kernel(perm_hbm, label_hbm, p_hbm, root_out, p_out, msg_hbm, perm_ref, label, sems, msg_sems):
    table = start(perm_hbm, perm_ref, sems.at[8])
    loads = [start(p_hbm.at[:, rows_of(d), :], p_out.at[:, rows_of(d), :], msg_sems.at[4, d]) for d in range(DEPTHS)]
    copies = []

    def work(zone, at):
        root_out[at] = jnp.sqrt(pick(zone, perm_ref, 3, 0))

    def done(d):
        loads[d].wait()
        for h in range(2):
            at = slice(h * HALF, (h + 1) * HALF)
            copies.append(start(p_out.at[:, rows_of(d), at], msg_hbm.at[d, h * 2 : h * 2 + 2], msg_sems.at[h, d]))
            copies.append(start(root_out.at[:, rows_of(d), at], msg_hbm.at[d, h * 2 + 4 : h * 2 + 6], msg_sems.at[2 + h, d]))

    table.wait()
    each_part(label_hbm, label, sems, work, done)
    for copy in copies:
        copy.wait()


def strength_kernel(asig_hbm, label_hbm, inv_hbm, asig_ref, label, inv, sems, inv_sems):
    start(asig_hbm, asig_ref, sems.at[8]).wait()
    copies = []

    def work(zone, at):
        inv[at] = 1.0 / pick(zone, asig_ref, 3, 0)

    def done(d):
        copies.append(start(inv.at[:, rows_of(d), :], inv_hbm.at[:, rows_of(d), :], inv_sems.at[d]))

    each_part(label_hbm, label, sems, work, done)
    for copy in copies:
        copy.wait()


def wells_kernel(where1_ref, where2_ref, amount_ref, col_ref, out1_ref, out2_ref, both, sems):
    def hits(where_ref, rows, s):
        row = lax.broadcasted_iota(jnp.int32, (rows, 512), 0)
        return jnp.where(row == where_ref[...], amount_ref[s : s + 1, :], 0.0).astype(BF16)

    left = jnp.concatenate([hits(where1_ref, 192, 0), hits(where2_ref, 128, 1)], 0)
    col_of = jnp.broadcast_to(col_ref[...], (512, 256))
    for c in range(N // 256):
        at = slice(c * 256, (c + 1) * 256)
        col = lax.broadcasted_iota(jnp.int32, (512, 256), 1) + c * 256
        both[:, at] = matmul(left, jnp.where(col == col_of, 1.0, 0.0).astype(BF16))
    copies = [start(both.at[0:192, :], out1_ref, sems.at[0]), start(both.at[192:320, :], out2_ref, sems.at[1])]
    for copy in copies:
        copy.wait()


def pack_kernel(p_ref, q_ref, before_ref, after_ref, msg_hbm, out_hbm, side_ref, sems):
    row = lax.broadcasted_iota(jnp.int32, (8, N), 0)
    half_row = lax.broadcasted_iota(jnp.int32, (8, HALF), 0) % 4
    copies = []
    for d in range(DEPTHS):
        both = []
        for v, ref in enumerate((p_ref, q_ref)):
            sides = []
            for l in range(2):
                prev = ref[l, d * 8 - 8 : d * 8, :] if d else before_ref[v, l]
                then = ref[l, d * 8 + 8 : d * 8 + 16, :] if d < DEPTHS - 1 else after_ref[v, l]
                sides.append(jnp.where(row < 4, then, prev))
            both.append(jnp.where((row < 2) | (row >= 6), sides[0], pltpu.roll(sides[1], 4, 0)))
        out_p, out_q = [jnp.where((row == 0) | (row == 4), pltpu.roll(x, 7, 0), pltpu.roll(x, 1, 0)) for x in both]
        both.append(out_q * (out_p - both[0]))
        for v, x in enumerate(both):
            side_ref[d, v] = jnp.where(
                (half_row == 0) | (half_row == 3), x[:, :HALF], pltpu.roll(x[:, HALF:], 2, 0)
            )
        copies.append(start(side_ref.at[d], out_hbm.at[d, 8:11], sems.at[d]))
    for copy in copies:
        copy.wait()


class Tiles:
    def __init__(self, load):
        self.load, self.kept, self.turned = load, {}, {}

    def __getitem__(self, c):
        if c not in self.kept:
            self.kept[c] = self.load(c)
        return self.kept[c]

    def roll(self, c, by):
        if (c, by) not in self.turned:
            self.turned[c, by] = pltpu.roll(self[c], by, 1)
        return self.turned[c, by]

    def beside(self, c, lane):
        left = self.roll(c - 1, 1) if c else 0.0
        right = self.roll(c + 1, 127) if c < TILES - 1 else 0.0
        return jnp.where(lane == 0, left, self.roll(c, 1)) + jnp.where(lane == 127, right, self.roll(c, 127))


def of_rows(main0, main1, side, row):
    first, last = row == 0, row == 7
    up0 = jnp.where(first, pltpu.roll(side, 1, 0), pltpu.roll(main0, 1, 0))
    down0 = jnp.where(last, pltpu.roll(side, 7, 0), pltpu.roll(main0, 7, 0))
    up1 = jnp.where(first, pltpu.roll(side, 5, 0), pltpu.roll(main1, 1, 0))
    down1 = jnp.where(last, pltpu.roll(side, 3, 0), pltpu.roll(main1, 7, 0))
    return up0 + down0, up1 + down1


def of_side_rows(main0, main1, row):
    of0 = jnp.where(row == 0, pltpu.roll(main0, 1, 0), pltpu.roll(main0, 7, 0))
    of1 = jnp.where(row == 4, pltpu.roll(main1, 5, 0), pltpu.roll(main1, 3, 0))
    return jnp.where((row == 0) | (row == 7), of0, of1)


def tile(c):
    return slice(c * LANES, (c + 1) * LANES)


def diffuse_kernel(me_ref, msg_ref, src1_hbm, src2_hbm, fwd_hbm, twist_ref, *rest):
    outs, spec_hbm = rest[:8], rest[8]
    w_ref, p_ref, s_ref, mid_ref, new_ref, spec_out, src1_ref, src2_ref, fwd_ref, sems = rest[9:]
    me = me_ref[0]
    for d in range(DEPTHS):
        start(src1_hbm.at[d], src1_ref.at[d], sems.at[3, d])
    src2_load = start(src2_hbm, src2_ref, sems.at[0, 1])
    fwd_load = start(fwd_hbm, fwd_ref, sems.at[0, 2])
    w_ref[0] = jnp.zeros((3, 8, N), F32)
    w_ref[DEPTHS + 1] = jnp.zeros((3, 8, N), F32)
    row = lax.broadcasted_iota(jnp.int32, (8, LANES), 0)
    lane = lax.broadcasted_iota(jnp.int32, (8, LANES), 1)
    of_second = (row >= 2) & (row < 6)

    def main(d, v, l, c):
        return msg_ref[d, v * 4 + c // HALVES * 2 + l, :, tile(c % HALVES)]

    def side(d, v, c):
        found = msg_ref[d, 8 + v, :, tile(c % HALVES)]
        return found if c < HALVES else pltpu.roll(found, 6, 0)

    def first(d, carry):
        below, above = jnp.maximum(d - 1, 0), jnp.minimum(d + 1, DEPTHS - 1)
        has_below, has_above = (d > 0).astype(F32), (d < DEPTHS - 1).astype(F32)
        pltpu.make_async_copy(src1_hbm.at[d], src1_ref.at[d], sems.at[3, d]).wait()

        def three(v):
            return [Tiles(lambda c, l=l: main(d, v, l, c)) for l in range(2)] + [Tiles(lambda c: side(d, v, c))]

        p, q = three(0), three(1)
        u = [Tiles(lambda c, i=i: q[i][c] * p[i][c]) for i in range(3)]
        for c in range(TILES):
            at = tile(c)
            q_below = [main(below, 1, 1, c) * has_below, side(below, 1, c) * has_below]
            q_above = [main(above, 1, 0, c) * has_above, side(above, 1, c) * has_above]
            u_below = [q_below[0] * main(below, 0, 1, c), q_below[1] * side(below, 0, c)]
            u_above = [q_above[0] * main(above, 0, 0, c), q_above[1] * side(above, 0, c)]
            sums = []
            for own, low, high in ((q, q_below, q_above), (u, u_below, u_above)):
                x0, x1, x2 = own[0][c], own[1][c], own[2][c]
                sum0, sum1 = of_rows(x0, x1, x2, row)
                depth = pltpu.roll(x2 + jnp.where(of_second, low[1], high[1]), 4, 0)
                sums.append((
                    sum0 + own[0].beside(c, lane) + (low[0] + x1),
                    sum1 + own[1].beside(c, lane) + (x0 + high[0]),
                    of_side_rows(x0, x1, row) + own[2].beside(c, lane) + depth,
                ))
            for i in range(3):
                s, t = sums[0][i], sums[1][i]
                gain = t - p[i][c] * s
                if i == 2:
                    gain = gain + side(d, 2, c)
                new = p[i][c] + (conduct * q[i][c]) * gain + src1_ref[d, i, :, at]
                w_ref[d + 1, i, :, at] = q[i][c] * new
                if i < 2:
                    s_ref[d, i, :, at] = s
                    p_ref[d, i, :, at] = new
        return carry

    lax.fori_loop(0, DEPTHS, first, 0)
    src2_load.wait()

    def second(n, carry):
        k = lax.rem(n + 1, DEPTHS)
        d = lax.rem(me + k, DEPTHS)
        w = [Tiles(lambda c, i=i: w_ref[d + 1, i, :, tile(c)]) for i in range(3)]
        for c in range(TILES):
            at = tile(c)
            x0, x1 = w[0][c], w[1][c]
            sum0, sum1 = of_rows(x0, x1, w[2][c], row)
            t0 = sum0 + w[0].beside(c, lane) + (w_ref[d, 1, :, at] + x1)
            t1 = sum1 + w[1].beside(c, lane) + (x0 + w_ref[d + 2, 0, :, at])
            for l, t in ((0, t0), (1, t1)):
                p = p_ref[d, l, :, at]
                new_ref[k, l, :, at] = (
                    p + (conduct * main(d, 1, l, c)) * (t - p * s_ref[d, l, :, at]) + src2_ref[d, l, :, at]
                )
        spectrum_of_rows(new_ref.at[k], twist_ref, mid_ref, d)
        return carry

    lax.fori_loop(0, DEPTHS, second, 0)
    copies = [start(new_ref.at[k], outs[k], sems.at[1, k]) for k in range(DEPTHS)]
    fwd_load.wait()
    for c in range(4):
        part = triple(mid_ref[c * 256 : (c + 1) * 256, :], 1)
        block = lax.dot_general(fwd_ref[...], part, (((1,), (1,)), ((), ())), preferred_element_type=F32)
        for h in range(2):
            at = c * 2 + h
            spec_out[:, at] = block[:, h * 128 : (h + 1) * 128].reshape(SLABS, 8, 128)
            copies.append(start(spec_out.at[:, at], spec_hbm.at[:, at], sems.at[2, at]))
    for copy in copies:
        copy.wait()


def spectrum_of_rows(p_ref, twist_ref, mid_ref, d):
    items = [(p_ref[0, :, n * 128 : (n + 1) * 128], p_ref[1, :, n * 128 : (n + 1) * 128]) for n in range(TILES)]
    for k, (re, im) in enumerate(dft16(items, -1)):
        if k:
            cos, sin = twist_ref[0, k : k + 1, :], twist_ref[1, k : k + 1, :]
            re, im = re * cos - im * sin, re * sin + im * cos
        at = pl.ds(pl.multiple_of(d * 128 + k * 8, 8), 8)
        mid_ref[at, 0:128] = re
        mid_ref[at, 128:256] = im


def dft8(items, sign):
    even, odd = radix4(items[0::2], sign), radix4(items[1::2], sign)
    odd = [scale_by(item, sign * 2.0 * math.pi * k / 8) for k, item in enumerate(odd)]
    plus = [(a[0] + b[0], a[1] + b[1]) for a, b in zip(even, odd)]
    minus = [(a[0] - b[0], a[1] - b[1]) for a, b in zip(even, odd)]
    return plus + minus


def turn(item, cos, sin, sign):
    re, im = item
    if sign < 0:
        return re * cos - im * sin, re * sin + im * cos
    return re * cos + im * sin, im * cos - re * sin


def across(ref, sign, col_ref, in_ref):
    def body(i, carry):
        at = pl.ds(pl.multiple_of(i * 8, 8), 8)

        def by_block(items):
            return [turn(item, col_ref[0, d, at, :], col_ref[1, d, at, :], sign) for d, item in enumerate(items)]

        def by_digit(items):
            return [turn(item, in_ref[0, d : d + 1, :], in_ref[1, d : d + 1, :], sign) for d, item in enumerate(items)]

        items = [(ref[0, d, at, :], ref[1, d, at, :]) for d in range(DEPTHS)]
        items = by_block(items) if sign < 0 else by_digit(items)
        items = dft8(items, sign)
        items = by_digit(items) if sign < 0 else by_block(items)
        for d, (re, im) in enumerate(items):
            ref[0, d, at, :] = re
            ref[1, d, at, :] = im
        return carry

    lax.fori_loop(0, STEP // 8, body, 0)


def middle_kernel(
    spec_ref, green_ref, mid_hbm, mid_inv_hbm, inner_hbm, inner_inv_hbm, col_hbm, in_ref, out_hbm,
    work, out_ref, mid_ref, mid_inv_ref, inner_ref, inner_inv_ref, col_ref, sems,
):
    pairs = (
        (mid_hbm, mid_ref), (col_hbm, col_ref), (inner_hbm, inner_ref), (inner_inv_hbm, inner_inv_ref),
        (mid_inv_hbm, mid_inv_ref),
    )
    loads = [start(src, dst, sems.at[i]) for i, (src, dst) in enumerate(pairs)]
    loads[0].wait()
    for d in range(0, DEPTHS, 2):
        part = jnp.concatenate([spec_ref[:, d + h].reshape(256, 128) for h in range(2)], 1)
        spread = matmul(mid_ref[...], triple(part, 0))
        for h in range(2):
            work[0, d + h] = spread[0:128, h * 128 : (h + 1) * 128]
            work[1, d + h] = spread[128:256, h * 128 : (h + 1) * 128]
    for copy in loads[1:]:
        copy.wait()
    across(work, -1, col_ref, in_ref)
    for k in range(0, DEPTHS, 2):
        part = [jnp.concatenate([work[0, k + h], work[1, k + h]], 1) for h in range(2)]
        freq = matmul(triple(jnp.concatenate(part, 0), 1), inner_ref[...])
        green = jnp.concatenate([green_ref[k], green_ref[k + 1]], 0)
        freq = freq * jnp.concatenate([green, green], 1)
        back = matmul(triple(freq, 1), inner_inv_ref[...])
        for h in range(2):
            work[0, k + h] = back[h * 128 : (h + 1) * 128, 0:128]
            work[1, k + h] = back[h * 128 : (h + 1) * 128, 128:256]
    across(work, 1, col_ref, in_ref)
    copies = []
    for d in range(0, DEPTHS, 2):
        part = [jnp.concatenate([work[0, d + h], work[1, d + h]], 0) for h in range(2)]
        at = slice(d * 128, (d + 2) * 128)
        out_ref[:, at] = matmul(mid_inv_ref[...], triple(jnp.concatenate(part, 1), 0))
        copies.append(start(out_ref.at[:, at], out_hbm.at[:, at], sems.at[5 + d]))
    for copy in copies:
        copy.wait()


def last_kernel(me_ref, weight_ref, spec_ref, inv_hbm, seis_hbm, table_hbm, twist_ref, *rest):
    parts, rest = rest[:DEPTHS], rest[DEPTHS:]
    p_out, state_out, rate_out, rest = rest[0], rest[1], rest[2], rest[3:]
    p_ref, inv_ref, seis_ref, table_ref, state_ref, rate_ref, mid_ref, sems = rest
    me = me_ref[0]
    table_load = start(table_hbm, table_ref, sems.at[4, 0])
    loads = [start(inv_hbm, inv_ref, sems.at[4, 1]), start(seis_hbm, seis_ref, sems.at[4, 2])]
    copies = []
    for k in range(DEPTHS):
        d = lax.rem(me + (DEPTHS - k), DEPTHS)
        loads.append(start(parts[k], p_ref.at[:, rows_of(d), :], sems.at[0, k]))
    table_load.wait()
    for c in range(4):
        turned = jnp.transpose(spec_ref[:, c * 256 : (c + 1) * 256])
        mid_ref[c * 256 : (c + 1) * 256, :] = matmul(triple(turned, 1), table_ref[...])
    for copy in loads:
        copy.wait()
    copies.append(start(p_ref, p_out, sems.at[1, 0]))

    def body(i, carry):
        rows = rows_of(i)
        items = []
        for k in range(TILES):
            at = pl.ds(pl.multiple_of(i * 128 + k * 8, 8), 8)
            item = (mid_ref[at, 0:128], mid_ref[at, 128:256])
            if k:
                item = turn(item, twist_ref[0, k : k + 1, :], twist_ref[1, k : k + 1, :], 1)
            items.append(item)
        for n, stress in enumerate(dft16(items, 1)):
            at = slice(n * 128, (n + 1) * 128)
            total = None
            for l in range(2):
                coulomb = stress[l] + friction * p_ref[l, rows, at]
                grown = seis_ref[l, rows, at] * jnp.exp(-coulomb * inv_ref[l, rows, at])
                state = 1.0 + (grown - 1.0) * recovery
                state_ref[i, l, :, at] = state
                term = weight_ref[l] / state
                total = term if total is None else total + term
            rate_ref[n // 2, rows, (n % 2) * 128 : (n % 2) * 128 + 128] = total
        pltpu.make_async_copy(state_ref.at[i], state_out.at[:, rows, :], sems.at[2, i]).start()
        return carry

    lax.fori_loop(0, DEPTHS, body, 0)
    copies.append(start(rate_ref, rate_out, sems.at[3, 0]))
    for i in range(DEPTHS):
        pltpu.make_async_copy(state_ref.at[i], state_out.at[:, rows_of(i), :], sems.at[2, i]).wait()
    for copy in copies:
        copy.wait()


def sum_kernel(part_ref, out_ref):
    total = part_ref[0]
    for d in range(1, DEPTHS):
        total = total + part_ref[d]
    out_ref[...] = total


def vec(*shape):
    return jax.ShapeDtypeStruct(shape, F32)


SMEM, VMEM, ANY, HBM = pltpu.SMEM, pltpu.VMEM, pl.ANY, pltpu.HBM
DMA = pltpu.SemaphoreType.DMA


def call(kernel, mib, args, outs, scratch=(), aliases={}):
    values = [pltpu.with_memory_space_constraint(value, space) if space is HBM else value for space, value in args]
    return pl.pallas_call(
        kernel,
        out_shape=[HBM(shape, F32) if space is HBM else vec(*shape) for space, shape in outs],
        in_specs=[pl.BlockSpec(memory_space=space) for space, _ in args],
        out_specs=[pl.BlockSpec(memory_space=space) for space, _ in outs],
        scratch_shapes=scratch,
        input_output_aliases=aliases,
        compiler_params=pltpu.CompilerParams(vmem_limit_bytes=mib * 1024 * 1024),
    )(*values)


def buf(*shape, dtype=F32):
    return pltpu.VMEM(shape, dtype)


def shift(value, axis, step):
    peers = lax.axis_size(axis)
    pairs = [(i, i + step) for i in range(peers) if 0 <= i + step < peers]
    return lax.ppermute(value, axis, pairs)


def rotate(values):
    moved = [lax.ppermute(v, "depth", [(i, (i + k) % DEPTHS) for i in range(DEPTHS)]) for k, v in enumerate(values) if k]
    return [values[0]] + moved


def shards(pressure, zone_labels, perm_table, asig_table, well_cells, rate_levels, green_spectrum, seis_state):
    tab = {name: jnp.asarray(value) for name, value in tables().items()}
    depth, slab = lax.axis_index("depth"), lax.axis_index("slab")
    me = (SMEM, depth.reshape(1))
    rows, block = (2, 8, N), (2, ROWS, N)

    table = pltpu.SMEM((perm_table.shape[0],), F32)
    first, last = call(
        edge_kernel,
        4,
        ((HBM, perm_table), (HBM, pressure), (HBM, zone_labels)),
        [(VMEM, (2,) + rows)] * 2,
        [table, buf(2, *rows, dtype=jnp.int32), DMA((5,))],
    )
    before, after = shift(last, "slab", 1), shift(first, "slab", -1)
    root, p_copy, msg = call(
        lookup_kernel,
        8,
        ((HBM, perm_table), (HBM, zone_labels), (HBM, pressure)),
        [(VMEM, block)] * 2 + [(HBM, (DEPTHS, 11, 8, HALF))],
        [table, buf(*block, dtype=jnp.int32), DMA((9,)), DMA((5, 8))],
    )
    (inv,) = call(
        strength_kernel,
        8,
        ((HBM, asig_table), (HBM, zone_labels)),
        [(HBM, block)],
        [table, buf(*block, dtype=jnp.int32), buf(*block), DMA((9,)), DMA((8,))],
    )

    layer, offset = well_cells[:, 0], well_cells[:, 1] - (slab * ROWS + depth * 8)
    own = (offset >= 0) & (offset < 8)
    near = (offset >= -2) & (offset < 10)
    inner = jnp.where(own, layer % 2 * 8 + offset, 16 + (offset + layer % 2 * 4) % 8)
    spot1 = jnp.where(near, layer // 2 * 24 + inner, -1)[None, :]
    spot2 = jnp.where(own, layer * 8 + offset, -1)[None, :]
    amounts = rate_unit * rate_levels.astype(F32)
    src1, src2 = call(
        wells_kernel,
        12,
        ((VMEM, spot1), (VMEM, spot2), (VMEM, amounts), (VMEM, well_cells[:, 2:3])),
        [(HBM, (192, N)), (HBM, (128, N))],
        [buf(320, N), DMA((2,))],
    )

    green = (green_spectrum * (1.0 / (N * N))).reshape(8, 8, SLABS, FREQS, TILES)
    green = green.transpose(1, 2, 3, 4, 0).reshape(8, STEP, LANES)

    (msg,) = call(
        pack_kernel,
        8,
        ((VMEM, p_copy), (VMEM, root), (VMEM, before), (VMEM, after), (HBM, msg)),
        [(HBM, (DEPTHS, 11, 8, HALF))],
        [buf(DEPTHS, 3, 8, HALF), DMA((8,))],
        {4: 0},
    )
    msg = lax.all_to_all(msg, "depth", 0, 0, tiled=True)
    *parts, spec = call(
        diffuse_kernel,
        24,
        (me, (VMEM, msg), (HBM, src1.reshape(DEPTHS, 3, 8, N)), (HBM, src2.reshape(DEPTHS, 2, 8, N)), (HBM, tab["fwd"]),
         (VMEM, tab["row_twist"])),
        [(HBM, rows)] * DEPTHS + [(HBM, (SLABS, DEPTHS, 8, LANES))],
        [buf(DEPTHS + 2, 3, 8, N), buf(DEPTHS, *rows), buf(DEPTHS, *rows), buf(1024, 256), buf(DEPTHS, *rows),
         buf(SLABS, DEPTHS, 8, LANES), buf(DEPTHS, 3, 8, N), buf(DEPTHS, *rows), buf(256, 768, dtype=BF16), DMA((4, 8))],
    )
    spec = lax.all_to_all(spec.reshape(SLABS * DEPTHS, 8, LANES), ("slab", "depth"), 0, 0, tiled=True)
    parts = rotate(parts)
    (spec,) = call(
        middle_kernel,
        16,
        ((VMEM, spec.reshape(SLABS, DEPTHS, 8, LANES)), (VMEM, green), (HBM, tab["mid"]), (HBM, tab["mid_inv"]),
         (HBM, tab["inner"]), (HBM, tab["inner_inv"]), (HBM, tab["col_twist"]), (VMEM, tab["in_twist"])),
        [(HBM, (256, 1024))],
        [buf(2, DEPTHS, STEP, LANES), buf(256, 1024), buf(256, 768, dtype=BF16), buf(256, 768, dtype=BF16),
         buf(768, 256, dtype=BF16), buf(768, 256, dtype=BF16), buf(2, 8, STEP, LANES), DMA((12,))],
    )
    spec = lax.all_to_all(spec.reshape(SLABS, 8, 1024), "slab", 0, 0, tiled=True).reshape(256, 1024)
    layer_pos = (depth * 2 + jnp.arange(2, dtype=jnp.int32)).astype(F32)
    weights = (1.0 + 2.0 * layer_pos / (2 * DEPTHS - 1)) / (4.0 * DEPTHS)
    press, state, rate = call(
        last_kernel,
        18,
        (me, (SMEM, weights), (VMEM, spec), (HBM, inv), (HBM, seis_state), (HBM, tab["inv"]), (VMEM, tab["row_twist"]),
         *[(ANY, v) for v in parts]),
        [(HBM, block)] * 2 + [(HBM, (DEPTHS, ROWS, 2 * LANES))],
        [buf(*block), buf(*block), buf(*block), buf(768, 256, dtype=BF16), buf(8, *rows),
         buf(DEPTHS, ROWS, 2 * LANES), buf(1024, 256), DMA((5, 8))],
    )
    rate = lax.all_to_all(rate, "depth", 0, 0, tiled=True)
    (rate_map,) = call(sum_kernel, 4, [(VMEM, rate)], [(VMEM, (ROWS, 2 * LANES))])
    return (press, state, rate_map)


def solution(mesh):
    in_specs = (
        P("depth", "slab", None),
        P("depth", "slab", None),
        P(),
        P(),
        P(),
        P(),
        P(None, "slab"),
        P("depth", "slab", None),
    )
    out_specs = (P("depth", "slab", None), P("depth", "slab", None), P("slab", "depth"))
    return jax.shard_map(shards, mesh=mesh, in_specs=in_specs, out_specs=out_specs, check_vma=False)
```

```python
import functools
import math

import jax
import jax.numpy as jnp
import ml_dtypes
import numpy as np
from jax import lax
from jax.experimental import pallas as pl
from jax.experimental.pallas import tpu as pltpu
from jax.sharding import PartitionSpec as P

conduct = 0.15
rate_unit = 0.5
friction = 0.6
recovery = 0.6065306597126334

LANES = 128
SLABS = 32
DEPTHS = 8
N = 2048
ROWS = N // SLABS
TILES = N // LANES
HALF = N // 2
HALVES = TILES // 2
FREQS = LANES // SLABS
STEP = SLABS * FREQS
F32 = jnp.float32
BF16 = jnp.bfloat16


def blocks(theta):
    cos, sin = np.cos(theta), np.sin(theta)
    return np.stack([np.stack([cos, -sin]), np.stack([sin, cos])])


def halves(table):
    high = table.astype(ml_dtypes.bfloat16)
    low = (table - high.astype(np.float64)).astype(ml_dtypes.bfloat16)
    return high, low


def left_table(table):
    high, low = halves(table)
    return np.concatenate([high, high, low], 1)


def right_table(table):
    high, low = halves(table)
    return np.concatenate([high, high, low], 0)


@functools.lru_cache(maxsize=None)
def tables():
    two_pi = 2.0 * np.pi
    k2, n2 = np.arange(128)[:, None], np.arange(128)[None, :]
    fwd = blocks(-two_pi * ((k2 * n2) % 128) / 128)
    fwd = fwd.reshape(2, 2, SLABS, FREQS, 128).transpose(2, 0, 3, 1, 4).reshape(256, 256)
    inv = blocks(two_pi * ((k2 * n2) % 128) / 128)
    inv = inv.reshape(2, 2, 128, SLABS, FREQS).transpose(3, 1, 4, 0, 2).reshape(256, 256)
    i, k = np.arange(SLABS)[:, None], np.arange(SLABS)[None, :]
    eye = np.eye(FREQS)
    angle = two_pi * ((i * k) % SLABS) / SLABS
    mid = np.einsum("absk,ij->akisbj", blocks(-angle), eye).reshape(256, 256)
    mid_inv = np.einsum("absk,ij->saibkj", blocks(angle), eye).reshape(256, 256)
    r, q = np.arange(8)[:, None], np.arange(8)[None, :]
    many = np.eye(TILES)
    angle = two_pi * ((r * q) % 8) / 8
    inner = np.einsum("abrq,ij->bjraiq", blocks(-angle), many).reshape(256, 256)
    inner_inv = np.einsum("abrq,ij->bjqair", blocks(angle), many).reshape(256, 256)
    row_angle = -two_pi * ((np.arange(TILES)[:, None] * np.arange(128)[None, :]) % N) / N
    row_twist = np.stack([np.cos(row_angle), np.sin(row_angle)]).astype(np.float32)
    row = (8 * np.arange(8)[:, None] + np.arange(8)[None, :])[:, None, :]
    col_angle = -two_pi * ((row * np.arange(SLABS)[None, :, None]) % N) / N
    col_angle = np.tile(np.repeat(col_angle, FREQS, 1), (1, 1, TILES))
    col_twist = np.stack([np.cos(col_angle), np.sin(col_angle)]).astype(np.float32)
    in_angle = np.tile(-two_pi * ((r * q) % 64) / 64, (1, TILES))
    in_twist = np.stack([np.cos(in_angle), np.sin(in_angle)]).astype(np.float32)
    return {
        "fwd": left_table(fwd),
        "inv": right_table(inv),
        "mid": left_table(mid),
        "mid_inv": left_table(mid_inv),
        "inner": right_table(inner),
        "inner_inv": right_table(inner_inv),
        "row_twist": row_twist,
        "col_twist": col_twist,
        "in_twist": in_twist,
    }


def triple(value, axis):
    high = value.astype(BF16)
    low = (value - high.astype(F32)).astype(BF16)
    return jnp.concatenate([high, low, high], axis)


def matmul(left, right):
    return jnp.dot(left, right, preferred_element_type=F32)


def radix4(items, sign):
    (ar, ai), (br, bi), (cr, ci), (dr, di) = items
    pr, pi, mr, mi = ar + cr, ai + ci, ar - cr, ai - ci
    qr, qi, nr, ni = br + dr, bi + di, br - dr, bi - di
    tr, ti = (-ni, nr) if sign > 0 else (ni, -nr)
    return [(pr + qr, pi + qi), (mr + tr, mi + ti), (pr - qr, pi - qi), (mr - tr, mi - ti)]


def scale_by(item, angle):
    c, s = math.cos(angle), math.sin(angle)
    re, im = item
    if abs(s) < 1e-12:
        return (re, im) if c > 0 else (-re, -im)
    if abs(c) < 1e-12:
        return (-im, re) if s > 0 else (im, -re)
    return (re * c - im * s, re * s + im * c)


def dft16(items, sign):
    mids = [radix4([items[4 * b + a] for b in range(4)], sign) for a in range(4)]
    out = [None] * 16
    for k in range(4):
        column = [scale_by(mids[a][k], sign * 2.0 * math.pi * a * k / 16) for a in range(4)]
        for m, item in enumerate(radix4(column, sign)):
            out[k + 4 * m] = item
    return out


def table_tiles(table, change):
    lane = lax.broadcasted_iota(jnp.int32, (8, LANES), 1)
    values = [change(jnp.full((8, LANES), table[zone], F32)) for zone in range(16)]
    found = values[0]
    for zone in range(1, 16):
        found = jnp.where(lane == zone, values[zone], found)
    return values, found


def choose(bits, values):
    if len(values) == 1:
        return values[0]
    half = len(values) // 2
    return jnp.where(bits[-1], choose(bits[:-1], values[half:]), choose(bits[:-1], values[:half]))


def pick(label, tiles):
    values, found = tiles
    parts = []
    for c in range(label.shape[1] // LANES):
        zone = label[:, tile(c)]
        if c % 8 in (1, 4, 6):
            parts.append(jnp.take_along_axis(found, zone, axis=1))
        else:
            parts.append(choose([(zone & (1 << bit)) != 0 for bit in range(4)], values))
    return jnp.concatenate(parts, 1)


def start(src, dst, sem):
    copy = pltpu.make_async_copy(src, dst, sem)
    copy.start()
    return copy


def rows_of(d):
    return pl.ds(pl.multiple_of(d * 8, 8), 8)


def edge_kernel(perm_hbm, p_hbm, label_hbm, first_out, last_out, perm_ref, label, p_ref, sems):
    load = start(perm_hbm, perm_ref, sems.at[4])
    first, last = slice(0, 8), slice(ROWS - 8, ROWS)
    loads = [
        start(label_hbm.at[:, first, :], label.at[0], sems.at[0]),
        start(label_hbm.at[:, last, :], label.at[1], sems.at[1]),
        start(p_hbm.at[:, first, :], p_ref.at[0], sems.at[2]),
        start(p_hbm.at[:, last, :], p_ref.at[1], sems.at[3]),
    ]
    load.wait()
    table = table_tiles(perm_ref, jnp.sqrt)
    for copy in loads:
        copy.wait()
    pair = lax.broadcasted_iota(jnp.int32, (8, N), 0) // 2
    for i, (out, at) in enumerate(((first_out, 0), (last_out, 3))):
        values = [p_ref[i, 0], p_ref[i, 1], pick(label[i, 0], table), pick(label[i, 1], table)]
        packed = values[0]
        for n in range(1, 4):
            packed = jnp.where(pair == (at + n) % 4, pltpu.roll(values[n], 2 * n, 0), packed)
        out[...] = packed


def each_part(label_hbm, label, sems, work, done):
    parts = [pl.ds(g * 2, 2) for g in range(4)]
    loads = [start(label_hbm.at[:, at], label.at[:, at], sems.at[g]) for g, at in enumerate(parts)]
    width = 1024
    for g in range(4):
        loads[g].wait()

        def body(n, carry, g=g):
            d = g * 2 + n // 2
            cols = pl.ds(pl.multiple_of(n % 2 * width, width), width)
            for l in range(2):
                work(label[l, d, :, cols], d, l, cols)
            return carry

        lax.fori_loop(0, 4, body, 0)
        done(g)


def lookup_kernel(perm_hbm, label_hbm, p_hbm, root_out, p_out, msg_hbm, perm_ref, label, sems, msg_sems):
    table = start(perm_hbm, perm_ref, sems.at[8])
    loads = [start(p_hbm.at[l], p_out.at[:, l], msg_sems.at[2, l]) for l in range(2)]
    copies = []

    def work(zone, d, l, cols):
        root_out[d, l, :, cols] = pick(zone, values)

    def done(g):
        for h in range(2):
            at = slice(h * HALF, (h + 1) * HALF)
            if g == 0:
                loads[h].wait()
            if g == 1:
                copies.append(start(p_out.at[:, :, :, at], msg_hbm.at[:, h * 2 : h * 2 + 2], msg_sems.at[h, 7]))
            if g % 2:
                rows = pl.ds(g * 2 - 2, 4)
                copies.append(start(root_out.at[rows, :, :, at], msg_hbm.at[rows, h * 2 + 4 : h * 2 + 6], msg_sems.at[h, g]))

    table.wait()
    values = table_tiles(perm_ref, jnp.sqrt)
    each_part(label_hbm, label, sems, work, done)
    for copy in copies:
        copy.wait()


def strength_kernel(asig_hbm, label_hbm, inv_hbm, asig_ref, label, inv, sems):
    start(asig_hbm, asig_ref, sems.at[8]).wait()
    values = table_tiles(asig_ref, lambda x: 1.0 / x)

    def work(zone, d, l, cols):
        inv[l, rows_of(d), cols] = pick(zone, values)

    each_part(label_hbm, label, sems, work, lambda g: None)
    start(inv, inv_hbm, sems.at[8]).wait()


def wells_kernel(where1_ref, where2_ref, amount_ref, col_ref, out1_ref, out2_ref, both, sems):
    def hits(where_ref, rows, s):
        row = lax.broadcasted_iota(jnp.int32, (rows, 512), 0)
        return jnp.where(row == where_ref[...], amount_ref[s : s + 1, :], 0.0).astype(BF16)

    left = jnp.concatenate([hits(where1_ref, 192, 0), hits(where2_ref, 128, 1)], 0)
    col_of = jnp.broadcast_to(col_ref[...], (512, 256))
    for c in range(N // 256):
        at = slice(c * 256, (c + 1) * 256)
        col = lax.broadcasted_iota(jnp.int32, (512, 256), 1) + c * 256
        both[:, at] = matmul(left, jnp.where(col == col_of, 1.0, 0.0).astype(BF16))
    copies = [start(both.at[0:192, :], out1_ref, sems.at[0]), start(both.at[192:320, :], out2_ref, sems.at[1])]
    for copy in copies:
        copy.wait()


def pack_kernel(p_ref, q_ref, before_ref, after_ref, msg_hbm, out_hbm, side_ref, sems):
    row = lax.broadcasted_iota(jnp.int32, (8, N), 0)
    half_row = lax.broadcasted_iota(jnp.int32, (8, HALF), 0) % 4
    copies = []
    for d in range(DEPTHS):
        both = []
        for v, ref in enumerate((p_ref, q_ref)):
            sides = []
            for l in range(2):
                back = (8 - 2 * (2 * v + l)) % 8
                prev = ref[d - 1, l] if d else pltpu.roll(before_ref[...], back, 0)
                then = ref[d + 1, l] if d < DEPTHS - 1 else pltpu.roll(after_ref[...], back, 0)
                sides.append(jnp.where(row < 4, then, prev))
            both.append(jnp.where((row < 2) | (row >= 6), sides[0], pltpu.roll(sides[1], 4, 0)))
        out_p, out_q = [jnp.where((row == 0) | (row == 4), pltpu.roll(x, 7, 0), pltpu.roll(x, 1, 0)) for x in both]
        both.append(out_q * (out_p - both[0]))
        for v, x in enumerate(both):
            side_ref[d, v] = jnp.where(
                (half_row == 0) | (half_row == 3), x[:, :HALF], pltpu.roll(x[:, HALF:], 2, 0)
            )
        if d % 4 == 3:
            done = pl.ds(d - 3, 4)
            copies.append(start(side_ref.at[done], out_hbm.at[done, 8:11], sems.at[d]))
    for copy in copies:
        copy.wait()


class Tiles:
    def __init__(self, load):
        self.load, self.kept, self.turned = load, {}, {}

    def __getitem__(self, c):
        if c not in self.kept:
            self.kept[c] = self.load(c)
        return self.kept[c]

    def roll(self, c, by):
        if (c, by) not in self.turned:
            self.turned[c, by] = pltpu.roll(self[c], by, 1)
        return self.turned[c, by]

    def beside(self, c, lane):
        left = self.roll(c - 1, 1) if c else 0.0
        right = self.roll(c + 1, 127) if c < TILES - 1 else 0.0
        return jnp.where(lane == 0, left, self.roll(c, 1)) + jnp.where(lane == 127, right, self.roll(c, 127))


def of_rows(main0, main1, side, row):
    first, last = row == 0, row == 7
    up0 = jnp.where(first, pltpu.roll(side, 1, 0), pltpu.roll(main0, 1, 0))
    down0 = jnp.where(last, pltpu.roll(side, 7, 0), pltpu.roll(main0, 7, 0))
    up1 = jnp.where(first, pltpu.roll(side, 5, 0), pltpu.roll(main1, 1, 0))
    down1 = jnp.where(last, pltpu.roll(side, 3, 0), pltpu.roll(main1, 7, 0))
    return up0 + down0, up1 + down1


def of_side_rows(main0, main1, row):
    of0 = jnp.where(row == 0, pltpu.roll(main0, 1, 0), pltpu.roll(main0, 7, 0))
    of1 = jnp.where(row == 4, pltpu.roll(main1, 5, 0), pltpu.roll(main1, 3, 0))
    return jnp.where((row == 0) | (row == 7), of0, of1)


def tile(c):
    return slice(c * LANES, (c + 1) * LANES)


def diffuse_kernel(me_ref, msg_ref, src1_hbm, src2_hbm, fwd_hbm, twist_ref, *rest):
    outs, spec_hbm = rest[:8], rest[8]
    w_ref, p_ref, s_ref, mid_ref, new_ref, spec_out, src1_ref, src2_ref, fwd_ref, sems = rest[9:]
    me = me_ref[0]
    for d in range(DEPTHS):
        start(src1_hbm.at[d], src1_ref.at[d], sems.at[3, d])
    src2_load = start(src2_hbm, src2_ref, sems.at[0, 1])
    fwd_load = start(fwd_hbm, fwd_ref, sems.at[0, 2])
    w_ref[0] = jnp.zeros((3, 8, N), F32)
    w_ref[DEPTHS + 1] = jnp.zeros((3, 8, N), F32)
    row = lax.broadcasted_iota(jnp.int32, (8, LANES), 0)
    lane = lax.broadcasted_iota(jnp.int32, (8, LANES), 1)
    of_second = (row >= 2) & (row < 6)

    def main(d, v, l, c):
        return msg_ref[d, v * 4 + c // HALVES * 2 + l, :, tile(c % HALVES)]

    def side(d, v, c):
        found = msg_ref[d, 8 + v, :, tile(c % HALVES)]
        return found if c < HALVES else pltpu.roll(found, 6, 0)

    def first(d, carry):
        below, above = jnp.maximum(d - 1, 0), jnp.minimum(d + 1, DEPTHS - 1)
        has_below, has_above = (d > 0).astype(F32), (d < DEPTHS - 1).astype(F32)
        pltpu.make_async_copy(src1_hbm.at[d], src1_ref.at[d], sems.at[3, d]).wait()

        def three(v):
            return [Tiles(lambda c, l=l: main(d, v, l, c)) for l in range(2)] + [Tiles(lambda c: side(d, v, c))]

        p, q = three(0), three(1)
        u = [Tiles(lambda c, i=i: q[i][c] * p[i][c]) for i in range(3)]
        for c in range(TILES):
            at = tile(c)
            q_below = [main(below, 1, 1, c) * has_below, side(below, 1, c) * has_below]
            q_above = [main(above, 1, 0, c) * has_above, side(above, 1, c) * has_above]
            u_below = [q_below[0] * main(below, 0, 1, c), q_below[1] * side(below, 0, c)]
            u_above = [q_above[0] * main(above, 0, 0, c), q_above[1] * side(above, 0, c)]
            sums = []
            for own, low, high in ((q, q_below, q_above), (u, u_below, u_above)):
                x0, x1, x2 = own[0][c], own[1][c], own[2][c]
                sum0, sum1 = of_rows(x0, x1, x2, row)
                depth = pltpu.roll(x2 + jnp.where(of_second, low[1], high[1]), 4, 0)
                sums.append((
                    sum0 + own[0].beside(c, lane) + (low[0] + x1),
                    sum1 + own[1].beside(c, lane) + (x0 + high[0]),
                    of_side_rows(x0, x1, row) + own[2].beside(c, lane) + depth,
                ))
            for i in range(3):
                s, t = sums[0][i], sums[1][i]
                gain = t - p[i][c] * s
                if i == 2:
                    gain = gain + side(d, 2, c)
                new = p[i][c] + (conduct * q[i][c]) * gain + src1_ref[d, i, :, at]
                w_ref[d + 1, i, :, at] = q[i][c] * new
                if i < 2:
                    s_ref[d, i, :, at] = s
                    p_ref[d, i, :, at] = new
        return carry

    lax.fori_loop(0, DEPTHS, first, 0)
    src2_load.wait()

    def second(d):
        k = lax.rem(d + DEPTHS - me, DEPTHS)
        w = [Tiles(lambda c, i=i: w_ref[d + 1, i, :, tile(c)]) for i in range(3)]
        for c in range(TILES):
            at = tile(c)
            x0, x1 = w[0][c], w[1][c]
            sum0, sum1 = of_rows(x0, x1, w[2][c], row)
            t0 = sum0 + w[0].beside(c, lane) + (w_ref[d, 1, :, at] + x1)
            t1 = sum1 + w[1].beside(c, lane) + (x0 + w_ref[d + 2, 0, :, at])
            for l, t in ((0, t0), (1, t1)):
                p = p_ref[d, l, :, at]
                new_ref[k, l, :, at] = (
                    p + (conduct * main(d, 1, l, c)) * (t - p * s_ref[d, l, :, at]) + src2_ref[d, l, :, at]
                )
        spectrum_of_rows(new_ref.at[k], twist_ref, mid_ref, d)

    copies = []

    def transform(c):
        part = triple(mid_ref[c * 256 : (c + 1) * 256, :], 1)
        block = lax.dot_general(fwd_ref[...], part, (((1,), (1,)), ((), ())), preferred_element_type=F32)
        for h in range(2):
            at = c * 2 + h
            spec_out[:, at] = block[:, h * 128 : (h + 1) * 128].reshape(SLABS, 8, 128)
        at = pl.ds(c * 2, 2)
        copies.append(start(spec_out.at[:, at], spec_hbm.at[:, at], sems.at[2, c]))

    second(0)
    second(1)
    fwd_load.wait()
    for d in range(2, DEPTHS, 2):
        transform(d // 2 - 1)
        second(d)
        second(d + 1)
    transform(DEPTHS // 2 - 1)
    copies.extend(start(new_ref.at[k], outs[k], sems.at[1, k]) for k in range(DEPTHS))
    for copy in copies:
        copy.wait()


def spectrum_of_rows(p_ref, twist_ref, mid_ref, d):
    items = [(p_ref[0, :, n * 128 : (n + 1) * 128], p_ref[1, :, n * 128 : (n + 1) * 128]) for n in range(TILES)]
    for k, (re, im) in enumerate(dft16(items, -1)):
        if k:
            cos, sin = twist_ref[0, k : k + 1, :], twist_ref[1, k : k + 1, :]
            re, im = re * cos - im * sin, re * sin + im * cos
        at = slice(d * 128 + k * 8, d * 128 + k * 8 + 8)
        mid_ref[at, 0:128] = re
        mid_ref[at, 128:256] = im


def dft8(items, sign):
    even, odd = radix4(items[0::2], sign), radix4(items[1::2], sign)
    odd = [scale_by(item, sign * 2.0 * math.pi * k / 8) for k, item in enumerate(odd)]
    plus = [(a[0] + b[0], a[1] + b[1]) for a, b in zip(even, odd)]
    minus = [(a[0] - b[0], a[1] - b[1]) for a, b in zip(even, odd)]
    return plus + minus


def turn(item, cos, sin, sign):
    re, im = item
    if sign < 0:
        return re * cos - im * sin, re * sin + im * cos
    return re * cos + im * sin, im * cos - re * sin


def across(ref, sign, col_ref, in_ref):
    def body(i, carry):
        at = pl.ds(pl.multiple_of(i * 8, 8), 8)

        def by_block(items):
            return [turn(item, col_ref[0, d, at, :], col_ref[1, d, at, :], sign) for d, item in enumerate(items)]

        def by_digit(items):
            return [turn(item, in_ref[0, d : d + 1, :], in_ref[1, d : d + 1, :], sign) for d, item in enumerate(items)]

        items = [(ref[0, d, at, :], ref[1, d, at, :]) for d in range(DEPTHS)]
        items = by_block(items) if sign < 0 else by_digit(items)
        items = dft8(items, sign)
        items = by_digit(items) if sign < 0 else by_block(items)
        for d, (re, im) in enumerate(items):
            ref[0, d, at, :] = re
            ref[1, d, at, :] = im
        return carry

    lax.fori_loop(0, STEP // 8, body, 0)


def middle_kernel(
    spec_ref, green_ref, mid_hbm, mid_inv_hbm, inner_hbm, inner_inv_hbm, col_hbm, in_ref, out_hbm,
    work, out_ref, mid_ref, mid_inv_ref, inner_ref, inner_inv_ref, col_ref, split_ref, sems,
):
    pairs = (
        (mid_hbm, mid_ref), (col_hbm, col_ref), (inner_hbm, inner_ref), (inner_inv_hbm, inner_inv_ref),
        (mid_inv_hbm, mid_inv_ref),
    )
    loads = [start(src, dst, sems.at[i]) for i, (src, dst) in enumerate(pairs)]
    for d in range(DEPTHS):
        split_ref[:, d * 128 : (d + 1) * 128] = triple(spec_ref[:, d].reshape(256, 128), 0)
    loads[0].wait()
    for d in range(0, DEPTHS, 2):
        spread = matmul(mid_ref[...], split_ref[:, d * 128 : (d + 2) * 128])
        for h in range(2):
            work[0, d + h] = spread[0:128, h * 128 : (h + 1) * 128]
            work[1, d + h] = spread[128:256, h * 128 : (h + 1) * 128]
    for copy in loads[1:]:
        copy.wait()
    across(work, -1, col_ref, in_ref)
    for k in range(0, DEPTHS, 2):
        part = [jnp.concatenate([work[0, k + h], work[1, k + h]], 1) for h in range(2)]
        freq = matmul(triple(jnp.concatenate(part, 0), 1), inner_ref[...])
        green = jnp.concatenate([green_ref[k], green_ref[k + 1]], 0)
        freq = freq * jnp.concatenate([green, green], 1)
        back = matmul(triple(freq, 1), inner_inv_ref[...])
        for h in range(2):
            work[0, k + h] = back[h * 128 : (h + 1) * 128, 0:128]
            work[1, k + h] = back[h * 128 : (h + 1) * 128, 128:256]
    across(work, 1, col_ref, in_ref)
    copies = []
    for d in range(0, DEPTHS, 2):
        part = [jnp.concatenate([work[0, d + h], work[1, d + h]], 0) for h in range(2)]
        at = slice(d * 128, (d + 2) * 128)
        out_ref[:, at] = matmul(mid_inv_ref[...], triple(jnp.concatenate(part, 1), 0))
        copies.append(start(out_ref.at[:, at], out_hbm.at[:, at], sems.at[5 + d]))
    for copy in copies:
        copy.wait()


def last_kernel(me_ref, weight_ref, spec_ref, inv_hbm, seis_hbm, table_hbm, twist_ref, *rest):
    parts, rest = rest[:DEPTHS], rest[DEPTHS:]
    p_out, state_out, rate_out, rest = rest[0], rest[1], rest[2], rest[3:]
    p_ref, inv_ref, seis_ref, table_ref, state_ref, rate_ref, mid_ref, split_ref, sems = rest
    me = me_ref[0]
    table_load = start(table_hbm, table_ref, sems.at[4, 0])
    loads = [start(inv_hbm, inv_ref, sems.at[4, 1]), start(seis_hbm, seis_ref, sems.at[4, 2])]
    copies = []
    for k in range(DEPTHS):
        d = lax.rem(me + (DEPTHS - k), DEPTHS)
        loads.append(start(parts[k], p_ref.at[:, rows_of(d), :], sems.at[0, k]))
    for c in range(4):
        split_ref[c * 256 : (c + 1) * 256, :] = triple(jnp.transpose(spec_ref[:, c * 256 : (c + 1) * 256]), 1)
    table_load.wait()
    for c in range(4):
        mid_ref[c * 256 : (c + 1) * 256, :] = matmul(split_ref[c * 256 : (c + 1) * 256, :], table_ref[...])
    for copy in loads:
        copy.wait()
    copies.append(start(p_ref, p_out, sems.at[1, 0]))

    def body(i, carry):
        rows = rows_of(i)
        items = []
        for k in range(TILES):
            at = pl.ds(pl.multiple_of(i * 128 + k * 8, 8), 8)
            item = (mid_ref[at, 0:128], mid_ref[at, 128:256])
            if k:
                item = turn(item, twist_ref[0, k : k + 1, :], twist_ref[1, k : k + 1, :], 1)
            items.append(item)
        for n, stress in enumerate(dft16(items, 1)):
            at = slice(n * 128, (n + 1) * 128)
            total = None
            for l in range(2):
                coulomb = stress[l] + friction * p_ref[l, rows, at]
                grown = seis_ref[l, rows, at] * jnp.exp(-coulomb * inv_ref[l, rows, at])
                state = 1.0 + (grown - 1.0) * recovery
                state_ref[i, l, :, at] = state
                term = weight_ref[l] / state
                total = term if total is None else total + term
            rate_ref[n // 2, rows, (n % 2) * 128 : (n % 2) * 128 + 128] = total
        pltpu.make_async_copy(state_ref.at[i], state_out.at[:, rows, :], sems.at[2, i]).start()
        pltpu.make_async_copy(rate_ref.at[:, rows, :], rate_out.at[:, rows, :], sems.at[3, i]).start()
        return carry

    lax.fori_loop(0, DEPTHS, body, 0)
    for i in range(DEPTHS):
        pltpu.make_async_copy(state_ref.at[i], state_out.at[:, rows_of(i), :], sems.at[2, i]).wait()
        pltpu.make_async_copy(rate_ref.at[:, rows_of(i), :], rate_out.at[:, rows_of(i), :], sems.at[3, i]).wait()
    for copy in copies:
        copy.wait()


def sum_kernel(part_ref, out_ref):
    total = part_ref[0]
    for d in range(1, DEPTHS):
        total = total + part_ref[d]
    out_ref[...] = total


def vec(*shape):
    return jax.ShapeDtypeStruct(shape, F32)


SMEM, VMEM, ANY, HBM = pltpu.SMEM, pltpu.VMEM, pl.ANY, pltpu.HBM
DMA = pltpu.SemaphoreType.DMA


def call(kernel, mib, args, outs, scratch=(), aliases={}):
    values = [pltpu.with_memory_space_constraint(value, space) if space is HBM else value for space, value in args]
    return pl.pallas_call(
        kernel,
        out_shape=[HBM(shape, F32) if space is HBM else vec(*shape) for space, shape in outs],
        in_specs=[pl.BlockSpec(memory_space=space) for space, _ in args],
        out_specs=[pl.BlockSpec(memory_space=space) for space, _ in outs],
        scratch_shapes=scratch,
        input_output_aliases=aliases,
        compiler_params=pltpu.CompilerParams(vmem_limit_bytes=mib * 1024 * 1024),
    )(*values)


def buf(*shape, dtype=F32):
    return pltpu.VMEM(shape, dtype)


def shift(value, axis, step):
    peers = lax.axis_size(axis)
    pairs = [(i, i + step) for i in range(peers) if 0 <= i + step < peers]
    return lax.ppermute(value, axis, pairs)


def rotate(values):
    moved = [lax.ppermute(v, "depth", [(i, (i + k) % DEPTHS) for i in range(DEPTHS)]) for k, v in enumerate(values) if k]
    return [values[0]] + moved


def shards(pressure, zone_labels, perm_table, asig_table, well_cells, rate_levels, green_spectrum, seis_state):
    tab = {name: jnp.asarray(value) for name, value in tables().items()}
    depth, slab = lax.axis_index("depth"), lax.axis_index("slab")
    me = (SMEM, depth.reshape(1))
    rows, block = (2, 8, N), (2, ROWS, N)

    table = pltpu.SMEM((perm_table.shape[0],), F32)
    first, last = call(
        edge_kernel,
        4,
        ((HBM, perm_table), (HBM, pressure), (HBM, zone_labels)),
        [(VMEM, (8, N))] * 2,
        [table, buf(2, *rows, dtype=jnp.int32), buf(2, *rows), DMA((5,))],
    )
    before, after = shift(last, "slab", 1), shift(first, "slab", -1)
    zones = zone_labels.reshape(2, DEPTHS, 8, N)
    root, p_copy, msg = call(
        lookup_kernel,
        8,
        ((HBM, perm_table), (HBM, zones), (HBM, pressure.reshape(2, DEPTHS, 8, N))),
        [(VMEM, (DEPTHS,) + rows)] * 2 + [(HBM, (DEPTHS, 11, 8, HALF))],
        [table, buf(2, DEPTHS, 8, N, dtype=jnp.int32), DMA((9,)), DMA((3, 8))],
    )
    (inv,) = call(
        strength_kernel,
        8,
        ((HBM, asig_table), (HBM, zones)),
        [(HBM, block)],
        [table, buf(2, DEPTHS, 8, N, dtype=jnp.int32), buf(*block), DMA((9,))],
    )

    layer, offset = well_cells[:, 0], well_cells[:, 1] - (slab * ROWS + depth * 8)
    own = (offset >= 0) & (offset < 8)
    near = (offset >= -2) & (offset < 10)
    inner = jnp.where(own, layer % 2 * 8 + offset, 16 + (offset + layer % 2 * 4) % 8)
    spot1 = jnp.where(near, layer // 2 * 24 + inner, -1)[None, :]
    spot2 = jnp.where(own, layer * 8 + offset, -1)[None, :]
    amounts = rate_unit * rate_levels.astype(F32)
    src1, src2 = call(
        wells_kernel,
        12,
        ((VMEM, spot1), (VMEM, spot2), (VMEM, amounts), (VMEM, well_cells[:, 2:3])),
        [(HBM, (192, N)), (HBM, (128, N))],
        [buf(320, N), DMA((2,))],
    )

    green = (green_spectrum * (1.0 / (N * N))).reshape(8, 8, SLABS, FREQS, TILES)
    green = green.transpose(1, 2, 3, 4, 0).reshape(8, STEP, LANES)

    (msg,) = call(
        pack_kernel,
        8,
        ((VMEM, p_copy), (VMEM, root), (VMEM, before), (VMEM, after), (HBM, msg)),
        [(HBM, (DEPTHS, 11, 8, HALF))],
        [buf(DEPTHS, 3, 8, HALF), DMA((8,))],
        {4: 0},
    )
    msg = lax.all_to_all(msg, "depth", 0, 0, tiled=True)
    *parts, spec = call(
        diffuse_kernel,
        24,
        (me, (VMEM, msg), (HBM, src1.reshape(DEPTHS, 3, 8, N)), (HBM, src2.reshape(DEPTHS, 2, 8, N)), (HBM, tab["fwd"]),
         (VMEM, tab["row_twist"])),
        [(HBM, rows)] * DEPTHS + [(HBM, (SLABS, DEPTHS, 8, LANES))],
        [buf(DEPTHS + 2, 3, 8, N), buf(DEPTHS, *rows), buf(DEPTHS, *rows), buf(1024, 256), buf(DEPTHS, *rows),
         buf(SLABS, DEPTHS, 8, LANES), buf(DEPTHS, 3, 8, N), buf(DEPTHS, *rows), buf(256, 768, dtype=BF16), DMA((4, 8))],
    )
    spec = lax.all_to_all(spec.reshape(SLABS * DEPTHS, 8, LANES), ("slab", "depth"), 0, 0, tiled=True)
    parts = rotate(parts)
    (spec,) = call(
        middle_kernel,
        16,
        ((VMEM, spec.reshape(SLABS, DEPTHS, 8, LANES)), (VMEM, green), (HBM, tab["mid"]), (HBM, tab["mid_inv"]),
         (HBM, tab["inner"]), (HBM, tab["inner_inv"]), (HBM, tab["col_twist"]), (VMEM, tab["in_twist"])),
        [(HBM, (256, 1024))],
        [buf(2, DEPTHS, STEP, LANES), buf(256, 1024), buf(256, 768, dtype=BF16), buf(256, 768, dtype=BF16),
         buf(768, 256, dtype=BF16), buf(768, 256, dtype=BF16), buf(2, 8, STEP, LANES), buf(768, 1024, dtype=BF16), DMA((12,))],
    )
    spec = lax.all_to_all(spec.reshape(SLABS, 8, 1024), "slab", 0, 0, tiled=True).reshape(256, 1024)
    layer_pos = (depth * 2 + jnp.arange(2, dtype=jnp.int32)).astype(F32)
    weights = (1.0 + 2.0 * layer_pos / (2 * DEPTHS - 1)) / (4.0 * DEPTHS)
    press, state, rate = call(
        last_kernel,
        18,
        (me, (SMEM, weights), (VMEM, spec), (HBM, inv), (HBM, seis_state), (HBM, tab["inv"]), (VMEM, tab["row_twist"]),
         *[(ANY, v) for v in parts]),
        [(HBM, block)] * 2 + [(HBM, (DEPTHS, ROWS, 2 * LANES))],
        [buf(*block), buf(*block), buf(*block), buf(768, 256, dtype=BF16), buf(8, *rows),
         buf(DEPTHS, ROWS, 2 * LANES), buf(1024, 256), buf(1024, 768, dtype=BF16), DMA((5, 8))],
    )
    rate = lax.all_to_all(rate, "depth", 0, 0, tiled=True)
    (rate_map,) = call(sum_kernel, 4, [(VMEM, rate)], [(VMEM, (ROWS, 2 * LANES))])
    return (press, state, rate_map)


def solution(mesh):
    in_specs = (
        P("depth", "slab", None),
        P("depth", "slab", None),
        P(),
        P(),
        P(),
        P(),
        P(None, "slab"),
        P("depth", "slab", None),
    )
    out_specs = (P("depth", "slab", None), P("depth", "slab", None), P("slab", "depth"))
    return jax.shard_map(shards, mesh=mesh, in_specs=in_specs, out_specs=out_specs, check_vma=False)
```

```python
import functools
import math

import jax
import jax.numpy as jnp
import ml_dtypes
import numpy as np
from jax import lax
from jax.experimental import pallas as pl
from jax.experimental.pallas import tpu as pltpu
from jax.sharding import PartitionSpec as P

conduct = 0.15
rate_unit = 0.5
friction = 0.6
recovery = 0.6065306597126334

LANES = 128
SLABS = 32
DEPTHS = 8
N = 2048
ROWS = N // SLABS
TILES = N // LANES
HALF = N // 2
HALVES = TILES // 2
FREQS = LANES // SLABS
STEP = SLABS * FREQS
F32 = jnp.float32
BF16 = jnp.bfloat16


def blocks(theta):
    cos, sin = np.cos(theta), np.sin(theta)
    return np.stack([np.stack([cos, -sin]), np.stack([sin, cos])])


def halves(table):
    high = table.astype(ml_dtypes.bfloat16)
    low = (table - high.astype(np.float64)).astype(ml_dtypes.bfloat16)
    return high, low


def left_table(table):
    high, low = halves(table)
    return np.concatenate([high, high, low], 1)


def right_table(table):
    high, low = halves(table)
    return np.concatenate([high, high, low], 0)


@functools.lru_cache(maxsize=None)
def tables():
    two_pi = 2.0 * np.pi
    k2, n2 = np.arange(128)[:, None], np.arange(128)[None, :]
    fwd = blocks(-two_pi * ((k2 * n2) % 128) / 128)
    fwd = fwd.reshape(2, 2, SLABS, FREQS, 128).transpose(2, 0, 3, 1, 4).reshape(256, 256)
    inv = blocks(two_pi * ((k2 * n2) % 128) / 128)
    inv = inv.reshape(2, 2, 128, SLABS, FREQS).transpose(3, 1, 4, 0, 2).reshape(256, 256)
    i, k = np.arange(SLABS)[:, None], np.arange(SLABS)[None, :]
    eye = np.eye(FREQS)
    angle = two_pi * ((i * k) % SLABS) / SLABS
    mid = np.einsum("absk,ij->akisbj", blocks(-angle), eye).reshape(256, 256)
    mid_inv = np.einsum("absk,ij->saibkj", blocks(angle), eye).reshape(256, 256)
    r, q = np.arange(8)[:, None], np.arange(8)[None, :]
    many = np.eye(TILES)
    angle = two_pi * ((r * q) % 8) / 8
    inner = np.einsum("abrq,ij->bjraiq", blocks(-angle), many).reshape(256, 256)
    inner_inv = np.einsum("abrq,ij->bjqair", blocks(angle), many).reshape(256, 256)
    row_angle = -two_pi * ((np.arange(TILES)[:, None] * np.arange(128)[None, :]) % N) / N
    row_twist = np.stack([np.cos(row_angle), np.sin(row_angle)]).astype(np.float32)
    row = (8 * np.arange(8)[:, None] + np.arange(8)[None, :])[:, None, :]
    col_angle = -two_pi * ((row * np.arange(SLABS)[None, :, None]) % N) / N
    col_angle = np.tile(np.repeat(col_angle, FREQS, 1), (1, 1, TILES))
    col_twist = np.stack([np.cos(col_angle), np.sin(col_angle)]).astype(np.float32)
    in_angle = np.tile(-two_pi * ((r * q) % 64) / 64, (1, TILES))
    in_twist = np.stack([np.cos(in_angle), np.sin(in_angle)]).astype(np.float32)
    return {
        "fwd": left_table(fwd),
        "inv": right_table(inv),
        "mid": left_table(mid),
        "mid_inv": left_table(mid_inv),
        "inner": right_table(inner),
        "inner_inv": right_table(inner_inv),
        "row_twist": row_twist,
        "col_twist": col_twist,
        "in_twist": in_twist,
    }


def triple(value, axis):
    high = value.astype(BF16)
    low = (value - high.astype(F32)).astype(BF16)
    return jnp.concatenate([high, low, high], axis)


def matmul(left, right):
    return jnp.dot(left, right, preferred_element_type=F32)


def radix4(items, sign):
    (ar, ai), (br, bi), (cr, ci), (dr, di) = items
    pr, pi, mr, mi = ar + cr, ai + ci, ar - cr, ai - ci
    qr, qi, nr, ni = br + dr, bi + di, br - dr, bi - di
    tr, ti = (-ni, nr) if sign > 0 else (ni, -nr)
    return [(pr + qr, pi + qi), (mr + tr, mi + ti), (pr - qr, pi - qi), (mr - tr, mi - ti)]


def scale_by(item, angle):
    c, s = math.cos(angle), math.sin(angle)
    re, im = item
    if abs(s) < 1e-12:
        return (re, im) if c > 0 else (-re, -im)
    if abs(c) < 1e-12:
        return (-im, re) if s > 0 else (im, -re)
    return (re * c - im * s, re * s + im * c)


def dft16(items, sign):
    mids = [radix4([items[4 * b + a] for b in range(4)], sign) for a in range(4)]
    out = [None] * 16
    for k in range(4):
        column = [scale_by(mids[a][k], sign * 2.0 * math.pi * a * k / 16) for a in range(4)]
        for m, item in enumerate(radix4(column, sign)):
            out[k + 4 * m] = item
    return out


def table_tiles(table, change):
    lane = lax.broadcasted_iota(jnp.int32, (8, LANES), 1)
    values = [change(jnp.full((8, LANES), table[zone], F32)) for zone in range(16)]
    found = values[0]
    for zone in range(1, 16):
        found = jnp.where(lane == zone, values[zone], found)
    return values, found


def choose(bits, values):
    if len(values) == 1:
        return values[0]
    half = len(values) // 2
    return jnp.where(bits[-1], choose(bits[:-1], values[half:]), choose(bits[:-1], values[:half]))


def pick(label, tiles):
    values, found = tiles
    parts = []
    for c in range(label.shape[1] // LANES):
        zone = label[:, tile(c)]
        if c % 8 in (1, 4, 6):
            parts.append(jnp.take_along_axis(found, zone, axis=1))
        else:
            parts.append(choose([(zone & (1 << bit)) != 0 for bit in range(4)], values))
    return jnp.concatenate(parts, 1)


def start(src, dst, sem):
    copy = pltpu.make_async_copy(src, dst, sem)
    copy.start()
    return copy


def rows_of(d):
    return pl.ds(pl.multiple_of(d * 8, 8), 8)


def edge_kernel(perm_hbm, p_hbm, label_hbm, first_out, last_out, perm_ref, label, p_ref, sems):
    load = start(perm_hbm, perm_ref, sems.at[4])
    first, last = slice(0, 8), slice(ROWS - 8, ROWS)
    loads = [
        start(label_hbm.at[:, first, :], label.at[0], sems.at[0]),
        start(label_hbm.at[:, last, :], label.at[1], sems.at[1]),
        start(p_hbm.at[:, first, :], p_ref.at[0], sems.at[2]),
        start(p_hbm.at[:, last, :], p_ref.at[1], sems.at[3]),
    ]
    load.wait()
    table = table_tiles(perm_ref, jnp.sqrt)
    for copy in loads:
        copy.wait()
    pair = lax.broadcasted_iota(jnp.int32, (8, N), 0) // 2
    for i, (out, at) in enumerate(((first_out, 0), (last_out, 3))):
        values = [p_ref[i, 0], p_ref[i, 1], pick(label[i, 0], table), pick(label[i, 1], table)]
        packed = values[0]
        for n in range(1, 4):
            packed = jnp.where(pair == (at + n) % 4, pltpu.roll(values[n], 2 * n, 0), packed)
        out[...] = packed


def each_part(label_hbm, label, sems, before, work, done):
    parts = [pl.ds(g * 2, 2) for g in range(4)]
    loads = [start(label_hbm.at[:, at], label.at[:, at], sems.at[g]) for g, at in enumerate(parts)]
    values = before()
    width = 1024
    for g in range(4):
        loads[g].wait()

        def body(n, carry, g=g):
            d = g * 2 + n // 2
            cols = pl.ds(pl.multiple_of(n % 2 * width, width), width)
            for l in range(2):
                work(values, label[l, d, :, cols], d, l, cols)
            return carry

        lax.fori_loop(0, 4, body, 0)
        done(g)


def lookup_kernel(perm_hbm, label_hbm, p_hbm, root_out, p_out, msg_hbm, perm_ref, label, sems, msg_sems):
    table = start(perm_hbm, perm_ref, sems.at[8])
    loads, copies = [], []

    def work(values, zone, d, l, cols):
        root_out[d, l, :, cols] = pick(zone, values)

    def done(g):
        if g == 1:
            for copy in loads:
                copy.wait()
        for h in range(2):
            at = slice(h * HALF, (h + 1) * HALF)
            if g == 1:
                copies.append(start(p_out.at[:, :, :, at], msg_hbm.at[:, h * 2 : h * 2 + 2], msg_sems.at[h, 7]))
            if g % 2:
                rows = pl.ds(g * 2 - 2, 4)
                copies.append(start(root_out.at[rows, :, :, at], msg_hbm.at[rows, h * 2 + 4 : h * 2 + 6], msg_sems.at[h, g]))

    def before():
        loads.extend(start(p_hbm.at[l], p_out.at[:, l], msg_sems.at[2, l]) for l in range(2))
        table.wait()
        return table_tiles(perm_ref, jnp.sqrt)

    each_part(label_hbm, label, sems, before, work, done)
    for copy in copies:
        copy.wait()


def strength_kernel(asig_hbm, label_hbm, inv_hbm, asig_ref, label, inv, sems):
    table = start(asig_hbm, asig_ref, sems.at[8])

    def work(values, zone, d, l, cols):
        inv[l, rows_of(d), cols] = pick(zone, values)

    def before():
        table.wait()
        return table_tiles(asig_ref, lambda x: 1.0 / x)

    each_part(label_hbm, label, sems, before, work, lambda g: None)
    start(inv, inv_hbm, sems.at[8]).wait()


def wells_kernel(where1_ref, where2_ref, amount_ref, col_ref, out1_ref, out2_ref, both, sems):
    def hits(where_ref, rows, s):
        row = lax.broadcasted_iota(jnp.int32, (rows, 512), 0)
        return jnp.where(row == where_ref[...], amount_ref[s : s + 1, :], 0.0).astype(BF16)

    left = jnp.concatenate([hits(where1_ref, 192, 0), hits(where2_ref, 128, 1)], 0)
    col_of = jnp.broadcast_to(col_ref[...], (512, 256))
    for c in range(N // 256):
        at = slice(c * 256, (c + 1) * 256)
        col = lax.broadcasted_iota(jnp.int32, (512, 256), 1) + c * 256
        both[:, at] = matmul(left, jnp.where(col == col_of, 1.0, 0.0).astype(BF16))
    copies = [start(both.at[0:192, :], out1_ref, sems.at[0]), start(both.at[192:320, :], out2_ref, sems.at[1])]
    for copy in copies:
        copy.wait()


def pack_kernel(p_ref, q_ref, before_ref, after_ref, msg_hbm, out_hbm, side_ref, sems):
    row = lax.broadcasted_iota(jnp.int32, (8, N), 0)
    half_row = lax.broadcasted_iota(jnp.int32, (8, HALF), 0) % 4
    copies = []
    for d in range(DEPTHS):
        both = []
        for v, ref in enumerate((p_ref, q_ref)):
            sides = []
            for l in range(2):
                back = (8 - 2 * (2 * v + l)) % 8
                prev = ref[d - 1, l] if d else pltpu.roll(before_ref[...], back, 0)
                then = ref[d + 1, l] if d < DEPTHS - 1 else pltpu.roll(after_ref[...], back, 0)
                sides.append(jnp.where(row < 4, then, prev))
            both.append(jnp.where((row < 2) | (row >= 6), sides[0], pltpu.roll(sides[1], 4, 0)))
        out_p, out_q = [jnp.where((row == 0) | (row == 4), pltpu.roll(x, 7, 0), pltpu.roll(x, 1, 0)) for x in both]
        both.append(out_q * (out_p - both[0]))
        for v, x in enumerate(both):
            side_ref[d, v] = jnp.where(
                (half_row == 0) | (half_row == 3), x[:, :HALF], pltpu.roll(x[:, HALF:], 2, 0)
            )
        if d % 4 == 3:
            done = pl.ds(d - 3, 4)
            copies.append(start(side_ref.at[done], out_hbm.at[done, 8:11], sems.at[d]))
    for copy in copies:
        copy.wait()


class Tiles:
    def __init__(self, load):
        self.load, self.kept, self.turned = load, {}, {}

    def __getitem__(self, c):
        if c not in self.kept:
            self.kept[c] = self.load(c)
        return self.kept[c]

    def roll(self, c, by):
        if (c, by) not in self.turned:
            self.turned[c, by] = pltpu.roll(self[c], by, 1)
        return self.turned[c, by]

    def beside(self, c, lane):
        left = self.roll(c - 1, 1) if c else 0.0
        right = self.roll(c + 1, 127) if c < TILES - 1 else 0.0
        return jnp.where(lane == 0, left, self.roll(c, 1)) + jnp.where(lane == 127, right, self.roll(c, 127))


def of_rows(main0, main1, side, row):
    first, last = row == 0, row == 7
    up0 = jnp.where(first, pltpu.roll(side, 1, 0), pltpu.roll(main0, 1, 0))
    down0 = jnp.where(last, pltpu.roll(side, 7, 0), pltpu.roll(main0, 7, 0))
    up1 = jnp.where(first, pltpu.roll(side, 5, 0), pltpu.roll(main1, 1, 0))
    down1 = jnp.where(last, pltpu.roll(side, 3, 0), pltpu.roll(main1, 7, 0))
    return up0 + down0, up1 + down1


def of_side_rows(main0, main1, row):
    of0 = jnp.where(row == 0, pltpu.roll(main0, 1, 0), pltpu.roll(main0, 7, 0))
    of1 = jnp.where(row == 4, pltpu.roll(main1, 5, 0), pltpu.roll(main1, 3, 0))
    return jnp.where((row == 0) | (row == 7), of0, of1)


def tile(c):
    return slice(c * LANES, (c + 1) * LANES)


def diffuse_kernel(me_ref, msg_ref, src1_hbm, src2_hbm, fwd_hbm, twist_ref, *rest):
    outs, spec_hbm = rest[:8], rest[8]
    w_ref, p_ref, s_ref, mid_ref, new_ref, spec_out, src1_ref, src2_ref, fwd_ref, sems = rest[9:]
    me = me_ref[0]
    for d in range(DEPTHS):
        start(src1_hbm.at[d], src1_ref.at[d], sems.at[3, d])
    src2_load = start(src2_hbm, src2_ref, sems.at[0, 1])
    fwd_load = start(fwd_hbm, fwd_ref, sems.at[0, 2])
    w_ref[0] = jnp.zeros((3, 8, N), F32)
    w_ref[DEPTHS + 1] = jnp.zeros((3, 8, N), F32)
    row = lax.broadcasted_iota(jnp.int32, (8, LANES), 0)
    lane = lax.broadcasted_iota(jnp.int32, (8, LANES), 1)
    of_second = (row >= 2) & (row < 6)

    def main(d, v, l, c):
        return msg_ref[d, v * 4 + c // HALVES * 2 + l, :, tile(c % HALVES)]

    def side(d, v, c):
        found = msg_ref[d, 8 + v, :, tile(c % HALVES)]
        return found if c < HALVES else pltpu.roll(found, 6, 0)

    def first(d, carry):
        below, above = jnp.maximum(d - 1, 0), jnp.minimum(d + 1, DEPTHS - 1)
        has_below, has_above = (d > 0).astype(F32), (d < DEPTHS - 1).astype(F32)
        pltpu.make_async_copy(src1_hbm.at[d], src1_ref.at[d], sems.at[3, d]).wait()

        def three(v):
            return [Tiles(lambda c, l=l: main(d, v, l, c)) for l in range(2)] + [Tiles(lambda c: side(d, v, c))]

        p, q = three(0), three(1)
        u = [Tiles(lambda c, i=i: q[i][c] * p[i][c]) for i in range(3)]
        for c in range(TILES):
            at = tile(c)
            q_below = [main(below, 1, 1, c) * has_below, side(below, 1, c) * has_below]
            q_above = [main(above, 1, 0, c) * has_above, side(above, 1, c) * has_above]
            u_below = [q_below[0] * main(below, 0, 1, c), q_below[1] * side(below, 0, c)]
            u_above = [q_above[0] * main(above, 0, 0, c), q_above[1] * side(above, 0, c)]
            sums = []
            for own, low, high in ((q, q_below, q_above), (u, u_below, u_above)):
                x0, x1, x2 = own[0][c], own[1][c], own[2][c]
                sum0, sum1 = of_rows(x0, x1, x2, row)
                depth = pltpu.roll(x2 + jnp.where(of_second, low[1], high[1]), 4, 0)
                sums.append((
                    sum0 + own[0].beside(c, lane) + (low[0] + x1),
                    sum1 + own[1].beside(c, lane) + (x0 + high[0]),
                    of_side_rows(x0, x1, row) + own[2].beside(c, lane) + depth,
                ))
            for i in range(3):
                s, t = sums[0][i], sums[1][i]
                gain = t - p[i][c] * s
                if i == 2:
                    gain = gain + side(d, 2, c)
                new = p[i][c] + (conduct * q[i][c]) * gain + src1_ref[d, i, :, at]
                w_ref[d + 1, i, :, at] = q[i][c] * new
                if i < 2:
                    s_ref[d, i, :, at] = s
                    p_ref[d, i, :, at] = new
        return carry

    lax.fori_loop(0, DEPTHS, first, 0)
    src2_load.wait()

    def second(d):
        k = lax.rem(d + DEPTHS - me, DEPTHS)
        w = [Tiles(lambda c, i=i: w_ref[d + 1, i, :, tile(c)]) for i in range(3)]
        for c in range(TILES):
            at = tile(c)
            x0, x1 = w[0][c], w[1][c]
            sum0, sum1 = of_rows(x0, x1, w[2][c], row)
            t0 = sum0 + w[0].beside(c, lane) + (w_ref[d, 1, :, at] + x1)
            t1 = sum1 + w[1].beside(c, lane) + (x0 + w_ref[d + 2, 0, :, at])
            for l, t in ((0, t0), (1, t1)):
                p = p_ref[d, l, :, at]
                new_ref[k, l, :, at] = (
                    p + (conduct * main(d, 1, l, c)) * (t - p * s_ref[d, l, :, at]) + src2_ref[d, l, :, at]
                )
        spectrum_of_rows(new_ref.at[k], twist_ref, mid_ref, d)

    copies = []

    def transform(c):
        part = triple(mid_ref[c * 256 : (c + 1) * 256, :], 1)
        block = lax.dot_general(fwd_ref[...], part, (((1,), (1,)), ((), ())), preferred_element_type=F32)
        for h in range(2):
            at = c * 2 + h
            spec_out[:, at] = block[:, h * 128 : (h + 1) * 128].reshape(SLABS, 8, 128)
        at = pl.ds(c * 2, 2)
        copies.append(start(spec_out.at[:, at], spec_hbm.at[:, at], sems.at[2, c]))

    second(0)
    second(1)
    fwd_load.wait()
    for d in range(2, DEPTHS, 2):
        transform(d // 2 - 1)
        second(d)
        second(d + 1)
    transform(DEPTHS // 2 - 1)
    copies.extend(start(new_ref.at[k], outs[k], sems.at[1, k]) for k in range(DEPTHS))
    for copy in copies:
        copy.wait()


def spectrum_of_rows(p_ref, twist_ref, mid_ref, d):
    items = [(p_ref[0, :, n * 128 : (n + 1) * 128], p_ref[1, :, n * 128 : (n + 1) * 128]) for n in range(TILES)]
    for k, (re, im) in enumerate(dft16(items, -1)):
        if k:
            cos, sin = twist_ref[0, k : k + 1, :], twist_ref[1, k : k + 1, :]
            re, im = re * cos - im * sin, re * sin + im * cos
        at = slice(d * 128 + k * 8, d * 128 + k * 8 + 8)
        mid_ref[at, 0:128] = re
        mid_ref[at, 128:256] = im


def dft8(items, sign):
    even, odd = radix4(items[0::2], sign), radix4(items[1::2], sign)
    odd = [scale_by(item, sign * 2.0 * math.pi * k / 8) for k, item in enumerate(odd)]
    plus = [(a[0] + b[0], a[1] + b[1]) for a, b in zip(even, odd)]
    minus = [(a[0] - b[0], a[1] - b[1]) for a, b in zip(even, odd)]
    return plus + minus


def turn(item, cos, sin, sign):
    re, im = item
    if sign < 0:
        return re * cos - im * sin, re * sin + im * cos
    return re * cos + im * sin, im * cos - re * sin


def across(ref, sign, col_ref, in_ref):
    def body(i, carry):
        at = pl.ds(pl.multiple_of(i * 8, 8), 8)

        def by_block(items):
            return [turn(item, col_ref[0, d, at, :], col_ref[1, d, at, :], sign) for d, item in enumerate(items)]

        def by_digit(items):
            return [turn(item, in_ref[0, d : d + 1, :], in_ref[1, d : d + 1, :], sign) for d, item in enumerate(items)]

        items = [(ref[0, d, at, :], ref[1, d, at, :]) for d in range(DEPTHS)]
        items = by_block(items) if sign < 0 else by_digit(items)
        items = dft8(items, sign)
        items = by_digit(items) if sign < 0 else by_block(items)
        for d, (re, im) in enumerate(items):
            ref[0, d, at, :] = re
            ref[1, d, at, :] = im
        return carry

    lax.fori_loop(0, STEP // 8, body, 0)


def middle_kernel(
    spec_ref, green_ref, mid_hbm, mid_inv_hbm, inner_hbm, inner_inv_hbm, col_hbm, in_ref, out_hbm,
    work, out_ref, mid_ref, mid_inv_ref, inner_ref, inner_inv_ref, col_ref, split_ref, sems,
):
    pairs = (
        (mid_hbm, mid_ref), (col_hbm, col_ref), (inner_hbm, inner_ref), (inner_inv_hbm, inner_inv_ref),
        (mid_inv_hbm, mid_inv_ref),
    )
    loads = [start(src, dst, sems.at[i]) for i, (src, dst) in enumerate(pairs)]
    for d in range(DEPTHS):
        split_ref[:, d * 128 : (d + 1) * 128] = triple(spec_ref[:, d].reshape(256, 128), 0)
    loads[0].wait()
    for d in range(0, DEPTHS, 2):
        spread = matmul(mid_ref[...], split_ref[:, d * 128 : (d + 2) * 128])
        for h in range(2):
            work[0, d + h] = spread[0:128, h * 128 : (h + 1) * 128]
            work[1, d + h] = spread[128:256, h * 128 : (h + 1) * 128]
    for copy in loads[1:]:
        copy.wait()
    across(work, -1, col_ref, in_ref)
    for k in range(0, DEPTHS, 2):
        part = [jnp.concatenate([work[0, k + h], work[1, k + h]], 1) for h in range(2)]
        freq = matmul(triple(jnp.concatenate(part, 0), 1), inner_ref[...])
        green = jnp.concatenate([green_ref[k], green_ref[k + 1]], 0)
        freq = freq * jnp.concatenate([green, green], 1)
        back = matmul(triple(freq, 1), inner_inv_ref[...])
        for h in range(2):
            work[0, k + h] = back[h * 128 : (h + 1) * 128, 0:128]
            work[1, k + h] = back[h * 128 : (h + 1) * 128, 128:256]
    across(work, 1, col_ref, in_ref)
    copies = []
    for d in range(0, DEPTHS, 2):
        part = [jnp.concatenate([work[0, d + h], work[1, d + h]], 0) for h in range(2)]
        at = slice(d * 128, (d + 2) * 128)
        out_ref[:, at] = matmul(mid_inv_ref[...], triple(jnp.concatenate(part, 1), 0))
        copies.append(start(out_ref.at[:, at], out_hbm.at[:, at], sems.at[5 + d]))
    for copy in copies:
        copy.wait()


def last_kernel(me_ref, weight_ref, spec_ref, inv_hbm, seis_hbm, table_hbm, twist_ref, *rest):
    parts, rest = rest[:DEPTHS], rest[DEPTHS:]
    p_out, state_out, rate_out, rest = rest[0], rest[1], rest[2], rest[3:]
    p_ref, inv_ref, seis_ref, table_ref, state_ref, rate_ref, mid_ref, split_ref, sems = rest
    me = me_ref[0]
    table_load = start(table_hbm, table_ref, sems.at[4, 0])
    loads = [start(inv_hbm, inv_ref, sems.at[4, 1]), start(seis_hbm, seis_ref, sems.at[4, 2])]
    copies = []
    for k in range(DEPTHS):
        d = lax.rem(me + (DEPTHS - k), DEPTHS)
        loads.append(start(parts[k], p_ref.at[:, rows_of(d), :], sems.at[0, k]))
    for c in range(4):
        split_ref[c * 256 : (c + 1) * 256, :] = triple(jnp.transpose(spec_ref[:, c * 256 : (c + 1) * 256]), 1)
    table_load.wait()
    for c in range(4):
        mid_ref[c * 256 : (c + 1) * 256, :] = matmul(split_ref[c * 256 : (c + 1) * 256, :], table_ref[...])
    for copy in loads:
        copy.wait()
    copies.append(start(p_ref, p_out, sems.at[1, 0]))

    def body(i, carry):
        rows = rows_of(i)
        items = []
        for k in range(TILES):
            at = pl.ds(pl.multiple_of(i * 128 + k * 8, 8), 8)
            item = (mid_ref[at, 0:128], mid_ref[at, 128:256])
            if k:
                item = turn(item, twist_ref[0, k : k + 1, :], twist_ref[1, k : k + 1, :], 1)
            items.append(item)
        for n, stress in enumerate(dft16(items, 1)):
            at = slice(n * 128, (n + 1) * 128)
            total = None
            for l in range(2):
                coulomb = stress[l] + friction * p_ref[l, rows, at]
                grown = seis_ref[l, rows, at] * jnp.exp(-coulomb * inv_ref[l, rows, at])
                state = 1.0 + (grown - 1.0) * recovery
                state_ref[i, l, :, at] = state
                term = weight_ref[l] / state
                total = term if total is None else total + term
            rate_ref[n // 2, rows, (n % 2) * 128 : (n % 2) * 128 + 128] = total
        pltpu.make_async_copy(state_ref.at[i], state_out.at[:, rows, :], sems.at[2, i]).start()
        pltpu.make_async_copy(rate_ref.at[:, rows, :], rate_out.at[:, rows, :], sems.at[3, i]).start()
        return carry

    lax.fori_loop(0, DEPTHS, body, 0)
    for i in range(DEPTHS):
        pltpu.make_async_copy(state_ref.at[i], state_out.at[:, rows_of(i), :], sems.at[2, i]).wait()
        pltpu.make_async_copy(rate_ref.at[:, rows_of(i), :], rate_out.at[:, rows_of(i), :], sems.at[3, i]).wait()
    for copy in copies:
        copy.wait()


def sum_kernel(part_ref, out_ref):
    total = part_ref[0]
    for d in range(1, DEPTHS):
        total = total + part_ref[d]
    out_ref[...] = total


def vec(*shape):
    return jax.ShapeDtypeStruct(shape, F32)


SMEM, VMEM, ANY, HBM = pltpu.SMEM, pltpu.VMEM, pl.ANY, pltpu.HBM
DMA = pltpu.SemaphoreType.DMA


def call(kernel, mib, args, outs, scratch=(), aliases={}):
    values = [pltpu.with_memory_space_constraint(value, space) if space is HBM else value for space, value in args]
    return pl.pallas_call(
        kernel,
        out_shape=[HBM(shape, F32) if space is HBM else vec(*shape) for space, shape in outs],
        in_specs=[pl.BlockSpec(memory_space=space) for space, _ in args],
        out_specs=[pl.BlockSpec(memory_space=space) for space, _ in outs],
        scratch_shapes=scratch,
        input_output_aliases=aliases,
        compiler_params=pltpu.CompilerParams(vmem_limit_bytes=mib * 1024 * 1024),
    )(*values)


def buf(*shape, dtype=F32):
    return pltpu.VMEM(shape, dtype)


def shift(value, axis, step):
    peers = lax.axis_size(axis)
    pairs = [(i, i + step) for i in range(peers) if 0 <= i + step < peers]
    return lax.ppermute(value, axis, pairs)


def rotate(values):
    moved = [lax.ppermute(v, "depth", [(i, (i + k) % DEPTHS) for i in range(DEPTHS)]) for k, v in enumerate(values) if k]
    return [values[0]] + moved


def shards(pressure, zone_labels, perm_table, asig_table, well_cells, rate_levels, green_spectrum, seis_state):
    tab = {name: jnp.asarray(value) for name, value in tables().items()}
    depth, slab = lax.axis_index("depth"), lax.axis_index("slab")
    me = (SMEM, depth.reshape(1))
    rows, block = (2, 8, N), (2, ROWS, N)

    table = pltpu.SMEM((perm_table.shape[0],), F32)
    first, last = call(
        edge_kernel,
        4,
        ((HBM, perm_table), (HBM, pressure), (HBM, zone_labels)),
        [(VMEM, (8, N))] * 2,
        [table, buf(2, *rows, dtype=jnp.int32), buf(2, *rows), DMA((5,))],
    )
    before, after = shift(last, "slab", 1), shift(first, "slab", -1)
    zones = zone_labels.reshape(2, DEPTHS, 8, N)
    root, p_copy, msg = call(
        lookup_kernel,
        8,
        ((HBM, perm_table), (HBM, zones), (HBM, pressure.reshape(2, DEPTHS, 8, N))),
        [(VMEM, (DEPTHS,) + rows)] * 2 + [(HBM, (DEPTHS, 11, 8, HALF))],
        [table, buf(2, DEPTHS, 8, N, dtype=jnp.int32), DMA((9,)), DMA((3, 8))],
    )
    (inv,) = call(
        strength_kernel,
        8,
        ((HBM, asig_table), (HBM, zones)),
        [(HBM, block)],
        [table, buf(2, DEPTHS, 8, N, dtype=jnp.int32), buf(*block), DMA((9,))],
    )

    layer, offset = well_cells[:, 0], well_cells[:, 1] - (slab * ROWS + depth * 8)
    own = (offset >= 0) & (offset < 8)
    near = (offset >= -2) & (offset < 10)
    inner = jnp.where(own, layer % 2 * 8 + offset, 16 + (offset + layer % 2 * 4) % 8)
    spot1 = jnp.where(near, layer // 2 * 24 + inner, -1)[None, :]
    spot2 = jnp.where(own, layer * 8 + offset, -1)[None, :]
    amounts = rate_unit * rate_levels.astype(F32)
    src1, src2 = call(
        wells_kernel,
        12,
        ((VMEM, spot1), (VMEM, spot2), (VMEM, amounts), (VMEM, well_cells[:, 2:3])),
        [(HBM, (192, N)), (HBM, (128, N))],
        [buf(320, N), DMA((2,))],
    )

    green = (green_spectrum * (1.0 / (N * N))).reshape(8, 8, SLABS, FREQS, TILES)
    green = green.transpose(1, 2, 3, 4, 0).reshape(8, STEP, LANES)

    (msg,) = call(
        pack_kernel,
        8,
        ((VMEM, p_copy), (VMEM, root), (VMEM, before), (VMEM, after), (HBM, msg)),
        [(HBM, (DEPTHS, 11, 8, HALF))],
        [buf(DEPTHS, 3, 8, HALF), DMA((8,))],
        {4: 0},
    )
    msg = lax.all_to_all(msg, "depth", 0, 0, tiled=True)
    *parts, spec = call(
        diffuse_kernel,
        24,
        (me, (VMEM, msg), (HBM, src1.reshape(DEPTHS, 3, 8, N)), (HBM, src2.reshape(DEPTHS, 2, 8, N)), (HBM, tab["fwd"]),
         (VMEM, tab["row_twist"])),
        [(HBM, rows)] * DEPTHS + [(HBM, (SLABS, DEPTHS, 8, LANES))],
        [buf(DEPTHS + 2, 3, 8, N), buf(DEPTHS, *rows), buf(DEPTHS, *rows), buf(1024, 256), buf(DEPTHS, *rows),
         buf(SLABS, DEPTHS, 8, LANES), buf(DEPTHS, 3, 8, N), buf(DEPTHS, *rows), buf(256, 768, dtype=BF16), DMA((4, 8))],
    )
    spec = lax.all_to_all(spec.reshape(SLABS * DEPTHS, 8, LANES), ("slab", "depth"), 0, 0, tiled=True)
    parts = rotate(parts)
    (spec,) = call(
        middle_kernel,
        16,
        ((VMEM, spec.reshape(SLABS, DEPTHS, 8, LANES)), (VMEM, green), (HBM, tab["mid"]), (HBM, tab["mid_inv"]),
         (HBM, tab["inner"]), (HBM, tab["inner_inv"]), (HBM, tab["col_twist"]), (VMEM, tab["in_twist"])),
        [(HBM, (256, 1024))],
        [buf(2, DEPTHS, STEP, LANES), buf(256, 1024), buf(256, 768, dtype=BF16), buf(256, 768, dtype=BF16),
         buf(768, 256, dtype=BF16), buf(768, 256, dtype=BF16), buf(2, 8, STEP, LANES), buf(768, 1024, dtype=BF16), DMA((12,))],
    )
    spec = lax.all_to_all(spec.reshape(SLABS, 8, 1024), "slab", 0, 0, tiled=True).reshape(256, 1024)
    layer_pos = (depth * 2 + jnp.arange(2, dtype=jnp.int32)).astype(F32)
    weights = (1.0 + 2.0 * layer_pos / (2 * DEPTHS - 1)) / (4.0 * DEPTHS)
    press, state, rate = call(
        last_kernel,
        18,
        (me, (SMEM, weights), (VMEM, spec), (HBM, inv), (HBM, seis_state), (HBM, tab["inv"]), (VMEM, tab["row_twist"]),
         *[(ANY, v) for v in parts]),
        [(HBM, block)] * 2 + [(HBM, (DEPTHS, ROWS, 2 * LANES))],
        [buf(*block), buf(*block), buf(*block), buf(768, 256, dtype=BF16), buf(8, *rows),
         buf(DEPTHS, ROWS, 2 * LANES), buf(1024, 256), buf(1024, 768, dtype=BF16), DMA((5, 8))],
    )
    rate = lax.all_to_all(rate, "depth", 0, 0, tiled=True)
    (rate_map,) = call(sum_kernel, 4, [(VMEM, rate)], [(VMEM, (ROWS, 2 * LANES))])
    return (press, state, rate_map)


def solution(mesh):
    in_specs = (
        P("depth", "slab", None),
        P("depth", "slab", None),
        P(),
        P(),
        P(),
        P(),
        P(None, "slab"),
        P("depth", "slab", None),
    )
    out_specs = (P("depth", "slab", None), P("depth", "slab", None), P("slab", "depth"))
    return jax.shard_map(shards, mesh=mesh, in_specs=in_specs, out_specs=out_specs, check_vma=False)
```
